128 devices in a mesh: tok: 4 (over z), code: 32 (over x, y, core).
Axes of the slice: x: 4, y: 4, z: 4, core: 2. Of those that a mesh axis runs over, the one named last changes fastest.
Arguments:
- tokens: float32 [65536, 256], P(('tok', 'code')), may hold values from -14 to 14
- codebook: float32 [8192, 256], P('code'), may hold values from -6 to 6
Outputs:
- centroids: float32 [8192, 256], P('code')
- counts: float32 [8192], P('code')
The draws below stay inside these ranges and needn't reach their ends.
All inputs are finite; a program needn't handle non-finite values.
Results may differ from the reference program's by a relative error of at most 0.0003.
Values sent between devices are 32-bit elements; how exact they have to be, the bound alone decides.
A program may use at most 128 MiB of HBM per device.

```python
import math
import jax
import jax.numpy as jnp
from jax import lax

D = 256
CODES_DEV = 256
ITERS = 2
K = 8192
TOKENS = 65536
N_CODE = 32


def draw_codebook(key, part):
    return jnp.clip(jax.random.normal(jax.random.fold_in(key, 101), (K, D), jnp.float32), -6.0, 6.0)


def draw_tokens(key, part):
    key = jax.random.fold_in(key, 5)
    return jnp.clip(jax.random.normal(key, (TOKENS, D), jnp.float32), -6.0, 6.0)


def setup_inputs(seed: int = 0) -> dict:
    streams_of = jax.random.split(jax.random.key(seed), 3)
    tokens = draw_tokens(jax.random.fold_in(streams_of[2], 71), 0)
    codebook = draw_codebook(jax.random.fold_in(streams_of[2], 71), 0)
    return {"tokens": tokens, "codebook": codebook}


PRIOR_WEIGHT = 1.0

def block_scores(frames, frame_norms, codes, sharpness):
    code_norms = lax.optimization_barrier(jnp.sum(codes * codes, axis=1))
    inner = lax.dot_general(frames, codes, (((1,), (1,)), ((), ())), precision=lax.Precision.HIGHEST, preferred_element_type=jnp.float32)
    return -sharpness * (frame_norms[:, None] + code_norms[None, :] - 2.0 * inner)

def em_update(frames, codebook):
    sharpness = 1.0 / math.sqrt(D)
    frame_norms = lax.optimization_barrier(jnp.sum(frames * frames, axis=1))
    blocks = codebook.reshape(N_CODE, CODES_DEV, D)

    def scan_stats(carry, codes):
        row_top, totals = carry
        scores = block_scores(frames, frame_norms, codes, sharpness)
        new_top = jnp.maximum(row_top, lax.optimization_barrier(jnp.max(scores, axis=1)))
        totals = totals * jnp.exp(row_top - new_top) + lax.optimization_barrier(jnp.sum(jnp.exp(scores - new_top[:, None]), axis=1))
        return ((new_top, totals), None)
    start_top = jnp.full((frames.shape[0],), -jnp.inf, dtype=jnp.float32)
    start_total = jnp.zeros((frames.shape[0],), dtype=jnp.float32)
    (row_top, totals), _ = lax.scan(scan_stats, (start_top, start_total), blocks)
    log_norm = row_top + jnp.log(totals)

    def update(codes):
        scores = block_scores(frames, frame_norms, codes, sharpness)
        weights = jnp.exp(scores - log_norm[:, None])
        counts = lax.optimization_barrier(jnp.sum(weights, axis=0))
        weighted = lax.dot_general(weights, frames, (((0,), (0,)), ((), ())), precision=lax.Precision.HIGHEST, preferred_element_type=jnp.float32)
        updated = (weighted + PRIOR_WEIGHT * codes) / (counts[:, None] + PRIOR_WEIGHT)
        return (updated, counts)
    updated, counts = lax.map(update, blocks)
    return (updated.reshape(-1, D), counts.reshape(-1))

def reference(tokens, codebook):
    centroids = codebook
    counts = jnp.zeros((codebook.shape[0],), dtype=jnp.float32)
    for iteration in range(ITERS):
        centroids, counts = em_update(tokens, centroids)
    return (centroids, counts)
```

```python
import functools
import math

import jax
import jax.numpy as jnp
from jax import lax
from jax.experimental import pallas as pl
from jax.experimental.pallas import tpu as pltpu
from jax.sharding import PartitionSpec as P

MESH = pl.DeviceIdType.MESH
F32, BF16 = jnp.float32, jnp.bfloat16
ITERS = 2
PRIOR_WEIGHT = 1.0
N = 4
CORES = 2
GROUP = N * CORES
D = 256
FRAMES = 512
OWNED = 256
HALF = OWNED // N // 2
BLOCK = N * HALF
BLOCKS = 2 * N
CHUNKS = 8
ROWS = FRAMES // CHUNKS
TILE = GROUP * ROWS
LEAD = 4
SHARPNESS = math.log2(math.e) / math.sqrt(D)
LAST = (((1,), (1,)), ((), ()))


def split(value):
    high = value.astype(BF16)
    return high, (value - high.astype(F32)).astype(BF16)


def em_kernel(
    frames, codebook, cent_out, count_out,
    tok, thi, tlo, tnorm, cod, chi, clo, cnorm, scores, tops, top, total, lognorm, stats, part, rs1, mid, rs2, fin, flip,
    own_sem, tok_send, tok_recv, c1_send, c1_recv, c2_send, c2_recv, st_send, st_recv,
    r1_send, r1_recv, r2_send, r2_recv, f_send, f_recv,
):
    z = lax.axis_index("tok")
    place = lax.axis_index("code")
    core = lax.rem(place, CORES)
    y = lax.rem(place // CORES, N)
    x = place // (CORES * N)
    mine = core * N + z

    def at(pz, px, py, pc):
        return (pz, (px * N + py) * CORES + pc)

    def ahead(p, o):
        return lax.rem(p + o, N)

    def remote(src, dst, send_sem, recv_sem, device):
        return pltpu.make_async_remote_copy(
            src_ref=src, dst_ref=dst, send_sem=send_sem, recv_sem=recv_sem, device_id=device, device_id_type=MESH
        )

    def await_bytes(ref, sem):
        pltpu.make_async_copy(ref, ref, sem).wait()

    def group_peer(j):
        peer = lax.rem(mine + j, GROUP)
        return at(lax.rem(peer, N), x, y, peer // N)

    barrier = pltpu.get_barrier_semaphore()
    peers = [at(z, ahead(x, o), y, core) for o in range(1, N)]
    peers += [at(z, x, ahead(y, o), core) for o in range(1, N)]
    peers += [group_peer(j) for j in range(1, GROUP)]
    for peer in peers:
        pl.semaphore_signal(barrier, inc=1, device_id=peer, device_id_type=MESH)
    pl.semaphore_wait(barrier, len(peers))

    def spread_start(it, half, src, stage):
        send, recv = ((c1_send, c1_recv), (c2_send, c2_recv))[stage]
        copies = []
        for o in range(1, N):
            along_x = (half + stage) % 2 == 0
            device = at(z, ahead(x, o), y, core) if along_x else at(z, x, ahead(y, o), core)
            block = y if half == 0 else N + x
            if stage == 0:
                dst = cod.at[it, block, x if half == 0 else y]
            else:
                dst = cod.at[it, block]
            copies.append(remote(src, dst, send.at[it, half, o - 1], recv.at[it, half, o - 1], device))
        return copies

    def block_of(half, o):
        return ahead(y, o) if half == 0 else N + ahead(x, o)

    def await_stage1(it):
        for half in range(2):
            for o in range(1, N):
                await_bytes(cod.at[it, 0, 0], c1_recv.at[it, half, o - 1])

    def start_stage2(it):
        for half in range(2):
            for copy in spread_start(it, half, cod.at[it, block_of(half, 0)], 1):
                copy.start()

    before, after = ahead(z, N - 1), ahead(z, 1)
    first = core * N

    def direct(g):
        remote(frames.at[g], tok.at[g, first + z], tok_send.at[g, 0], tok_recv.at[g, 0], at(after, x, y, core)).start()
        remote(frames.at[g], tok.at[g, first + z], tok_send.at[g, 1], tok_recv.at[g, 1], at(before, x, y, core)).start()

    def forward(g):
        await_bytes(tok.at[g, 0], tok_recv.at[g, 0])
        low = tok.at[g, first + before, pl.ds(0, ROWS // 2)]
        remote(low, low, tok_send.at[g, 2], tok_recv.at[g, 2], at(after, x, y, core)).start()
        await_bytes(tok.at[g, 0], tok_recv.at[g, 1])
        high = tok.at[g, first + after, pl.ds(ROWS // 2, ROWS // 2)]
        remote(high, high, tok_send.at[g, 3], tok_recv.at[g, 3], at(before, x, y, core)).start()

    def share(g):
        await_bytes(tok.at[g, 0, pl.ds(0, ROWS // 2)], tok_recv.at[g, 2])
        await_bytes(tok.at[g, 0, pl.ds(0, ROWS // 2)], tok_recv.at[g, 3])
        ours = tok.at[g, pl.ds(first, N)]
        remote(ours, ours, tok_send.at[g, 4], tok_recv.at[g, 4], at(z, x, y, 1 - core)).start()

    own_codes = [codebook.at[z, half] for half in range(2)]
    keep = [
        pltpu.make_async_copy(own_codes[0], cod.at[0, y, x], own_sem.at[0]),
        pltpu.make_async_copy(own_codes[1], cod.at[0, N + x, y], own_sem.at[1]),
        pltpu.make_async_copy(frames, tok.at[:, first + z], own_sem.at[2]),
    ]
    for half in range(2):
        for copy in spread_start(0, half, own_codes[half], 0):
            copy.start()
    for copy in keep:
        copy.start()
    for g in range(LEAD):
        direct(g)
    for copy in keep:
        copy.wait()
    await_stage1(0)
    start_stage2(0)
    forward(0)
    forward(1)
    share(0)
    for half in range(2):
        for o in range(1, N):
            await_bytes(cod.at[0, 0], c2_recv.at[0, half, o - 1])

    def parts_of(codes):
        norms = jnp.sum(codes * codes, axis=1, keepdims=True) * SHARPNESS
        return *split(codes * (2.0 * SHARPNESS)), jnp.broadcast_to(norms, (codes.shape[0], 128))

    def split_block(b, _):
        chi[b], clo[b], cnorm[b] = parts_of(cod[0, b].reshape(BLOCK, D))
        return 0

    lax.fori_loop(0, BLOCKS, split_block, 0)

    def score(high, low, norms, g):
        inner = lax.dot_general(
            jnp.concatenate([high, high, low], axis=1),
            jnp.concatenate([thi[g], tlo[g], thi[g]], axis=1),
            LAST,
            preferred_element_type=F32,
        )
        return inner - jnp.tile(norms, (1, TILE // 128))

    def add_up(g, tiles, carry):
        old_top, old_total = carry if carry is not None else (None, None)
        new_top = tops[g] if carry is None else jnp.maximum(old_top, tops[g])
        new_total = None if carry is None else old_total * jnp.exp2(old_top - new_top)
        for tile in tiles:
            more = jnp.sum(jnp.exp2(tile - new_top), axis=0, keepdims=True)
            new_total = more if new_total is None else new_total + more
        return new_top, new_total

    def publish(it, g, row_top, row_total):
        norm = tnorm[g]
        score_top = row_top - norm
        stats[it, g, mine] = jnp.concatenate([score_top, row_total * jnp.exp2(row_top - (score_top + norm))], axis=0)
        for j in range(1, GROUP):
            own = stats.at[it, g, mine]
            remote(own, own, st_send.at[it, g], st_recv.at[it, g], group_peer(j)).start()

    def normalise(it):
        def of_tile(g, _):
            await_bytes(stats.at[it, g, pl.ds(0, GROUP - 1)], st_recv.at[it, g])
            row_tops, totals = stats[it, g, :, 0, :], stats[it, g, :, 1, :]
            highest = jnp.max(row_tops, axis=0, keepdims=True)
            whole = jnp.sum(totals * jnp.exp2(row_tops - highest), axis=0, keepdims=True)
            lognorm[g] = (highest + tnorm[g]) + jnp.log2(whole)
            return 0

        lax.fori_loop(0, CHUNKS, of_tile, 0)

    def score_tile(g):
        tile = tok[g].reshape(TILE, D)
        thi[g], tlo[g] = split(tile)
        squares = tile * tile
        squares = squares[:, :128] + squares[:, 128:]
        tnorm[g] = jnp.sum(squares.T, axis=0, keepdims=True) * SHARPNESS
        high, low = chi[...].reshape(BLOCKS * BLOCK, D), clo[...].reshape(BLOCKS * BLOCK, D)
        tile_scores = score(high, low, cnorm[...].reshape(BLOCKS * BLOCK, 128), g)
        scores[:, g] = tile_scores.reshape(BLOCKS, BLOCK, TILE)
        tops[g] = jnp.max(tile_scores, axis=0, keepdims=True)

    def sum_tile(g):
        publish(0, g, *add_up(g, [scores[:, g].reshape(BLOCKS * BLOCK, TILE)], None))

    def move_on(g):
        @pl.when(g + LEAD < CHUNKS)
        def _():
            direct(g + LEAD)

        @pl.when(g + 2 < CHUNKS)
        def _():
            forward(g + 2)

        @pl.when(g + 1 < CHUNKS)
        def _():
            share(g + 1)

        await_bytes(tok.at[g, pl.ds(0, N)], tok_recv.at[g, 4])

    move_on(0)
    score_tile(0)

    def step(g, _):
        move_on(g)
        sum_tile(g - 1)
        score_tile(g)
        return 0

    lax.fori_loop(1, CHUNKS, step, 0)
    sum_tile(CHUNKS - 1)

    def gray(i):
        return jnp.bitwise_xor(i, i // 2)

    def sums_to(it, o):
        for half in range(2):
            device = at(z, x, ahead(y, o), core) if half == 0 else at(z, ahead(x, o), y, core)
            yield remote(
                part.at[block_of(half, o)], rs1.at[it, half, o - 1], r1_send.at[it, half, o - 1], r1_recv.at[it, half, o - 1], device
            )

    def moments(it):
        def pair(i, _):
            o = gray(N - 1 - i)
            blocks = [block_of(half, o) for half in range(2)]
            lefts, rights, counts = [], [], None
            for g in range(CHUNKS):
                pair_scores = jnp.concatenate([scores[b, g] for b in blocks], axis=0)
                weights = jnp.exp2(pair_scores - lognorm[g])
                for q in range(TILE // 128):
                    piece = weights[:, q * 128 : (q + 1) * 128]
                    counts = piece if counts is None else counts + piece
                high, low = split(weights)
                lefts += [high, high, low]
                rights += [thi[g], tlo[g], thi[g]]
            weighted = jnp.dot(
                jnp.concatenate(lefts, axis=1), jnp.concatenate(rights, axis=0), preferred_element_type=F32
            )
            for half in range(2):
                part[blocks[half], pl.ds(0, BLOCK)] = weighted[half * BLOCK : (half + 1) * BLOCK]
                row = jnp.sum(counts[half * BLOCK : (half + 1) * BLOCK].T, axis=0, keepdims=True)
                part[blocks[half], pl.ds(BLOCK, 8)] = jnp.broadcast_to(jnp.tile(row, (1, 2)), (8, D))

            @pl.when(o != 0)
            def _():
                for copy in sums_to(it, o):
                    copy.start()

            return 0

        lax.fori_loop(0, N, pair, 0)

    def reduce_sums(it):
        slot = (x, y)
        for half in range(2):
            for o in range(1, N):
                await_bytes(part.at[0], r1_recv.at[it, half, o - 1])
            row = part[block_of(half, 0)] + rs1[it, half, 0] + rs1[it, half, 1] + rs1[it, half, 2]
            for p in range(N):
                mid[half, p, pl.ds(0, HALF)] = row[p * HALF : (p + 1) * HALF]
                mid[half, p, pl.ds(HALF, 8)] = row[BLOCK:]
            for o in range(1, N):
                device = at(z, ahead(x, o), y, core) if half == 0 else at(z, x, ahead(y, o), core)
                remote(
                    mid.at[half, ahead(slot[half], o)], rs2.at[it, half, o - 1], r2_send.at[it, half, o - 1], r2_recv.at[it, half, o - 1], device
                ).start()
        codes, counts = [], []
        for half in range(2):
            for o in range(1, N):
                await_bytes(mid.at[0, 0], r2_recv.at[it, half, o - 1])
            sums = mid[half, slot[half]] + rs2[it, half, 0] + rs2[it, half, 1] + rs2[it, half, 2]
            flip[half] = jnp.broadcast_to(sums[HALF : HALF + 1, :128], (128, 128)).T
            count = flip[half, pl.ds(pl.multiple_of(slot[half] * HALF, HALF), HALF)]
            old = cod[it, block_of(half, 0), slot[half]]
            new = (sums[:HALF] + PRIOR_WEIGHT * old) / (jnp.tile(count, (1, 2)) + PRIOR_WEIGHT)
            codes.append(new)
            counts.append(count)
        return codes, counts

    def sent(it):
        for half in range(2):
            for o in range(1, N):
                await_bytes(part.at[0], r1_send.at[it, half, o - 1])
                await_bytes(mid.at[0, 0], r2_send.at[it, half, o - 1])

    normalise(0)
    moments(0)
    new_codes, _ = reduce_sums(0)
    cod[1, y, x] = new_codes[0]
    cod[1, N + x, y] = new_codes[1]
    for half in range(2):
        for copy in spread_start(1, half, cod.at[1, block_of(half, 0), (x, y)[half]], 0):
            copy.start()
    sent(0)
    await_stage1(1)
    start_stage2(1)

    def score_pair(o):
        blocks = [block_of(half, o) for half in range(2)]
        codes = jnp.concatenate([cod[1, b].reshape(BLOCK, D) for b in blocks], axis=0)
        high, low, norms = parts_of(codes)
        for g in range(CHUNKS):
            tile_scores = score(high, low, norms, g)
            for half in range(2):
                scores[blocks[half], g] = tile_scores[half * BLOCK : (half + 1) * BLOCK]
            tops[g] = jnp.max(tile_scores, axis=0, keepdims=True)

    def sum_pair(o, g):
        blocks = [block_of(half, o) for half in range(2)]
        return add_up(g, [scores[b, g] for b in blocks], (top[g], total[g]))

    top[...] = jnp.full_like(top, -1e30)
    total[...] = jnp.zeros_like(total)
    score_pair(0)

    def pair_step(i, _):
        o, previous = gray(i), gray(i - 1)
        for half in range(2):
            await_bytes(cod.at[1, 0], c2_recv.at[1, half, N - 1 - o])
        for g in range(CHUNKS):
            top[g], total[g] = sum_pair(previous, g)
        score_pair(o)
        return 0

    lax.fori_loop(1, N, pair_step, 0)

    def last_sum(g, _):
        publish(1, g, *sum_pair(gray(N - 1), g))
        return 0

    lax.fori_loop(0, CHUNKS, last_sum, 0)
    normalise(1)
    moments(1)
    new_codes, counts = reduce_sums(1)

    for half in range(2):
        fin[z, pl.ds(half * HALF, HALF)] = new_codes[half]
        flip[0, pl.ds(half * HALF, HALF)] = counts[half]
    row = flip[0].T[:8]
    fin[z, pl.ds(2 * HALF, 8)] = jnp.tile(row, (1, 2))
    for o in range(1, N):
        remote(fin.at[z], fin.at[z], f_send.at[o - 1], f_recv.at[o - 1], at(ahead(z, o), x, y, core)).start()
    sent(1)

    def tokens_sent(g, _):
        for i in range(2):
            await_bytes(tok.at[g, 0], tok_send.at[g, i])
            await_bytes(tok.at[g, 0, pl.ds(0, ROWS // 2)], tok_send.at[g, 2 + i])
        await_bytes(tok.at[g, pl.ds(0, N)], tok_send.at[g, 4])
        for it in range(ITERS):
            await_bytes(stats.at[it, g, pl.ds(0, GROUP - 1)], st_send.at[it, g])
        return 0

    lax.fori_loop(0, CHUNKS, tokens_sent, 0)
    for it in range(ITERS):
        for half in range(2):
            for o in range(1, N):
                await_bytes(cod.at[it, 0, 0], c1_send.at[it, half, o - 1])
                await_bytes(cod.at[it, 0], c2_send.at[it, half, o - 1])
    for o in range(1, N):
        await_bytes(fin.at[0], f_send.at[o - 1])
        await_bytes(fin.at[0], f_recv.at[o - 1])
    for p in range(N):
        cent_out[pl.ds(p * 2 * HALF, 2 * HALF)] = fin[p, pl.ds(0, 2 * HALF)]
        count_out[:, pl.ds(p * 2 * HALF, 2 * HALF)] = fin[p, pl.ds(2 * HALF, 1), pl.ds(0, 2 * HALF)]


def on_device(tokens, codebook):
    vmem, dma = pltpu.VMEM, pltpu.SemaphoreType.DMA
    peers = N - 1
    centroids, counts = pl.pallas_call(
        em_kernel,
        out_shape=[jax.ShapeDtypeStruct((OWNED, D), F32), jax.ShapeDtypeStruct((1, OWNED), F32)],
        in_specs=[pl.BlockSpec(memory_space=pl.ANY)] * 2,
        out_specs=[pl.BlockSpec(memory_space=vmem)] * 2,
        scratch_shapes=[
            vmem((CHUNKS, GROUP, ROWS, D), F32),
            vmem((CHUNKS, TILE, D), BF16),
            vmem((CHUNKS, TILE, D), BF16),
            vmem((CHUNKS, 1, TILE), F32),
            vmem((ITERS, BLOCKS, N, HALF, D), F32),
            vmem((BLOCKS, BLOCK, D), BF16),
            vmem((BLOCKS, BLOCK, D), BF16),
            vmem((BLOCKS, BLOCK, 128), F32),
            vmem((BLOCKS, CHUNKS, BLOCK, TILE), F32),
            vmem((CHUNKS, 1, TILE), F32),
            vmem((CHUNKS, 1, TILE), F32),
            vmem((CHUNKS, 1, TILE), F32),
            vmem((CHUNKS, 1, TILE), F32),
            vmem((ITERS, CHUNKS, GROUP, 2, TILE), F32),
            vmem((BLOCKS, BLOCK + 8, D), F32),
            vmem((ITERS, 2, peers, BLOCK + 8, D), F32),
            vmem((2, N, HALF + 8, D), F32),
            vmem((ITERS, 2, peers, HALF + 8, D), F32),
            vmem((N, 2 * HALF + 8, D), F32),
            vmem((2, 128, 128), F32),
            dma((3,)),
            dma((CHUNKS, 5)),
            dma((CHUNKS, 5)),
            dma((ITERS, 2, peers)),
            dma((ITERS, 2, peers)),
            dma((ITERS, 2, peers)),
            dma((ITERS, 2, peers)),
            dma((ITERS, CHUNKS)),
            dma((ITERS, CHUNKS)),
            dma((ITERS, 2, peers)),
            dma((ITERS, 2, peers)),
            dma((ITERS, 2, peers)),
            dma((ITERS, 2, peers)),
            dma((peers,)),
            dma((peers,)),
        ],
        compiler_params=pltpu.CompilerParams(collective_id=0, has_side_effects=True, vmem_limit_bytes=56 << 20),
        cost_estimate=pl.CostEstimate(
            flops=ITERS * 2 * 3 * 2 * CHUNKS * TILE * BLOCKS * BLOCK * D,
            bytes_accessed=4 * (FRAMES + 2 * OWNED) * D,
            transcendentals=ITERS * 2 * CHUNKS * TILE * BLOCKS * BLOCK,
        ),
    )(tokens.reshape(CHUNKS, ROWS, D), codebook.reshape(N, 2, HALF, D))
    return centroids, counts.reshape(OWNED)


def solution(mesh):
    return jax.shard_map(
        on_device,
        mesh=mesh,
        in_specs=(P(("tok", "code"), None), P("code", None)),
        out_specs=(P("code", None), P("code")),
        check_vma=False,
    )
```

```python
import functools
import math

import jax
import jax.numpy as jnp
from jax import lax
from jax.experimental import pallas as pl
from jax.experimental.pallas import tpu as pltpu
from jax.sharding import PartitionSpec as P

MESH = pl.DeviceIdType.MESH
F32, BF16 = jnp.float32, jnp.bfloat16
ITERS = 2
PRIOR_WEIGHT = 1.0
N = 4
CORES = 2
GROUP = N * CORES
D = 256
FRAMES = 512
OWNED = 256
HALF = OWNED // N // 2
BLOCK = N * HALF
BLOCKS = 2 * N
CHUNKS = 8
ROWS = FRAMES // CHUNKS
TILE = GROUP * ROWS
LEAD = 4
AHEAD = 5
BATCH = 4
BATCHES = CHUNKS // BATCH
LOW = 2 * HALF + 8
SUMS = LOW + 2 * HALF
SHARPNESS = math.log2(math.e) / math.sqrt(D)
LAST = (((1,), (1,)), ((), ()))


def split(value):
    high = value.astype(BF16)
    return high, (value - high.astype(F32)).astype(BF16)


def em_kernel(
    frames, codebook, cent_out, count_out,
    tok, thi, tlo, tnorm, cod, chi, clo, cnorm, scores, tops, top, total, lognorm, stats, part, rs1, rlow, rhigh, mid, rs2, fin, flip,
    own_sem, tok_send, tok_recv, c1_send, c1_recv, c2_send, c2_recv, st_send, st_recv,
    r1_send, r1_recv, r2_send, r2_recv, f_send, f_recv,
):
    z = lax.axis_index("tok")
    place = lax.axis_index("code")
    core = lax.rem(place, CORES)
    y = lax.rem(place // CORES, N)
    x = place // (CORES * N)
    mine = core * N + z

    def at(pz, px, py, pc):
        return (pz, (px * N + py) * CORES + pc)

    def ahead(p, o):
        return lax.rem(p + o, N)

    def remote(src, dst, send_sem, recv_sem, device):
        return pltpu.make_async_remote_copy(
            src_ref=src, dst_ref=dst, send_sem=send_sem, recv_sem=recv_sem, device_id=device, device_id_type=MESH
        )

    def await_bytes(ref, sem):
        pltpu.make_async_copy(ref, ref, sem).wait()

    def group_peer(j):
        peer = lax.rem(mine + j, GROUP)
        return at(lax.rem(peer, N), x, y, peer // N)

    barrier = pltpu.get_barrier_semaphore()
    peers = [at(z, ahead(x, o), y, core) for o in range(1, N)]
    peers += [at(z, x, ahead(y, o), core) for o in range(1, N)]
    peers += [group_peer(j) for j in range(1, GROUP)]
    for peer in peers:
        pl.semaphore_signal(barrier, inc=1, device_id=peer, device_id_type=MESH)
    pl.semaphore_wait(barrier, len(peers))

    def block_of(half, o):
        return ahead(y, o) if half == 0 else N + ahead(x, o)

    def across(half, o):
        return at(z, ahead(x, o), y, core) if half == 0 else at(z, x, ahead(y, o), core)

    def along(half, o):
        return at(z, x, ahead(y, o), core) if half == 0 else at(z, ahead(x, o), y, core)

    slot = (x, y)

    def start_stage1(it, half, src):
        dst = cod.at[it, block_of(half, 0), slot[half]]
        for o in (2, 1, 3):
            remote(src, dst, c1_send.at[it, half, o - 1], c1_recv.at[it, half, o - 1], across(half, o)).start()

    def await_stage1(it, half):
        for o in range(1, N):
            await_bytes(cod.at[it, 0, 0], c1_recv.at[it, half, o - 1])

    def start_stage2(it, half):
        block = cod.at[it, block_of(half, 0)]
        for i, o in ((0, 1), (2, N - 1)):
            remote(block, block, c2_send.at[it, half, i], c2_recv.at[it, half, i], along(half, o)).start()

    def pass_on(it, half):
        for i, o, start in ((0, N - 1, 0), (2, 1, N // 2)):
            await_bytes(cod.at[it, 0], c2_recv.at[it, half, i])
            block = cod.at[it, block_of(half, o), pl.ds(start, N // 2)]
            remote(block, block, c2_send.at[it, half, i + 1], c2_recv.at[it, half, i + 1], along(half, N - o)).start()

    def await_passed(it, half):
        for i in (1, 3):
            await_bytes(cod.at[it, 0, pl.ds(0, N // 2)], c2_recv.at[it, half, i])

    before, after = ahead(z, N - 1), ahead(z, 1)
    first = core * N

    def direct(g):
        remote(frames.at[g], tok.at[g, first + z], tok_send.at[g, 0], tok_recv.at[g, 0], at(after, x, y, core)).start()
        remote(frames.at[g], tok.at[g, first + z], tok_send.at[g, 1], tok_recv.at[g, 1], at(before, x, y, core)).start()

    def forward(g):
        await_bytes(tok.at[g, 0], tok_recv.at[g, 0])
        low = tok.at[g, first + before, pl.ds(0, ROWS // 2)]
        remote(low, low, tok_send.at[g, 2], tok_recv.at[g, 2], at(after, x, y, core)).start()
        await_bytes(tok.at[g, 0], tok_recv.at[g, 1])
        high = tok.at[g, first + after, pl.ds(ROWS // 2, ROWS // 2)]
        remote(high, high, tok_send.at[g, 3], tok_recv.at[g, 3], at(before, x, y, core)).start()

    def share(g):
        await_bytes(tok.at[g, 0, pl.ds(0, ROWS // 2)], tok_recv.at[g, 2])
        await_bytes(tok.at[g, 0, pl.ds(0, ROWS // 2)], tok_recv.at[g, 3])
        ours = tok.at[g, pl.ds(first, N)]
        remote(ours, ours, tok_send.at[g, 4], tok_recv.at[g, 4], at(z, x, y, 1 - core)).start()

    own_codes = [codebook.at[z, half] for half in range(2)]
    keep = [
        pltpu.make_async_copy(own_codes[0], cod.at[0, y, x], own_sem.at[0]),
        pltpu.make_async_copy(own_codes[1], cod.at[0, N + x, y], own_sem.at[1]),
        pltpu.make_async_copy(frames, tok.at[:, first + z], own_sem.at[2]),
    ]
    for half in range(2):
        start_stage1(0, half, own_codes[half])
    for copy in keep:
        copy.start()
    for g in range(LEAD):
        direct(g)
    for copy in keep:
        copy.wait()
    for half in range(2):
        await_stage1(0, half)
        start_stage2(0, half)
    for g in range(AHEAD):
        forward(g)
        if g + LEAD < CHUNKS:
            direct(g + LEAD)
        if g > 0:
            share(g - 1)
        if g == 2:
            for half in range(2):
                pass_on(0, half)
    for half in range(2):
        await_passed(0, half)

    def parts_of(codes):
        norms = jnp.sum(codes * codes, axis=1, keepdims=True) * SHARPNESS
        return *split(codes * (2.0 * SHARPNESS)), jnp.broadcast_to(norms, (codes.shape[0], 128))

    def split_block(b, _):
        chi[b], clo[b], cnorm[b] = parts_of(cod[0, b].reshape(BLOCK, D))
        return 0

    lax.fori_loop(0, BLOCKS, split_block, 0)

    def score(high, low, norms, g):
        inner = lax.dot_general(
            jnp.concatenate([high, high, low], axis=1),
            jnp.concatenate([thi[g], tlo[g], thi[g]], axis=1),
            LAST,
            preferred_element_type=F32,
        )
        return inner - jnp.tile(norms, (1, TILE // 128))

    def add_up(g, tiles, carry):
        old_top, old_total = carry if carry is not None else (None, None)
        new_top = tops[g] if carry is None else jnp.maximum(old_top, tops[g])
        new_total = None if carry is None else old_total * jnp.exp2(old_top - new_top)
        for tile in tiles:
            more = jnp.sum(jnp.exp2(tile - new_top), axis=0, keepdims=True)
            new_total = more if new_total is None else new_total + more
        return new_top, new_total

    def publish(it, g, row_top, row_total):
        norm = tnorm[g]
        score_top = row_top - norm
        stats[it, g // BATCH, mine, g % BATCH] = jnp.concatenate(
            [score_top, row_total * jnp.exp2(row_top - (score_top + norm))], axis=0
        )

    def send_stats(it, batch):
        own = stats.at[it, batch, mine]
        for j in range(1, GROUP):
            remote(own, own, st_send.at[it, batch], st_recv.at[it, batch], group_peer(j)).start()

    def normalise(it, batch):
        await_bytes(stats.at[it, batch, pl.ds(0, GROUP - 1)], st_recv.at[it, batch])
        for q in range(BATCH):
            g = batch * BATCH + q
            row_tops, totals = stats[it, batch, :, q, 0, :], stats[it, batch, :, q, 1, :]
            highest = jnp.max(row_tops, axis=0, keepdims=True)
            whole = jnp.sum(totals * jnp.exp2(row_tops - highest), axis=0, keepdims=True)
            lognorm[g] = (highest + tnorm[g]) + jnp.log2(whole)

    def score_tile(g):
        tile = tok[g].reshape(TILE, D)
        thi[g], tlo[g] = split(tile)
        squares = tile * tile
        squares = squares[:, :128] + squares[:, 128:]
        tnorm[g] = jnp.sum(squares.T, axis=0, keepdims=True) * SHARPNESS
        high, low = chi[...].reshape(BLOCKS * BLOCK, D), clo[...].reshape(BLOCKS * BLOCK, D)
        tile_scores = score(high, low, cnorm[...].reshape(BLOCKS * BLOCK, 128), g)
        scores[:, g] = tile_scores.reshape(BLOCKS, BLOCK, TILE)
        tops[g] = jnp.max(tile_scores, axis=0, keepdims=True)

    def sum_tile(g):
        publish(0, g, *add_up(g, [scores[:, g].reshape(BLOCKS * BLOCK, TILE)], None))

    def move_on(g):
        @pl.when(g + AHEAD < CHUNKS)
        def _():
            forward(g + AHEAD)

        @pl.when(g + AHEAD - 1 < CHUNKS)
        def _():
            share(g + AHEAD - 1)

        await_bytes(tok.at[g, pl.ds(0, N)], tok_recv.at[g, 4])

    move_on(0)
    score_tile(0)

    def step(g, _):
        move_on(g)
        sum_tile(g - 1)
        score_tile(g)

        @pl.when(g == BATCH)
        def _():
            send_stats(0, 0)

        return 0

    lax.fori_loop(1, CHUNKS, step, 0)
    sum_tile(CHUNKS - 1)
    send_stats(0, 1)

    def gray(i):
        return jnp.bitwise_xor(i, i // 2)

    def weigh(blocks, tiles):
        lefts, rights, counts = [], [], None
        for g in tiles:
            pair_scores = jnp.concatenate([scores[b, g] for b in blocks], axis=0)
            weights = jnp.exp2(pair_scores - lognorm[g])
            for q in range(TILE // 128):
                piece = weights[:, q * 128 : (q + 1) * 128]
                counts = piece if counts is None else counts + piece
            high, low = split(weights)
            lefts += [high, high, low]
            rights += [thi[g], tlo[g], thi[g]]
        weighted = jnp.dot(jnp.concatenate(lefts, axis=1), jnp.concatenate(rights, axis=0), preferred_element_type=F32)
        return weighted, counts

    def keep_sums(blocks, weighted, counts):
        for half in range(2):
            rows = weighted[half * BLOCK : (half + 1) * BLOCK]
            part[blocks[half], pl.ds(0, 2 * HALF)] = rows[: 2 * HALF]
            part[blocks[half], pl.ds(LOW, 2 * HALF)] = rows[2 * HALF :]
            row = jnp.sum(counts[half * BLOCK : (half + 1) * BLOCK].T, axis=0, keepdims=True)
            part[blocks[half], pl.ds(2 * HALF, 8)] = jnp.broadcast_to(jnp.tile(row, (1, 2)), (8, D))

    low_rows, high_rows = pl.ds(0, LOW), pl.ds(LOW, 2 * HALF)

    def moments(it):
        normalise(it, 0)
        blocks = [block_of(half, N // 2) for half in range(2)]
        weighted, counts = weigh(blocks, range(BATCH))
        normalise(it, 1)
        more = weigh(blocks, range(BATCH, CHUNKS))
        keep_sums(blocks, weighted + more[0], counts + more[1])
        for half in range(2):
            both = part.at[blocks[half]]
            remote(both.at[low_rows], rlow.at[it, half], r1_send.at[it, half, 1], r1_recv.at[it, half, 1], along(half, 1)).start()
            remote(
                both.at[high_rows], rhigh.at[it, half], r1_send.at[it, half, 3], r1_recv.at[it, half, 3], along(half, N - 1)
            ).start()

        def pair(i, _):
            o = gray(N - 1 - i)
            blocks = [block_of(half, o) for half in range(2)]
            keep_sums(blocks, *weigh(blocks, range(CHUNKS)))

            @pl.when(o == 1)
            def _():
                for half in range(2):
                    await_bytes(rlow.at[it, half], r1_recv.at[it, half, 1])
                    part[blocks[half], low_rows] += rlow[it, half]
                    remote(
                        part.at[blocks[half]], rs1.at[it, half, 0], r1_send.at[it, half, 0], r1_recv.at[it, half, 0], along(half, 1)
                    ).start()

            @pl.when(o == N - 1)
            def _():
                for half in range(2):
                    await_bytes(rhigh.at[it, half], r1_recv.at[it, half, 3])
                    part[blocks[half], high_rows] += rhigh[it, half]
                    remote(
                        part.at[blocks[half]], rs1.at[it, half, 1], r1_send.at[it, half, 2], r1_recv.at[it, half, 2], along(half, N - 1)
                    ).start()

            return 0

        lax.fori_loop(1, N, pair, 0)

    def reduce_sums(it, use):
        for half in range(2):
            for i in (0, 2):
                await_bytes(part.at[0], r1_recv.at[it, half, i])
            row = part[block_of(half, 0)] + rs1[it, half, 0] + rs1[it, half, 1]
            for p in range(N):
                start = p * HALF + (8 if p >= N // 2 else 0)
                mid[half, p, pl.ds(0, HALF)] = row[start : start + HALF]
                mid[half, p, pl.ds(HALF, 8)] = row[2 * HALF : LOW]
            for o in (2, 1, 3):
                remote(
                    mid.at[half, ahead(slot[half], o)], rs2.at[it, half, o - 1], r2_send.at[it, half, o - 1], r2_recv.at[it, half, o - 1], across(half, o)
                ).start()
        for half in range(2):
            for o in range(1, N):
                await_bytes(mid.at[0, 0], r2_recv.at[it, half, o - 1])
            sums = mid[half, slot[half]] + rs2[it, half, 0] + rs2[it, half, 1] + rs2[it, half, 2]
            flip[half] = jnp.broadcast_to(sums[HALF : HALF + 1, :128], (128, 128)).T
            count = flip[half, pl.ds(pl.multiple_of(slot[half] * HALF, HALF), HALF)]
            old = cod[it, block_of(half, 0), slot[half]]
            use(half, (sums[:HALF] + PRIOR_WEIGHT * old) / (jnp.tile(count, (1, 2)) + PRIOR_WEIGHT), count)

    def sent(it):
        for half in range(2):
            for i in (0, 2):
                await_bytes(part.at[0], r1_send.at[it, half, i])
            await_bytes(part.at[0, low_rows], r1_send.at[it, half, 1])
            await_bytes(part.at[0, high_rows], r1_send.at[it, half, 3])
            for o in range(1, N):
                await_bytes(mid.at[0, 0], r2_send.at[it, half, o - 1])

    def next_codes(half, codes, _):
        cod[1, block_of(half, 0), slot[half]] = codes
        start_stage1(1, half, cod.at[1, block_of(half, 0), slot[half]])

    moments(0)
    reduce_sums(0, next_codes)
    for half in range(2):
        await_stage1(1, half)
        start_stage2(1, half)

    def score_pair(o, tiles):
        blocks = [block_of(half, o) for half in range(2)]
        codes = jnp.concatenate([cod[1, b].reshape(BLOCK, D) for b in blocks], axis=0)
        high, low, norms = parts_of(codes)
        for g in tiles:
            tile_scores = score(high, low, norms, g)
            for half in range(2):
                scores[blocks[half], g] = tile_scores[half * BLOCK : (half + 1) * BLOCK]
            tops[g] = jnp.max(tile_scores, axis=0, keepdims=True)

    def sum_pair(o, g):
        blocks = [block_of(half, o) for half in range(2)]
        return add_up(g, [scores[b, g] for b in blocks], (top[g], total[g]))

    def sum_pairs(o, tiles):
        for g in tiles:
            top[g], total[g] = sum_pair(o, g)

    every, early, late = range(CHUNKS), range(BATCH), range(BATCH, CHUNKS)
    top[...] = jnp.full_like(top, -1e30)
    total[...] = jnp.zeros_like(total)
    score_pair(0, every)
    for half in range(2):
        pass_on(1, half)

    def pair_step(i, _):
        sum_pairs(gray(i - 1), every)
        score_pair(gray(i), every)
        return 0

    lax.fori_loop(1, N - 1, pair_step, 0)
    for half in range(2):
        await_passed(1, half)
    sum_pairs(N - 1, early)
    score_pair(N // 2, early)
    sum_pairs(N - 1, late)
    for g in early:
        publish(1, g, *sum_pair(N // 2, g))
    score_pair(N // 2, late)
    send_stats(1, 0)
    for g in late:
        publish(1, g, *sum_pair(N // 2, g))
    send_stats(1, 1)
    sent(0)
    moments(1)

    def last_codes(half, codes, count):
        fin[half, z, pl.ds(0, HALF)] = codes
        flip[half, pl.ds(0, HALF)] = count
        fin[half, z, pl.ds(HALF, 8)] = jnp.tile(flip[half].T[:8], (1, 2))
        own = fin.at[half, z]
        for o in (2, 1, 3):
            remote(own, own, f_send.at[half, o - 1], f_recv.at[half, o - 1], at(ahead(z, o), x, y, core)).start()

    reduce_sums(1, last_codes)
    sent(1)

    def tokens_sent(g, _):
        for i in range(2):
            await_bytes(tok.at[g, 0], tok_send.at[g, i])
            await_bytes(tok.at[g, 0, pl.ds(0, ROWS // 2)], tok_send.at[g, 2 + i])
        await_bytes(tok.at[g, pl.ds(0, N)], tok_send.at[g, 4])
        return 0

    lax.fori_loop(0, CHUNKS, tokens_sent, 0)
    for it in range(ITERS):
        for batch in range(BATCHES):
            await_bytes(stats.at[it, batch, pl.ds(0, GROUP - 1)], st_send.at[it, batch])
        for half in range(2):
            for o in range(1, N):
                await_bytes(cod.at[it, 0, 0], c1_send.at[it, half, o - 1])
            for i in (0, 2):
                await_bytes(cod.at[it, 0], c2_send.at[it, half, i])
                await_bytes(cod.at[it, 0, pl.ds(0, N // 2)], c2_send.at[it, half, i + 1])
    for half in range(2):
        for o in range(1, N):
            await_bytes(fin.at[0, 0], f_send.at[half, o - 1])
            await_bytes(fin.at[0, 0], f_recv.at[half, o - 1])
        for p in range(N):
            start = (2 * p + half) * HALF
            cent_out[pl.ds(start, HALF)] = fin[half, p, pl.ds(0, HALF)]
            count_out[:, pl.ds(start, HALF)] = fin[half, p, pl.ds(HALF, 1), pl.ds(0, HALF)]


def on_device(tokens, codebook):
    vmem, dma = pltpu.VMEM, pltpu.SemaphoreType.DMA
    peers = N - 1
    centroids, counts = pl.pallas_call(
        em_kernel,
        out_shape=[jax.ShapeDtypeStruct((OWNED, D), F32), jax.ShapeDtypeStruct((1, OWNED), F32)],
        in_specs=[pl.BlockSpec(memory_space=pl.ANY)] * 2,
        out_specs=[pl.BlockSpec(memory_space=vmem)] * 2,
        scratch_shapes=[
            vmem((CHUNKS, GROUP, ROWS, D), F32),
            vmem((CHUNKS, TILE, D), BF16),
            vmem((CHUNKS, TILE, D), BF16),
            vmem((CHUNKS, 1, TILE), F32),
            vmem((ITERS, BLOCKS, N, HALF, D), F32),
            vmem((BLOCKS, BLOCK, D), BF16),
            vmem((BLOCKS, BLOCK, D), BF16),
            vmem((BLOCKS, BLOCK, 128), F32),
            vmem((BLOCKS, CHUNKS, BLOCK, TILE), F32),
            vmem((CHUNKS, 1, TILE), F32),
            vmem((CHUNKS, 1, TILE), F32),
            vmem((CHUNKS, 1, TILE), F32),
            vmem((CHUNKS, 1, TILE), F32),
            vmem((ITERS, BATCHES, GROUP, BATCH, 2, TILE), F32),
            vmem((BLOCKS, SUMS, D), F32),
            vmem((ITERS, 2, 2, SUMS, D), F32),
            vmem((ITERS, 2, LOW, D), F32),
            vmem((ITERS, 2, 2 * HALF, D), F32),
            vmem((2, N, HALF + 8, D), F32),
            vmem((ITERS, 2, peers, HALF + 8, D), F32),
            vmem((2, N, HALF + 8, D), F32),
            vmem((2, 128, 128), F32),
            dma((3,)),
            dma((CHUNKS, 5)),
            dma((CHUNKS, 5)),
            dma((ITERS, 2, peers)),
            dma((ITERS, 2, peers)),
            dma((ITERS, 2, 4)),
            dma((ITERS, 2, 4)),
            dma((ITERS, BATCHES)),
            dma((ITERS, BATCHES)),
            dma((ITERS, 2, 4)),
            dma((ITERS, 2, 4)),
            dma((ITERS, 2, peers)),
            dma((ITERS, 2, peers)),
            dma((2, peers)),
            dma((2, peers)),
        ],
        compiler_params=pltpu.CompilerParams(collective_id=0, has_side_effects=True, vmem_limit_bytes=56 << 20),
        cost_estimate=pl.CostEstimate(
            flops=ITERS * 2 * 3 * 2 * CHUNKS * TILE * BLOCKS * BLOCK * D,
            bytes_accessed=4 * (FRAMES + 2 * OWNED) * D,
            transcendentals=ITERS * 2 * CHUNKS * TILE * BLOCKS * BLOCK,
        ),
    )(tokens.reshape(CHUNKS, ROWS, D), codebook.reshape(N, 2, HALF, D))
    return centroids, counts.reshape(OWNED)


def solution(mesh):
    return jax.shard_map(
        on_device,
        mesh=mesh,
        in_specs=(P(("tok", "code"), None), P("code", None)),
        out_specs=(P("code", None), P("code")),
        check_vma=False,
    )
```

```python
import functools
import math

import jax
import jax.numpy as jnp
from jax import lax
from jax.experimental import pallas as pl
from jax.experimental.pallas import tpu as pltpu
from jax.sharding import PartitionSpec as P

MESH = pl.DeviceIdType.MESH
F32, BF16 = jnp.float32, jnp.bfloat16
ITERS = 2
PRIOR_WEIGHT = 1.0
N = 4
CORES = 2
GROUP = N * CORES
D = 256
FRAMES = 512
OWNED = 256
HALF = OWNED // N // 2
BLOCK = N * HALF
BLOCKS = 2 * N
CHUNKS = 8
ROWS = FRAMES // CHUNKS
TILE = GROUP * ROWS
LEAD = 4
AHEAD = 3
BATCH = 4
BATCHES = CHUNKS // BATCH
SUMS = BLOCK + 8
SHARPNESS = math.log2(math.e) / math.sqrt(D)
LAST = (((1,), (1,)), ((), ()))


def split(value):
    high = value.astype(BF16)
    return high, (value - high.astype(F32)).astype(BF16)


def em_kernel(
    frames, codebook, cent_out, count_out,
    tok, thi, tlo, tnorm, cod, chi, clo, cnorm, scores, tops, top, total, lognorm, stats, part, rs1, mid, rs2, fin, flip,
    own_sem, tok_send, tok_recv, c1_send, c1_recv, c2_send, c2_recv, st_send, st_recv,
    r1_send, r1_recv, r2_send, r2_recv, f_send, f_recv,
):
    z = lax.axis_index("tok")
    place = lax.axis_index("code")
    core = lax.rem(place, CORES)
    y = lax.rem(place // CORES, N)
    x = place // (CORES * N)
    mine = core * N + z

    def at(pz, px, py, pc):
        return (pz, (px * N + py) * CORES + pc)

    def ahead(p, o):
        return lax.rem(p + o, N)

    def remote(src, dst, send_sem, recv_sem, device):
        return pltpu.make_async_remote_copy(
            src_ref=src, dst_ref=dst, send_sem=send_sem, recv_sem=recv_sem, device_id=device, device_id_type=MESH
        )

    def await_bytes(ref, sem):
        pltpu.make_async_copy(ref, ref, sem).wait()

    def group_peer(j):
        peer = lax.rem(mine + j, GROUP)
        return at(lax.rem(peer, N), x, y, peer // N)

    barrier = pltpu.get_barrier_semaphore()
    peers = [at(z, ahead(x, o), y, core) for o in range(1, N)]
    peers += [at(z, x, ahead(y, o), core) for o in range(1, N)]
    peers += [group_peer(j) for j in range(1, GROUP)]
    for peer in peers:
        pl.semaphore_signal(barrier, inc=1, device_id=peer, device_id_type=MESH)
    pl.semaphore_wait(barrier, len(peers))

    def block_of(half, o):
        return ahead(y, o) if half == 0 else N + ahead(x, o)

    def across(half, o):
        return at(z, ahead(x, o), y, core) if half == 0 else at(z, x, ahead(y, o), core)

    def along(half, o):
        return at(z, x, ahead(y, o), core) if half == 0 else at(z, ahead(x, o), y, core)

    slot = (x, y)

    def start_stage1(it, half, src):
        dst = cod.at[it, block_of(half, 0), slot[half]]
        for o in (2, 1, 3):
            remote(src, dst, c1_send.at[it, half, o - 1], c1_recv.at[it, half, o - 1], across(half, o)).start()

    def await_stage1(it, half):
        for o in range(1, N):
            await_bytes(cod.at[it, 0, 0], c1_recv.at[it, half, o - 1])

    def start_stage2(it, half):
        block = cod.at[it, block_of(half, 0)]
        for o in (1, 3, 2):
            remote(block, block, c2_send.at[it, half, o - 1], c2_recv.at[it, half, o - 1], along(half, o)).start()

    def await_block(it, half, o):
        await_bytes(cod.at[it, 0], c2_recv.at[it, half, N - 1 - o])

    before, after = ahead(z, N - 1), ahead(z, 1)
    first = core * N

    def direct(g):
        remote(frames.at[g], tok.at[g, first + z], tok_send.at[g, 0], tok_recv.at[g, 0], at(after, x, y, core)).start()
        remote(frames.at[g], tok.at[g, first + z], tok_send.at[g, 1], tok_recv.at[g, 1], at(before, x, y, core)).start()

    def forward(g):
        await_bytes(tok.at[g, 0], tok_recv.at[g, 0])
        low = tok.at[g, first + before, pl.ds(0, ROWS // 2)]
        remote(low, low, tok_send.at[g, 2], tok_recv.at[g, 2], at(after, x, y, core)).start()
        await_bytes(tok.at[g, 0], tok_recv.at[g, 1])
        high = tok.at[g, first + after, pl.ds(ROWS // 2, ROWS // 2)]
        remote(high, high, tok_send.at[g, 3], tok_recv.at[g, 3], at(before, x, y, core)).start()

    def share(g):
        await_bytes(tok.at[g, 0, pl.ds(0, ROWS // 2)], tok_recv.at[g, 2])
        await_bytes(tok.at[g, 0, pl.ds(0, ROWS // 2)], tok_recv.at[g, 3])
        ours = tok.at[g, pl.ds(first, N)]
        remote(ours, ours, tok_send.at[g, 4], tok_recv.at[g, 4], at(z, x, y, 1 - core)).start()

    own_codes = [codebook.at[z, half] for half in range(2)]
    keep = [
        pltpu.make_async_copy(own_codes[0], cod.at[0, y, x], own_sem.at[0]),
        pltpu.make_async_copy(own_codes[1], cod.at[0, N + x, y], own_sem.at[1]),
        pltpu.make_async_copy(frames, tok.at[:, first + z], own_sem.at[2]),
    ]
    for half in range(2):
        start_stage1(0, half, own_codes[half])
    for copy in keep:
        copy.start()
    for g in range(LEAD):
        direct(g)
    for copy in keep:
        copy.wait()
    for half in range(2):
        await_stage1(0, half)
        start_stage2(0, half)
    for g in range(AHEAD):
        forward(g)
        direct(g + LEAD)
    for g in range(AHEAD + LEAD, CHUNKS):
        direct(g)
    share(0)
    for half in range(2):
        for o in range(1, N):
            await_block(0, half, o)

    def parts_of(codes):
        norms = jnp.sum(codes * codes, axis=1, keepdims=True) * SHARPNESS
        return *split(codes * (2.0 * SHARPNESS)), jnp.broadcast_to(norms, (codes.shape[0], 128))

    def split_block(b, _):
        chi[b], clo[b], cnorm[b] = parts_of(cod[0, b].reshape(BLOCK, D))
        return 0

    lax.fori_loop(0, BLOCKS, split_block, 0)

    def score(high, low, norms, g):
        inner = lax.dot_general(
            jnp.concatenate([high, high, low], axis=1),
            jnp.concatenate([thi[g], tlo[g], thi[g]], axis=1),
            LAST,
            preferred_element_type=F32,
        )
        return inner - jnp.tile(norms, (1, TILE // 128))

    def add_up(g, tiles, carry):
        old_top, old_total = carry if carry is not None else (None, None)
        new_top = tops[g] if carry is None else jnp.maximum(old_top, tops[g])
        new_total = None if carry is None else old_total * jnp.exp2(old_top - new_top)
        for tile in tiles:
            more = jnp.sum(jnp.exp2(tile - new_top), axis=0, keepdims=True)
            new_total = more if new_total is None else new_total + more
        return new_top, new_total

    def publish(it, g, row_top, row_total):
        norm = tnorm[g]
        score_top = row_top - norm
        stats[it, g // BATCH, mine, g % BATCH] = jnp.concatenate(
            [score_top, row_total * jnp.exp2(row_top - (score_top + norm))], axis=0
        )

    def send_stats(it, batch):
        own = stats.at[it, batch, mine]
        for j in range(1, GROUP):
            remote(own, own, st_send.at[it, batch], st_recv.at[it, batch], group_peer(j)).start()

    def normalise(it, batch):
        await_bytes(stats.at[it, batch, pl.ds(0, GROUP - 1)], st_recv.at[it, batch])
        for q in range(BATCH):
            g = batch * BATCH + q
            row_tops, totals = stats[it, batch, :, q, 0, :], stats[it, batch, :, q, 1, :]
            highest = jnp.max(row_tops, axis=0, keepdims=True)
            whole = jnp.sum(totals * jnp.exp2(row_tops - highest), axis=0, keepdims=True)
            lognorm[g] = (highest + tnorm[g]) + jnp.log2(whole)

    def score_tile(g):
        tile = tok[g].reshape(TILE, D)
        thi[g], tlo[g] = split(tile)
        squares = tile * tile
        squares = squares[:, :128] + squares[:, 128:]
        tnorm[g] = jnp.sum(squares.T, axis=0, keepdims=True) * SHARPNESS
        high, low = chi[...].reshape(BLOCKS * BLOCK, D), clo[...].reshape(BLOCKS * BLOCK, D)
        tile_scores = score(high, low, cnorm[...].reshape(BLOCKS * BLOCK, 128), g)
        scores[:, g] = tile_scores.reshape(BLOCKS, BLOCK, TILE)
        tops[g] = jnp.max(tile_scores, axis=0, keepdims=True)

    def sum_tile(g):
        publish(0, g, *add_up(g, [scores[:, g].reshape(BLOCKS * BLOCK, TILE)], None))

    def move_on(g):
        @pl.when(g + AHEAD < CHUNKS)
        def _():
            forward(g + AHEAD)

        @pl.when(g + 1 < CHUNKS)
        def _():
            share(g + 1)

        await_bytes(tok.at[g, pl.ds(0, N)], tok_recv.at[g, 4])

    move_on(0)
    score_tile(0)

    def step(g, _):
        move_on(g)
        sum_tile(g - 1)
        score_tile(g)

        @pl.when(g == BATCH)
        def _():
            send_stats(0, 0)

        return 0

    lax.fori_loop(1, CHUNKS, step, 0)
    sum_tile(CHUNKS - 1)
    send_stats(0, 1)

    def gray(i):
        return jnp.bitwise_xor(i, i // 2)

    def weigh(blocks, batch):
        lefts, rights, counts = [], [], None
        for q in range(BATCH):
            g = batch * BATCH + q
            pair_scores = jnp.concatenate([scores[b, g] for b in blocks], axis=0)
            weights = jnp.exp2(pair_scores - lognorm[g])
            for c in range(TILE // 128):
                piece = weights[:, c * 128 : (c + 1) * 128]
                counts = piece if counts is None else counts + piece
            high, low = split(weights)
            lefts += [high, high, low]
            rights += [thi[g], tlo[g], thi[g]]
        weighted = jnp.dot(jnp.concatenate(lefts, axis=1), jnp.concatenate(rights, axis=0), preferred_element_type=F32)
        for half in range(2):
            part[blocks[half], pl.ds(0, BLOCK)] += weighted[half * BLOCK : (half + 1) * BLOCK]
            row = jnp.sum(counts[half * BLOCK : (half + 1) * BLOCK].T, axis=0, keepdims=True)
            part[blocks[half], pl.ds(BLOCK, 8)] += jnp.broadcast_to(jnp.tile(row, (1, 2)), (8, D))

    def moments(it):
        part[...] = jnp.zeros_like(part)
        normalise(it, 0)

        def step(i, _):
            begin = i < 2 * BATCHES
            o = gray(N - 1 - jnp.where(begin, i % 2, i // 2))
            batch = jnp.where(begin, i // 2, i % 2)

            @pl.when(i == 2)
            def _():
                normalise(it, 1)

            blocks = [block_of(half, o) for half in range(2)]
            weigh(blocks, batch)

            @pl.when((batch == 1) & (o != 0))
            def _():
                for half in range(2):
                    remote(
                        part.at[blocks[half]], rs1.at[it, half, o - 1], r1_send.at[it, half, o - 1], r1_recv.at[it, half, o - 1], along(half, o)
                    ).start()

            return 0

        lax.fori_loop(0, N * BATCHES, step, 0)

    def reduce_sums(it, use):
        for half in range(2):
            for o in range(1, N):
                await_bytes(part.at[0], r1_recv.at[it, half, o - 1])
            row = part[block_of(half, 0)] + rs1[it, half, 0] + rs1[it, half, 1] + rs1[it, half, 2]
            for p in range(N):
                mid[half, p, pl.ds(0, HALF)] = row[p * HALF : (p + 1) * HALF]
                mid[half, p, pl.ds(HALF, 8)] = row[BLOCK:]
            for o in (2, 1, 3):
                remote(
                    mid.at[half, ahead(slot[half], o)], rs2.at[it, half, o - 1], r2_send.at[it, half, o - 1], r2_recv.at[it, half, o - 1], across(half, o)
                ).start()
        for half in range(2):
            for o in range(1, N):
                await_bytes(mid.at[0, 0], r2_recv.at[it, half, o - 1])
            sums = mid[half, slot[half]] + rs2[it, half, 0] + rs2[it, half, 1] + rs2[it, half, 2]
            flip[half] = jnp.broadcast_to(sums[HALF : HALF + 1, :128], (128, 128)).T
            count = flip[half, pl.ds(pl.multiple_of(slot[half] * HALF, HALF), HALF)]
            old = cod[it, block_of(half, 0), slot[half]]
            use(half, (sums[:HALF] + PRIOR_WEIGHT * old) / (jnp.tile(count, (1, 2)) + PRIOR_WEIGHT), count)

    def sent(it):
        for half in range(2):
            for o in range(1, N):
                await_bytes(part.at[0], r1_send.at[it, half, o - 1])
                await_bytes(mid.at[0, 0], r2_send.at[it, half, o - 1])

    def next_codes(half, codes, _):
        cod[1, block_of(half, 0), slot[half]] = codes
        start_stage1(1, half, cod.at[1, block_of(half, 0), slot[half]])

    moments(0)
    reduce_sums(0, next_codes)
    for half in range(2):
        await_stage1(1, half)
        start_stage2(1, half)

    def score_pair(o):
        blocks = [block_of(half, o) for half in range(2)]
        codes = jnp.concatenate([cod[1, b].reshape(BLOCK, D) for b in blocks], axis=0)
        high, low, norms = parts_of(codes)
        for g in range(CHUNKS):
            tile_scores = score(high, low, norms, g)
            for half in range(2):
                scores[blocks[half], g] = tile_scores[half * BLOCK : (half + 1) * BLOCK]
            tops[g] = jnp.max(tile_scores, axis=0, keepdims=True)

    def sum_pair(o, g):
        blocks = [block_of(half, o) for half in range(2)]
        return add_up(g, [scores[b, g] for b in blocks], (top[g], total[g]))

    top[...] = jnp.full_like(top, -1e30)
    total[...] = jnp.zeros_like(total)
    score_pair(0)

    def pair_step(i, _):
        o, previous = gray(i), gray(i - 1)
        for half in range(2):
            await_block(1, half, o)
        for g in range(CHUNKS):
            top[g], total[g] = sum_pair(previous, g)
        score_pair(o)
        return 0

    lax.fori_loop(1, N, pair_step, 0)

    def last_sum(batch, _):
        for q in range(BATCH):
            g = batch * BATCH + q
            publish(1, g, *sum_pair(N // 2, g))
        send_stats(1, batch)
        return 0

    lax.fori_loop(0, BATCHES, last_sum, 0)
    sent(0)
    moments(1)

    def last_codes(half, codes, count):
        fin[half, z, pl.ds(0, HALF)] = codes
        flip[half, pl.ds(0, HALF)] = count
        fin[half, z, pl.ds(HALF, 8)] = jnp.tile(flip[half].T[:8], (1, 2))
        own = fin.at[half, z]
        for o in (2, 1, 3):
            remote(own, own, f_send.at[half, o - 1], f_recv.at[half, o - 1], at(ahead(z, o), x, y, core)).start()

    reduce_sums(1, last_codes)
    sent(1)

    def tokens_sent(g, _):
        for i in range(2):
            await_bytes(tok.at[g, 0], tok_send.at[g, i])
            await_bytes(tok.at[g, 0, pl.ds(0, ROWS // 2)], tok_send.at[g, 2 + i])
        await_bytes(tok.at[g, pl.ds(0, N)], tok_send.at[g, 4])
        return 0

    lax.fori_loop(0, CHUNKS, tokens_sent, 0)
    for it in range(ITERS):
        for batch in range(BATCHES):
            await_bytes(stats.at[it, batch, pl.ds(0, GROUP - 1)], st_send.at[it, batch])
        for half in range(2):
            for o in range(1, N):
                await_bytes(cod.at[it, 0, 0], c1_send.at[it, half, o - 1])
                await_bytes(cod.at[it, 0], c2_send.at[it, half, o - 1])
    for half in range(2):
        for o in range(1, N):
            await_bytes(fin.at[0, 0], f_send.at[half, o - 1])
            await_bytes(fin.at[0, 0], f_recv.at[half, o - 1])
        for p in range(N):
            start = (2 * p + half) * HALF
            cent_out[pl.ds(start, HALF)] = fin[half, p, pl.ds(0, HALF)]
            count_out[:, pl.ds(start, HALF)] = fin[half, p, pl.ds(HALF, 1), pl.ds(0, HALF)]


def on_device(tokens, codebook):
    vmem, dma = pltpu.VMEM, pltpu.SemaphoreType.DMA
    peers = N - 1
    centroids, counts = pl.pallas_call(
        em_kernel,
        out_shape=[jax.ShapeDtypeStruct((OWNED, D), F32), jax.ShapeDtypeStruct((1, OWNED), F32)],
        in_specs=[pl.BlockSpec(memory_space=pl.ANY)] * 2,
        out_specs=[pl.BlockSpec(memory_space=vmem)] * 2,
        scratch_shapes=[
            vmem((CHUNKS, GROUP, ROWS, D), F32),
            vmem((CHUNKS, TILE, D), BF16),
            vmem((CHUNKS, TILE, D), BF16),
            vmem((CHUNKS, 1, TILE), F32),
            vmem((ITERS, BLOCKS, N, HALF, D), F32),
            vmem((BLOCKS, BLOCK, D), BF16),
            vmem((BLOCKS, BLOCK, D), BF16),
            vmem((BLOCKS, BLOCK, 128), F32),
            vmem((BLOCKS, CHUNKS, BLOCK, TILE), F32),
            vmem((CHUNKS, 1, TILE), F32),
            vmem((CHUNKS, 1, TILE), F32),
            vmem((CHUNKS, 1, TILE), F32),
            vmem((CHUNKS, 1, TILE), F32),
            vmem((ITERS, BATCHES, GROUP, BATCH, 2, TILE), F32),
            vmem((BLOCKS, SUMS, D), F32),
            vmem((ITERS, 2, peers, SUMS, D), F32),
            vmem((2, N, HALF + 8, D), F32),
            vmem((ITERS, 2, peers, HALF + 8, D), F32),
            vmem((2, N, HALF + 8, D), F32),
            vmem((2, 128, 128), F32),
            dma((3,)),
            dma((CHUNKS, 5)),
            dma((CHUNKS, 5)),
            dma((ITERS, 2, peers)),
            dma((ITERS, 2, peers)),
            dma((ITERS, 2, peers)),
            dma((ITERS, 2, peers)),
            dma((ITERS, BATCHES)),
            dma((ITERS, BATCHES)),
            dma((ITERS, 2, peers)),
            dma((ITERS, 2, peers)),
            dma((ITERS, 2, peers)),
            dma((ITERS, 2, peers)),
            dma((2, peers)),
            dma((2, peers)),
        ],
        compiler_params=pltpu.CompilerParams(collective_id=0, has_side_effects=True, vmem_limit_bytes=56 << 20),
        cost_estimate=pl.CostEstimate(
            flops=ITERS * 2 * 3 * 2 * CHUNKS * TILE * BLOCKS * BLOCK * D,
            bytes_accessed=4 * (FRAMES + 2 * OWNED) * D,
            transcendentals=ITERS * 2 * CHUNKS * TILE * BLOCKS * BLOCK,
        ),
    )(tokens.reshape(CHUNKS, ROWS, D), codebook.reshape(N, 2, HALF, D))
    return centroids, counts.reshape(OWNED)


def solution(mesh):
    return jax.shard_map(
        on_device,
        mesh=mesh,
        in_specs=(P(("tok", "code"), None), P("code", None)),
        out_specs=(P("code", None), P("code")),
        check_vma=False,
    )
```

```python
import functools
import math

import jax
import jax.numpy as jnp
from jax import lax
from jax.experimental import pallas as pl
from jax.experimental.pallas import tpu as pltpu
from jax.sharding import PartitionSpec as P

MESH = pl.DeviceIdType.MESH
F32, BF16 = jnp.float32, jnp.bfloat16
ITERS = 2
PRIOR_WEIGHT = 1.0
N = 4
CORES = 2
GROUP = N * CORES
D = 256
FRAMES = 512
OWNED = 256
HALF = OWNED // N // 2
BLOCK = N * HALF
BLOCKS = 2 * N
TILES = GROUP
TILE = FRAMES
PIECES = 4
ROWS = FRAMES // PIECES
BATCH = 4
BATCHES = TILES // BATCH
SUMS = BLOCK + 8
SHARPNESS = math.log2(math.e) / math.sqrt(D)
LAST = (((1,), (1,)), ((), ()))


def split(value):
    high = value.astype(BF16)
    return high, (value - high.astype(F32)).astype(BF16)


def em_kernel(
    frames, codebook, cent_out, count_out,
    tok, thi, tlo, tnorm, cod, chi, clo, cnorm, scores, tops, top, total, lognorm, stats, part, rs1, mid, rs2, fin, flip,
    own_sem, tok_send, tok_recv, share_send, share_recv, c1_send, c1_recv, c2_send, c2_recv, st_send, st_recv,
    r1_send, r1_recv, r2_send, r2_recv, f_send, f_recv,
):
    z = lax.axis_index("tok")
    place = lax.axis_index("code")
    core = lax.rem(place, CORES)
    y = lax.rem(place // CORES, N)
    x = place // (CORES * N)
    mine = core * N + z

    def at(pz, px, py, pc):
        return (pz, (px * N + py) * CORES + pc)

    def ahead(p, o):
        return lax.rem(p + o, N)

    def remote(src, dst, send_sem, recv_sem, device):
        return pltpu.make_async_remote_copy(
            src_ref=src, dst_ref=dst, send_sem=send_sem, recv_sem=recv_sem, device_id=device, device_id_type=MESH
        )

    def await_bytes(ref, sem):
        pltpu.make_async_copy(ref, ref, sem).wait()

    def group_peer(j):
        peer = lax.rem(mine + j, GROUP)
        return at(lax.rem(peer, N), x, y, peer // N)

    barrier = pltpu.get_barrier_semaphore()
    peers = [at(z, ahead(x, o), y, core) for o in range(1, N)]
    peers += [at(z, x, ahead(y, o), core) for o in range(1, N)]
    peers += [group_peer(j) for j in range(1, GROUP)]
    for peer in peers:
        pl.semaphore_signal(barrier, inc=1, device_id=peer, device_id_type=MESH)
    pl.semaphore_wait(barrier, len(peers))

    def block_of(half, o):
        return ahead(y, o) if half == 0 else N + ahead(x, o)

    def across(half, o):
        return at(z, ahead(x, o), y, core) if half == 0 else at(z, x, ahead(y, o), core)

    def along(half, o):
        return at(z, x, ahead(y, o), core) if half == 0 else at(z, ahead(x, o), y, core)

    slot = (x, y)

    def start_stage1(it, half, src):
        dst = cod.at[it, block_of(half, 0), slot[half]]
        for o in (2, 1, 3):
            remote(src, dst, c1_send.at[it, half, o - 1], c1_recv.at[it, half, o - 1], across(half, o)).start()

    def await_stage1(it, half):
        for o in range(1, N):
            await_bytes(cod.at[it, 0, 0], c1_recv.at[it, half, o - 1])

    def start_stage2(it, half):
        block = cod.at[it, block_of(half, 0)]
        for o in (1, 3, 2):
            remote(block, block, c2_send.at[it, half, o - 1], c2_recv.at[it, half, o - 1], along(half, o)).start()

    def await_block(it, half, o):
        await_bytes(cod.at[it, 0], c2_recv.at[it, half, N - 1 - o])

    before, after, opposite = ahead(z, N - 1), ahead(z, 1), ahead(z, 2)
    first, other = core * N, (1 - core) * N
    next_device, last_device = at(after, x, y, core), at(before, x, y, core)

    def rows_of(p, part=0, parts=1):
        return pl.ds(p * ROWS + part * (ROWS // parts), ROWS // parts)

    def direct(p):
        src, dst = frames.at[rows_of(p)], tok.at[first + z, rows_of(p)]
        remote(src, dst, tok_send.at[p, 0], tok_recv.at[p, 0], next_device).start()
        remote(src, dst, tok_send.at[p, 1], tok_recv.at[p, 1], last_device).start()

    def forward(p):
        await_bytes(tok.at[0, rows_of(p)], tok_recv.at[p, 0])
        low = tok.at[first + before, rows_of(p, 0, 2)]
        remote(low, low, tok_send.at[p, 2], tok_recv.at[p, 2], next_device).start()
        await_bytes(tok.at[0, rows_of(p)], tok_recv.at[p, 1])
        high = tok.at[first + after, rows_of(p, 1, 2)]
        remote(high, high, tok_send.at[p, 3], tok_recv.at[p, 3], last_device).start()

    def await_forwarded():
        for p in range(PIECES):
            await_bytes(tok.at[0, rows_of(p, 0, 2)], tok_recv.at[p, 2])
            await_bytes(tok.at[0, rows_of(p, 1, 2)], tok_recv.at[p, 3])

    def share(i, src, place):
        remote(src, tok.at[first + place], share_send.at[i], share_recv.at[i], at(z, x, y, 1 - core)).start()

    def await_shared(i):
        await_bytes(tok.at[0], share_recv.at[i])

    own_codes = [codebook.at[z, half] for half in range(2)]
    keep = [
        pltpu.make_async_copy(own_codes[0], cod.at[0, y, x], own_sem.at[0]),
        pltpu.make_async_copy(own_codes[1], cod.at[0, N + x, y], own_sem.at[1]),
        pltpu.make_async_copy(frames, tok.at[first + z], own_sem.at[2]),
    ]
    for half in range(2):
        start_stage1(0, half, own_codes[half])
    for copy in keep:
        copy.start()
    for p in range(PIECES):
        direct(p)
    share(0, frames, z)
    for copy in keep:
        copy.wait()
    for half in range(2):
        await_stage1(0, half)
        start_stage2(0, half)
    for half in range(2):
        for o in range(1, N):
            await_block(0, half, o)

    def parts_of(codes):
        norms = jnp.sum(codes * codes, axis=1, keepdims=True) * SHARPNESS
        return *split(codes * (2.0 * SHARPNESS)), jnp.broadcast_to(norms, (codes.shape[0], 128))

    def split_block(b, _):
        chi[b], clo[b], cnorm[b] = parts_of(cod[0, b].reshape(BLOCK, D))
        return 0

    lax.fori_loop(0, BLOCKS, split_block, 0)

    def score(high, low, norms, g):
        inner = lax.dot_general(
            jnp.concatenate([high, high, low], axis=1),
            jnp.concatenate([thi[g], tlo[g], thi[g]], axis=1),
            LAST,
            preferred_element_type=F32,
        )
        return inner - jnp.tile(norms, (1, TILE // 128))

    def add_up(g, tiles, carry):
        old_top, old_total = carry if carry is not None else (None, None)
        new_top = tops[g] if carry is None else jnp.maximum(old_top, tops[g])
        new_total = None if carry is None else old_total * jnp.exp2(old_top - new_top)
        for tile in tiles:
            more = jnp.sum(jnp.exp2(tile - new_top), axis=0, keepdims=True)
            new_total = more if new_total is None else new_total + more
        return new_top, new_total

    def publish(it, g, row_top, row_total):
        norm = tnorm[g]
        score_top = row_top - norm
        stats[it, g // BATCH, mine, g % BATCH] = jnp.concatenate(
            [score_top, row_total * jnp.exp2(row_top - (score_top + norm))], axis=0
        )

    def send_stats(it, batch):
        own = stats.at[it, batch, mine]
        for j in range(1, GROUP):
            remote(own, own, st_send.at[it, batch], st_recv.at[it, batch], group_peer(j)).start()

    def normalise(it, batch):
        await_bytes(stats.at[it, batch, pl.ds(0, GROUP - 1)], st_recv.at[it, batch])
        for q in range(BATCH):
            g = batch * BATCH + q
            row_tops, totals = stats[it, batch, :, q, 0, :], stats[it, batch, :, q, 1, :]
            highest = jnp.max(row_tops, axis=0, keepdims=True)
            whole = jnp.sum(totals * jnp.exp2(row_tops - highest), axis=0, keepdims=True)
            lognorm[g] = (highest + tnorm[g]) + jnp.log2(whole)

    def score_tile(g):
        tile = tok[g]
        thi[g], tlo[g] = split(tile)
        squares = tile * tile
        squares = squares[:, :128] + squares[:, 128:]
        tnorm[g] = jnp.sum(squares.T, axis=0, keepdims=True) * SHARPNESS
        high, low = chi[...].reshape(BLOCKS * BLOCK, D), clo[...].reshape(BLOCKS * BLOCK, D)
        tile_scores = score(high, low, cnorm[...].reshape(BLOCKS * BLOCK, 128), g)
        scores[:, g] = tile_scores.reshape(BLOCKS, BLOCK, TILE)
        tops[g] = jnp.max(tile_scores, axis=0, keepdims=True)

    def sum_tile(g):
        publish(0, g, *add_up(g, [scores[:, g].reshape(BLOCKS * BLOCK, TILE)], None))

    def source(i):
        place = jnp.where(i < 2, z, jnp.where(i < 6, jnp.where(i % 2 == 0, before, after), opposite))
        ours = (i == 0) | (i == 2) | (i == 3)
        return jnp.where(i < 6, jnp.where(ours, core, 1 - core), i - 6) * N + place

    def move_on(i):
        @pl.when(i == 1)
        def _():
            forward(0)
            forward(1)
            await_shared(0)

        @pl.when(i == 2)
        def _():
            forward(2)
            forward(3)
            share(1, tok.at[first + before], before)
            share(2, tok.at[first + after], after)

        @pl.when(i == 4)
        def _():
            await_shared(1)

        @pl.when(i == 5)
        def _():
            await_shared(2)

        @pl.when(i == 6)
        def _():
            await_forwarded()
            share(3, tok.at[first + opposite], opposite)
            await_shared(3)

    score_tile(source(0))

    def step(i, _):
        move_on(i)
        sum_tile(source(i - 1))
        score_tile(source(i))

        @pl.when(i == TILES - 1)
        def _():
            send_stats(0, 0)

        return 0

    lax.fori_loop(1, TILES, step, 0)
    sum_tile(source(TILES - 1))
    send_stats(0, 1)

    def gray(i):
        return jnp.bitwise_xor(i, i // 2)

    def weigh(blocks, batch):
        lefts, rights, counts = [], [], None
        for q in range(BATCH):
            g = batch * BATCH + q
            pair_scores = jnp.concatenate([scores[b, g] for b in blocks], axis=0)
            weights = jnp.exp2(pair_scores - lognorm[g])
            for c in range(TILE // 128):
                piece = weights[:, c * 128 : (c + 1) * 128]
                counts = piece if counts is None else counts + piece
            high, low = split(weights)
            lefts += [high, high, low]
            rights += [thi[g], tlo[g], thi[g]]
        weighted = jnp.dot(jnp.concatenate(lefts, axis=1), jnp.concatenate(rights, axis=0), preferred_element_type=F32)
        for half in range(2):
            part[blocks[half], pl.ds(0, BLOCK)] += weighted[half * BLOCK : (half + 1) * BLOCK]
            row = jnp.sum(counts[half * BLOCK : (half + 1) * BLOCK].T, axis=0, keepdims=True)
            part[blocks[half], pl.ds(BLOCK, 8)] += jnp.broadcast_to(jnp.tile(row, (1, 2)), (8, D))

    def moments(it):
        part[...] = jnp.zeros_like(part)
        normalise(it, 0)

        def step(i, _):
            o, batch = gray(N - 1 - i // BATCHES), i % BATCHES

            @pl.when(i == 1)
            def _():
                normalise(it, 1)

            blocks = [block_of(half, o) for half in range(2)]
            weigh(blocks, batch)

            @pl.when((batch == BATCHES - 1) & (o != 0))
            def _():
                for half in range(2):
                    remote(
                        part.at[blocks[half]], rs1.at[it, half, o - 1], r1_send.at[it, half, o - 1], r1_recv.at[it, half, o - 1], along(half, o)
                    ).start()

            return 0

        lax.fori_loop(0, N * BATCHES, step, 0)

    def reduce_sums(it, use):
        for half in range(2):
            for o in range(1, N):
                await_bytes(part.at[0], r1_recv.at[it, half, o - 1])
            row = part[block_of(half, 0)] + rs1[it, half, 0] + rs1[it, half, 1] + rs1[it, half, 2]
            for p in range(N):
                mid[half, p, pl.ds(0, HALF)] = row[p * HALF : (p + 1) * HALF]
                mid[half, p, pl.ds(HALF, 8)] = row[BLOCK:]
            for o in (2, 1, 3):
                remote(
                    mid.at[half, ahead(slot[half], o)], rs2.at[it, half, o - 1], r2_send.at[it, half, o - 1], r2_recv.at[it, half, o - 1], across(half, o)
                ).start()
        for half in range(2):
            for o in range(1, N):
                await_bytes(mid.at[0, 0], r2_recv.at[it, half, o - 1])
            sums = mid[half, slot[half]] + rs2[it, half, 0] + rs2[it, half, 1] + rs2[it, half, 2]
            flip[half] = jnp.broadcast_to(sums[HALF : HALF + 1, :128], (128, 128)).T
            count = flip[half, pl.ds(pl.multiple_of(slot[half] * HALF, HALF), HALF)]
            old = cod[it, block_of(half, 0), slot[half]]
            use(half, (sums[:HALF] + PRIOR_WEIGHT * old) / (jnp.tile(count, (1, 2)) + PRIOR_WEIGHT), count)

    def sent(it):
        for half in range(2):
            for o in range(1, N):
                await_bytes(part.at[0], r1_send.at[it, half, o - 1])
                await_bytes(mid.at[0, 0], r2_send.at[it, half, o - 1])

    def next_codes(half, codes, _):
        cod[1, block_of(half, 0), slot[half]] = codes
        start_stage1(1, half, cod.at[1, block_of(half, 0), slot[half]])

    moments(0)
    reduce_sums(0, next_codes)
    for half in range(2):
        await_stage1(1, half)
        start_stage2(1, half)

    def score_pair(o):
        blocks = [block_of(half, o) for half in range(2)]
        codes = jnp.concatenate([cod[1, b].reshape(BLOCK, D) for b in blocks], axis=0)
        high, low, norms = parts_of(codes)
        for g in range(TILES):
            tile_scores = score(high, low, norms, g)
            for half in range(2):
                scores[blocks[half], g] = tile_scores[half * BLOCK : (half + 1) * BLOCK]
            tops[g] = jnp.max(tile_scores, axis=0, keepdims=True)

    def sum_pair(o, g):
        blocks = [block_of(half, o) for half in range(2)]
        return add_up(g, [scores[b, g] for b in blocks], (top[g], total[g]))

    top[...] = jnp.full_like(top, -1e30)
    total[...] = jnp.zeros_like(total)
    score_pair(0)

    def pair_step(i, _):
        o, previous = gray(i), gray(i - 1)
        for half in range(2):
            await_block(1, half, o)
        for g in range(TILES):
            top[g], total[g] = sum_pair(previous, g)
        score_pair(o)
        return 0

    lax.fori_loop(1, N, pair_step, 0)

    def last_sum(batch, _):
        for q in range(BATCH):
            g = batch * BATCH + q
            publish(1, g, *sum_pair(N // 2, g))
        send_stats(1, batch)
        return 0

    lax.fori_loop(0, BATCHES, last_sum, 0)
    sent(0)
    moments(1)

    def last_codes(half, codes, count):
        fin[half, z, pl.ds(0, HALF)] = codes
        flip[half, pl.ds(0, HALF)] = count
        fin[half, z, pl.ds(HALF, 8)] = jnp.tile(flip[half].T[:8], (1, 2))
        own = fin.at[half, z]
        for o in (2, 1, 3):
            remote(own, own, f_send.at[half, o - 1], f_recv.at[half, o - 1], at(ahead(z, o), x, y, core)).start()

    reduce_sums(1, last_codes)
    sent(1)

    for p in range(PIECES):
        for i in range(2):
            await_bytes(tok.at[0, rows_of(p)], tok_send.at[p, i])
            await_bytes(tok.at[0, rows_of(p, 0, 2)], tok_send.at[p, 2 + i])
    for i in range(4):
        await_bytes(tok.at[0], share_send.at[i])
    for it in range(ITERS):
        for batch in range(BATCHES):
            await_bytes(stats.at[it, batch, pl.ds(0, GROUP - 1)], st_send.at[it, batch])
        for half in range(2):
            for o in range(1, N):
                await_bytes(cod.at[it, 0, 0], c1_send.at[it, half, o - 1])
                await_bytes(cod.at[it, 0], c2_send.at[it, half, o - 1])
    for half in range(2):
        for o in range(1, N):
            await_bytes(fin.at[0, 0], f_send.at[half, o - 1])
            await_bytes(fin.at[0, 0], f_recv.at[half, o - 1])
        for p in range(N):
            start = (2 * p + half) * HALF
            cent_out[pl.ds(start, HALF)] = fin[half, p, pl.ds(0, HALF)]
            count_out[:, pl.ds(start, HALF)] = fin[half, p, pl.ds(HALF, 1), pl.ds(0, HALF)]


def on_device(tokens, codebook):
    vmem, dma = pltpu.VMEM, pltpu.SemaphoreType.DMA
    peers = N - 1
    centroids, counts = pl.pallas_call(
        em_kernel,
        out_shape=[jax.ShapeDtypeStruct((OWNED, D), F32), jax.ShapeDtypeStruct((1, OWNED), F32)],
        in_specs=[pl.BlockSpec(memory_space=pl.ANY)] * 2,
        out_specs=[pl.BlockSpec(memory_space=vmem)] * 2,
        scratch_shapes=[
            vmem((TILES, TILE, D), F32),
            vmem((TILES, TILE, D), BF16),
            vmem((TILES, TILE, D), BF16),
            vmem((TILES, 1, TILE), F32),
            vmem((ITERS, BLOCKS, N, HALF, D), F32),
            vmem((BLOCKS, BLOCK, D), BF16),
            vmem((BLOCKS, BLOCK, D), BF16),
            vmem((BLOCKS, BLOCK, 128), F32),
            vmem((BLOCKS, TILES, BLOCK, TILE), F32),
            vmem((TILES, 1, TILE), F32),
            vmem((TILES, 1, TILE), F32),
            vmem((TILES, 1, TILE), F32),
            vmem((TILES, 1, TILE), F32),
            vmem((ITERS, BATCHES, GROUP, BATCH, 2, TILE), F32),
            vmem((BLOCKS, SUMS, D), F32),
            vmem((ITERS, 2, peers, SUMS, D), F32),
            vmem((2, N, HALF + 8, D), F32),
            vmem((ITERS, 2, peers, HALF + 8, D), F32),
            vmem((2, N, HALF + 8, D), F32),
            vmem((2, 128, 128), F32),
            dma((3,)),
            dma((PIECES, 4)),
            dma((PIECES, 4)),
            dma((4,)),
            dma((4,)),
            dma((ITERS, 2, peers)),
            dma((ITERS, 2, peers)),
            dma((ITERS, 2, peers)),
            dma((ITERS, 2, peers)),
            dma((ITERS, BATCHES)),
            dma((ITERS, BATCHES)),
            dma((ITERS, 2, peers)),
            dma((ITERS, 2, peers)),
            dma((ITERS, 2, peers)),
            dma((ITERS, 2, peers)),
            dma((2, peers)),
            dma((2, peers)),
        ],
        compiler_params=pltpu.CompilerParams(collective_id=0, has_side_effects=True, vmem_limit_bytes=56 << 20),
        cost_estimate=pl.CostEstimate(
            flops=ITERS * 2 * 3 * 2 * TILES * TILE * BLOCKS * BLOCK * D,
            bytes_accessed=4 * (FRAMES + 2 * OWNED) * D,
            transcendentals=ITERS * 2 * TILES * TILE * BLOCKS * BLOCK,
        ),
    )(tokens, codebook.reshape(N, 2, HALF, D))
    return centroids, counts.reshape(OWNED)


def solution(mesh):
    return jax.shard_map(
        on_device,
        mesh=mesh,
        in_specs=(P(("tok", "code"), None), P("code", None)),
        out_specs=(P("code", None), P("code")),
        check_vma=False,
    )
```

```python
import functools
import math

import jax
import jax.numpy as jnp
from jax import lax
from jax.experimental import pallas as pl
from jax.experimental.pallas import tpu as pltpu
from jax.sharding import PartitionSpec as P

MESH = pl.DeviceIdType.MESH
F32, BF16 = jnp.float32, jnp.bfloat16
ITERS = 2
PRIOR_WEIGHT = 1.0
N = 4
CORES = 2
GROUP = N * CORES
D = 256
FRAMES = 512
OWNED = 256
HALF = OWNED // N // 2
BLOCK = N * HALF
BLOCKS = 2 * N
TILES = GROUP
TILE = FRAMES
PIECES = 4
ROWS = FRAMES // PIECES
BATCH = 4
BATCHES = TILES // BATCH
SUMS = BLOCK + 8
SHARPNESS = math.log2(math.e) / math.sqrt(D)
LAST = (((1,), (1,)), ((), ()))


def split(value):
    high = value.astype(BF16)
    return high, (value - high.astype(F32)).astype(BF16)


def em_kernel(
    frames, codebook, cent_out, count_out,
    tok, thi, tlo, tnorm, cod, chi, clo, cnorm, scores, tops, top, total, lognorm, stats, part, rs1, mid, rs2, fin, flip,
    own_sem, tok_send, tok_recv, share_send, share_recv, c1_send, c1_recv, c2_send, c2_recv, st_send, st_recv,
    r1_send, r1_recv, r2_send, r2_recv, f_send, f_recv,
):
    z = lax.axis_index("tok")
    place = lax.axis_index("code")
    core = lax.rem(place, CORES)
    y = lax.rem(place // CORES, N)
    x = place // (CORES * N)
    mine = core * N + z

    def at(pz, px, py, pc):
        return (pz, (px * N + py) * CORES + pc)

    def ahead(p, o):
        return lax.rem(p + o, N)

    def remote(src, dst, send_sem, recv_sem, device):
        return pltpu.make_async_remote_copy(
            src_ref=src, dst_ref=dst, send_sem=send_sem, recv_sem=recv_sem, device_id=device, device_id_type=MESH
        )

    def await_bytes(ref, sem):
        pltpu.make_async_copy(ref, ref, sem).wait()

    def group_peer(j):
        peer = lax.rem(mine + j, GROUP)
        return at(lax.rem(peer, N), x, y, peer // N)

    barrier = pltpu.get_barrier_semaphore()
    peers = [at(z, ahead(x, o), y, core) for o in range(1, N)]
    peers += [at(z, x, ahead(y, o), core) for o in range(1, N)]
    peers += [group_peer(j) for j in range(1, GROUP)]
    for peer in peers:
        pl.semaphore_signal(barrier, inc=1, device_id=peer, device_id_type=MESH)
    pl.semaphore_wait(barrier, len(peers))

    def block_of(half, o):
        return ahead(y, o) if half == 0 else N + ahead(x, o)

    def across(half, o):
        return at(z, ahead(x, o), y, core) if half == 0 else at(z, x, ahead(y, o), core)

    def along(half, o):
        return at(z, x, ahead(y, o), core) if half == 0 else at(z, ahead(x, o), y, core)

    slot = (x, y)

    def start_stage1(it, half, src):
        dst = cod.at[it, block_of(half, 0), slot[half]]
        for o in (2, 1, 3):
            remote(src, dst, c1_send.at[it, half, o - 1], c1_recv.at[it, half, o - 1], across(half, o)).start()

    def await_stage1(it, half):
        for o in range(1, N):
            await_bytes(cod.at[it, 0, 0], c1_recv.at[it, half, o - 1])

    def start_stage2(it, half):
        block = cod.at[it, block_of(half, 0)]
        for o in (1, 3, 2):
            remote(block, block, c2_send.at[it, half, o - 1], c2_recv.at[it, half, o - 1], along(half, o)).start()

    def await_block(it, half, o):
        await_bytes(cod.at[it, 0], c2_recv.at[it, half, N - 1 - o])

    before, after, opposite = ahead(z, N - 1), ahead(z, 1), ahead(z, 2)
    first, other = core * N, (1 - core) * N
    next_device, last_device = at(after, x, y, core), at(before, x, y, core)

    def rows_of(p, part=0, parts=1):
        return pl.ds(p * ROWS + part * (ROWS // parts), ROWS // parts)

    def direct(p):
        src, dst = frames.at[rows_of(p)], tok.at[first + z, rows_of(p)]
        remote(src, dst, tok_send.at[p, 0], tok_recv.at[p, 0], next_device).start()
        remote(src, dst, tok_send.at[p, 1], tok_recv.at[p, 1], last_device).start()

    def forward(p):
        await_bytes(tok.at[0, rows_of(p)], tok_recv.at[p, 0])
        low = tok.at[first + before, rows_of(p, 0, 2)]
        remote(low, low, tok_send.at[p, 2], tok_recv.at[p, 2], next_device).start()
        await_bytes(tok.at[0, rows_of(p)], tok_recv.at[p, 1])
        high = tok.at[first + after, rows_of(p, 1, 2)]
        remote(high, high, tok_send.at[p, 3], tok_recv.at[p, 3], last_device).start()

    def await_forwarded():
        for p in range(PIECES):
            await_bytes(tok.at[0, rows_of(p, 0, 2)], tok_recv.at[p, 2])
            await_bytes(tok.at[0, rows_of(p, 1, 2)], tok_recv.at[p, 3])

    def share(i, src, place):
        remote(src, tok.at[first + place], share_send.at[i], share_recv.at[i], at(z, x, y, 1 - core)).start()

    def await_shared(i):
        await_bytes(tok.at[0], share_recv.at[i])

    own_codes = [codebook.at[z, half] for half in range(2)]
    keep = [
        pltpu.make_async_copy(own_codes[0], cod.at[0, y, x], own_sem.at[0]),
        pltpu.make_async_copy(own_codes[1], cod.at[0, N + x, y], own_sem.at[1]),
        pltpu.make_async_copy(frames, tok.at[first + z], own_sem.at[2]),
    ]
    for half in range(2):
        start_stage1(0, half, own_codes[half])
    for copy in keep:
        copy.start()
    for p in range(PIECES):
        direct(p)
    share(0, frames, z)
    for copy in keep:
        copy.wait()
    for half in range(2):
        await_stage1(0, half)
        start_stage2(0, half)
    forward(0)
    forward(1)
    for half in range(2):
        for o in range(1, N):
            await_block(0, half, o)

    def parts_of(codes):
        norms = jnp.sum(codes * codes, axis=1, keepdims=True) * SHARPNESS
        return *split(codes * (2.0 * SHARPNESS)), jnp.broadcast_to(norms, (codes.shape[0], 128))

    def split_block(b, _):
        chi[b], clo[b], cnorm[b] = parts_of(cod[0, b].reshape(BLOCK, D))
        return 0

    lax.fori_loop(0, BLOCKS, split_block, 0)

    def score(high, low, norms, g):
        inner = lax.dot_general(
            jnp.concatenate([high, high, low], axis=1),
            jnp.concatenate([thi[g], tlo[g], thi[g]], axis=1),
            LAST,
            preferred_element_type=F32,
        )
        return inner - jnp.tile(norms, (1, TILE // 128))

    def add_up(g, tiles, carry):
        old_top, old_total = carry if carry is not None else (None, None)
        new_top = tops[g] if carry is None else jnp.maximum(old_top, tops[g])
        new_total = None if carry is None else old_total * jnp.exp2(old_top - new_top)
        for tile in tiles:
            more = jnp.sum(jnp.exp2(tile - new_top), axis=0, keepdims=True)
            new_total = more if new_total is None else new_total + more
        return new_top, new_total

    def publish(it, g, row_top, row_total):
        norm = tnorm[g]
        shift = (row_top - norm) + norm
        stats[it, g // BATCH, mine, g % BATCH] = shift + jnp.log2(row_total * jnp.exp2(row_top - shift))

    def send_stats(it, batch):
        own = stats.at[it, batch, mine]
        for j in range(1, GROUP):
            remote(own, own, st_send.at[it, batch], st_recv.at[it, batch], group_peer(j)).start()

    def normalise(it, batch):
        await_bytes(stats.at[it, batch, pl.ds(0, GROUP - 1)], st_recv.at[it, batch])
        for q in range(BATCH):
            g = batch * BATCH + q
            logs = stats[it, batch, :, q, 0, :]
            highest = jnp.max(logs, axis=0, keepdims=True)
            lognorm[g] = highest + jnp.log2(jnp.sum(jnp.exp2(logs - highest), axis=0, keepdims=True))

    def score_tile(g):
        tile = tok[g]
        thi[g], tlo[g] = split(tile)
        squares = tile * tile
        squares = squares[:, :128] + squares[:, 128:]
        tnorm[g] = jnp.sum(squares.T, axis=0, keepdims=True) * SHARPNESS
        high, low = chi[...].reshape(BLOCKS * BLOCK, D), clo[...].reshape(BLOCKS * BLOCK, D)
        tile_scores = score(high, low, cnorm[...].reshape(BLOCKS * BLOCK, 128), g)
        scores[:, g] = tile_scores.reshape(BLOCKS, BLOCK, TILE)
        tops[g] = jnp.max(tile_scores, axis=0, keepdims=True)

    def sum_tile(g):
        publish(0, g, *add_up(g, [scores[:, g].reshape(BLOCKS * BLOCK, TILE)], None))

    def source(i):
        place = jnp.where(i < 2, z, jnp.where(i < 6, jnp.where(i % 2 == 0, before, after), opposite))
        ours = (i == 0) | (i == 2) | (i == 3)
        return jnp.where(i < 6, jnp.where(ours, core, 1 - core), i - 6) * N + place

    def move_on(i):
        @pl.when(i == 1)
        def _():
            forward(2)
            await_shared(0)

        @pl.when(i == 2)
        def _():
            forward(3)
            share(1, tok.at[first + before], before)
            share(2, tok.at[first + after], after)

        @pl.when(i == 4)
        def _():
            await_shared(1)

        @pl.when(i == 5)
        def _():
            await_shared(2)

        @pl.when(i == 6)
        def _():
            await_forwarded()
            share(3, tok.at[first + opposite], opposite)
            await_shared(3)

    score_tile(source(0))

    def step(i, _):
        move_on(i)
        sum_tile(source(i - 1))
        score_tile(source(i))

        @pl.when(i == TILES - 1)
        def _():
            send_stats(0, 0)

        return 0

    lax.fori_loop(1, TILES, step, 0)
    sum_tile(source(TILES - 1))
    send_stats(0, 1)

    def gray(i):
        return jnp.bitwise_xor(i, i // 2)

    def weigh(blocks, batch):
        lefts, rights, counts = [], [], None
        for q in range(BATCH):
            g = batch * BATCH + q
            pair_scores = jnp.concatenate([scores[b, g] for b in blocks], axis=0)
            weights = jnp.exp2(pair_scores - lognorm[g])
            for c in range(TILE // 128):
                piece = weights[:, c * 128 : (c + 1) * 128]
                counts = piece if counts is None else counts + piece
            high, low = split(weights)
            lefts += [high, high, low]
            rights += [thi[g], tlo[g], thi[g]]
        weighted = jnp.dot(jnp.concatenate(lefts, axis=1), jnp.concatenate(rights, axis=0), preferred_element_type=F32)
        for half in range(2):
            part[blocks[half], pl.ds(0, BLOCK)] += weighted[half * BLOCK : (half + 1) * BLOCK]
            row = jnp.sum(counts[half * BLOCK : (half + 1) * BLOCK].T, axis=0, keepdims=True)
            part[blocks[half], pl.ds(BLOCK, 8)] += jnp.broadcast_to(jnp.tile(row, (1, 2)), (8, D))

    def moments(it):
        part[...] = jnp.zeros_like(part)
        normalise(it, 0)

        def step(i, _):
            o, batch = gray(N - 1 - i // BATCHES), i % BATCHES

            @pl.when(i == 1)
            def _():
                normalise(it, 1)

            blocks = [block_of(half, o) for half in range(2)]
            weigh(blocks, batch)

            @pl.when((batch == BATCHES - 1) & (o != 0))
            def _():
                for half in range(2):
                    remote(
                        part.at[blocks[half]], rs1.at[it, half, o - 1], r1_send.at[it, half, o - 1], r1_recv.at[it, half, o - 1], along(half, o)
                    ).start()

            return 0

        lax.fori_loop(0, N * BATCHES, step, 0)

    def reduce_sums(it, use):
        for half in range(2):
            for o in range(1, N):
                await_bytes(part.at[0], r1_recv.at[it, half, o - 1])
            row = part[block_of(half, 0)] + rs1[it, half, 0] + rs1[it, half, 1] + rs1[it, half, 2]
            for p in range(N):
                mid[half, p, pl.ds(0, HALF)] = row[p * HALF : (p + 1) * HALF]
                mid[half, p, pl.ds(HALF, 8)] = row[BLOCK:]
            for o in (2, 1, 3):
                remote(
                    mid.at[half, ahead(slot[half], o)], rs2.at[it, half, o - 1], r2_send.at[it, half, o - 1], r2_recv.at[it, half, o - 1], across(half, o)
                ).start()
        for half in range(2):
            for o in range(1, N):
                await_bytes(mid.at[0, 0], r2_recv.at[it, half, o - 1])
            sums = mid[half, slot[half]] + rs2[it, half, 0] + rs2[it, half, 1] + rs2[it, half, 2]
            flip[half] = jnp.broadcast_to(sums[HALF : HALF + 1, :128], (128, 128)).T
            count = flip[half, pl.ds(pl.multiple_of(slot[half] * HALF, HALF), HALF)]
            old = cod[it, block_of(half, 0), slot[half]]
            use(half, (sums[:HALF] + PRIOR_WEIGHT * old) / (jnp.tile(count, (1, 2)) + PRIOR_WEIGHT), count)

    def sent(it):
        for half in range(2):
            for o in range(1, N):
                await_bytes(part.at[0], r1_send.at[it, half, o - 1])
                await_bytes(mid.at[0, 0], r2_send.at[it, half, o - 1])

    def next_codes(half, codes, _):
        cod[1, block_of(half, 0), slot[half]] = codes
        start_stage1(1, half, cod.at[1, block_of(half, 0), slot[half]])

    moments(0)
    reduce_sums(0, next_codes)
    for half in range(2):
        await_stage1(1, half)
        start_stage2(1, half)

    def score_pair(o):
        blocks = [block_of(half, o) for half in range(2)]
        codes = jnp.concatenate([cod[1, b].reshape(BLOCK, D) for b in blocks], axis=0)
        high, low, norms = parts_of(codes)
        for g in range(TILES):
            tile_scores = score(high, low, norms, g)
            for half in range(2):
                scores[blocks[half], g] = tile_scores[half * BLOCK : (half + 1) * BLOCK]
            tops[g] = jnp.max(tile_scores, axis=0, keepdims=True)

    def sum_pair(o, g):
        blocks = [block_of(half, o) for half in range(2)]
        return add_up(g, [scores[b, g] for b in blocks], (top[g], total[g]))

    top[...] = jnp.full_like(top, -1e30)
    total[...] = jnp.zeros_like(total)
    score_pair(0)

    def pair_step(i, _):
        o, previous = gray(i), gray(i - 1)
        for half in range(2):
            await_block(1, half, o)
        for g in range(TILES):
            top[g], total[g] = sum_pair(previous, g)
        score_pair(o)
        return 0

    lax.fori_loop(1, N, pair_step, 0)

    def last_sum(batch, _):
        for q in range(BATCH):
            g = batch * BATCH + q
            publish(1, g, *sum_pair(N // 2, g))
        send_stats(1, batch)
        return 0

    lax.fori_loop(0, BATCHES, last_sum, 0)
    sent(0)
    moments(1)

    def last_codes(half, codes, count):
        fin[z, pl.ds(half * HALF, HALF)] = codes
        flip[2, pl.ds(half * HALF, HALF)] = count

    flip[2] = jnp.zeros((128, 128), F32)
    reduce_sums(1, last_codes)
    fin[z, pl.ds(2 * HALF, 8)] = jnp.tile(flip[2].T[:8], (1, 2))
    for o in (2, 1, 3):
        remote(fin.at[z], fin.at[z], f_send.at[o - 1], f_recv.at[o - 1], at(ahead(z, o), x, y, core)).start()
    sent(1)

    for p in range(PIECES):
        for i in range(2):
            await_bytes(tok.at[0, rows_of(p)], tok_send.at[p, i])
            await_bytes(tok.at[0, rows_of(p, 0, 2)], tok_send.at[p, 2 + i])
    for i in range(4):
        await_bytes(tok.at[0], share_send.at[i])
    for it in range(ITERS):
        for batch in range(BATCHES):
            await_bytes(stats.at[it, batch, pl.ds(0, GROUP - 1)], st_send.at[it, batch])
        for half in range(2):
            for o in range(1, N):
                await_bytes(cod.at[it, 0, 0], c1_send.at[it, half, o - 1])
                await_bytes(cod.at[it, 0], c2_send.at[it, half, o - 1])
    for o in range(1, N):
        await_bytes(fin.at[0], f_send.at[o - 1])
        await_bytes(fin.at[0], f_recv.at[o - 1])
    for p in range(N):
        cent_out[pl.ds(p * 2 * HALF, 2 * HALF)] = fin[p, pl.ds(0, 2 * HALF)]
        count_out[:, pl.ds(p * 2 * HALF, 2 * HALF)] = fin[p, pl.ds(2 * HALF, 1), pl.ds(0, 2 * HALF)]


def on_device(tokens, codebook):
    vmem, dma = pltpu.VMEM, pltpu.SemaphoreType.DMA
    peers = N - 1
    centroids, counts = pl.pallas_call(
        em_kernel,
        out_shape=[jax.ShapeDtypeStruct((OWNED, D), F32), jax.ShapeDtypeStruct((1, OWNED), F32)],
        in_specs=[pl.BlockSpec(memory_space=pl.ANY)] * 2,
        out_specs=[pl.BlockSpec(memory_space=vmem)] * 2,
        scratch_shapes=[
            vmem((TILES, TILE, D), F32),
            vmem((TILES, TILE, D), BF16),
            vmem((TILES, TILE, D), BF16),
            vmem((TILES, 1, TILE), F32),
            vmem((ITERS, BLOCKS, N, HALF, D), F32),
            vmem((BLOCKS, BLOCK, D), BF16),
            vmem((BLOCKS, BLOCK, D), BF16),
            vmem((BLOCKS, BLOCK, 128), F32),
            vmem((BLOCKS, TILES, BLOCK, TILE), F32),
            vmem((TILES, 1, TILE), F32),
            vmem((TILES, 1, TILE), F32),
            vmem((TILES, 1, TILE), F32),
            vmem((TILES, 1, TILE), F32),
            vmem((ITERS, BATCHES, GROUP, BATCH, 1, TILE), F32),
            vmem((BLOCKS, SUMS, D), F32),
            vmem((ITERS, 2, peers, SUMS, D), F32),
            vmem((2, N, HALF + 8, D), F32),
            vmem((ITERS, 2, peers, HALF + 8, D), F32),
            vmem((N, 2 * HALF + 8, D), F32),
            vmem((3, 128, 128), F32),
            dma((3,)),
            dma((PIECES, 4)),
            dma((PIECES, 4)),
            dma((4,)),
            dma((4,)),
            dma((ITERS, 2, peers)),
            dma((ITERS, 2, peers)),
            dma((ITERS, 2, peers)),
            dma((ITERS, 2, peers)),
            dma((ITERS, BATCHES)),
            dma((ITERS, BATCHES)),
            dma((ITERS, 2, peers)),
            dma((ITERS, 2, peers)),
            dma((ITERS, 2, peers)),
            dma((ITERS, 2, peers)),
            dma((peers,)),
            dma((peers,)),
        ],
        compiler_params=pltpu.CompilerParams(collective_id=0, has_side_effects=True, vmem_limit_bytes=56 << 20),
        cost_estimate=pl.CostEstimate(
            flops=ITERS * 2 * 3 * 2 * TILES * TILE * BLOCKS * BLOCK * D,
            bytes_accessed=4 * (FRAMES + 2 * OWNED) * D,
            transcendentals=ITERS * 2 * TILES * TILE * BLOCKS * BLOCK,
        ),
    )(tokens, codebook.reshape(N, 2, HALF, D))
    return centroids, counts.reshape(OWNED)


def solution(mesh):
    return jax.shard_map(
        on_device,
        mesh=mesh,
        in_specs=(P(("tok", "code"), None), P("code", None)),
        out_specs=(P("code", None), P("code")),
        check_vma=False,
    )
```

```python
import functools
import math

import jax
import jax.numpy as jnp
from jax import lax
from jax.experimental import pallas as pl
from jax.experimental.pallas import tpu as pltpu
from jax.sharding import PartitionSpec as P

MESH = pl.DeviceIdType.MESH
F32, BF16 = jnp.float32, jnp.bfloat16
ITERS = 2
PRIOR_WEIGHT = 1.0
N = 4
CORES = 2
GROUP = N * CORES
D = 256
FRAMES = 512
OWNED = 256
HALF = OWNED // N // 2
BLOCK = N * HALF
BLOCKS = 2 * N
TILES = GROUP
TILE = FRAMES
PIECES = 4
ROWS = FRAMES // PIECES
BATCH = 4
BATCHES = TILES // BATCH
SUMS = BLOCK + 8
SHARPNESS = math.log2(math.e) / math.sqrt(D)
LAST = (((1,), (1,)), ((), ()))


def split(value):
    high = value.astype(BF16)
    return high, (value - high.astype(F32)).astype(BF16)


def em_kernel(
    frames, codebook, cent_out, count_out,
    tok, thi, tlo, tnorm, cod, chi, clo, cnorm, scores, tops, top, total, lognorm, stats, part, rs1, mid, rs2, fin, flip,
    own_sem, tok_send, tok_recv, share_send, share_recv, c1_send, c1_recv, c2_send, c2_recv, st_send, st_recv,
    r1_send, r1_recv, r2_send, r2_recv, f_send, f_recv,
):
    z = lax.axis_index("tok")
    place = lax.axis_index("code")
    core = lax.rem(place, CORES)
    y = lax.rem(place // CORES, N)
    x = place // (CORES * N)
    mine = core * N + z

    def at(pz, px, py, pc):
        return (pz, (px * N + py) * CORES + pc)

    def ahead(p, o):
        return lax.rem(p + o, N)

    def remote(src, dst, send_sem, recv_sem, device):
        return pltpu.make_async_remote_copy(
            src_ref=src, dst_ref=dst, send_sem=send_sem, recv_sem=recv_sem, device_id=device, device_id_type=MESH
        )

    def await_bytes(ref, sem):
        pltpu.make_async_copy(ref, ref, sem).wait()

    def group_peer(j):
        peer = lax.rem(mine + j, GROUP)
        return at(lax.rem(peer, N), x, y, peer // N)

    barrier = pltpu.get_barrier_semaphore()
    peers = [at(z, ahead(x, o), y, core) for o in range(1, N)]
    peers += [at(z, x, ahead(y, o), core) for o in range(1, N)]
    peers += [group_peer(j) for j in range(1, GROUP)]
    for peer in peers:
        pl.semaphore_signal(barrier, inc=1, device_id=peer, device_id_type=MESH)
    pl.semaphore_wait(barrier, len(peers))

    def block_of(half, o):
        return ahead(y, o) if half == 0 else N + ahead(x, o)

    def across(half, o):
        return at(z, ahead(x, o), y, core) if half == 0 else at(z, x, ahead(y, o), core)

    def along(half, o):
        return at(z, x, ahead(y, o), core) if half == 0 else at(z, ahead(x, o), y, core)

    slot = (x, y)

    def start_stage1(it, half, src):
        dst = cod.at[it, block_of(half, 0), slot[half]]
        for o in (2, 1, 3):
            remote(src, dst, c1_send.at[it, half, o - 1], c1_recv.at[it, half, o - 1], across(half, o)).start()

    def await_stage1(it, half):
        for o in range(1, N):
            await_bytes(cod.at[it, 0, 0], c1_recv.at[it, half, o - 1])

    def start_stage2(it, half, places):
        block = cod.at[it, block_of(half, 0)]
        for o in places:
            remote(block, block, c2_send.at[it, half, o - 1], c2_recv.at[it, half, o - 1], along(half, o)).start()

    def await_block(it, half, o):
        await_bytes(cod.at[it, 0], c2_recv.at[it, half, N - 1 - o])

    before, after, opposite = ahead(z, N - 1), ahead(z, 1), ahead(z, 2)
    first, other = core * N, (1 - core) * N
    next_device, last_device = at(after, x, y, core), at(before, x, y, core)

    def rows_of(p, part=0, parts=1):
        return pl.ds(p * ROWS + part * (ROWS // parts), ROWS // parts)

    def direct(p):
        src, dst = frames.at[rows_of(p)], tok.at[first + z, rows_of(p)]
        remote(src, dst, tok_send.at[p, 0], tok_recv.at[p, 0], next_device).start()
        remote(src, dst, tok_send.at[p, 1], tok_recv.at[p, 1], last_device).start()

    def forward(p):
        await_bytes(tok.at[0, rows_of(p)], tok_recv.at[p, 0])
        low = tok.at[first + before, rows_of(p, 0, 2)]
        remote(low, low, tok_send.at[p, 2], tok_recv.at[p, 2], next_device).start()
        await_bytes(tok.at[0, rows_of(p)], tok_recv.at[p, 1])
        high = tok.at[first + after, rows_of(p, 1, 2)]
        remote(high, high, tok_send.at[p, 3], tok_recv.at[p, 3], last_device).start()

    def await_forwarded():
        for p in range(PIECES):
            await_bytes(tok.at[0, rows_of(p, 0, 2)], tok_recv.at[p, 2])
            await_bytes(tok.at[0, rows_of(p, 1, 2)], tok_recv.at[p, 3])

    def share(i, src, place):
        remote(src, tok.at[first + place], share_send.at[i], share_recv.at[i], at(z, x, y, 1 - core)).start()

    def await_shared(i):
        await_bytes(tok.at[0], share_recv.at[i])

    own_codes = [codebook.at[z, half] for half in range(2)]
    keep = [
        pltpu.make_async_copy(own_codes[0], cod.at[0, y, x], own_sem.at[0]),
        pltpu.make_async_copy(own_codes[1], cod.at[0, N + x, y], own_sem.at[1]),
        pltpu.make_async_copy(frames, tok.at[first + z], own_sem.at[2]),
    ]
    for half in range(2):
        start_stage1(0, half, own_codes[half])
    for copy in keep:
        copy.start()
    for p in range(PIECES):
        direct(p)
    share(0, frames, z)
    for copy in keep:
        copy.wait()
    for half in range(2):
        await_stage1(0, half)
        start_stage2(0, half, (1, 3, 2))
    forward(0)
    forward(1)
    for half in range(2):
        for o in range(1, N):
            await_block(0, half, o)

    def parts_of(codes):
        norms = jnp.sum(codes * codes, axis=1, keepdims=True) * SHARPNESS
        return *split(codes * (2.0 * SHARPNESS)), jnp.broadcast_to(norms, (codes.shape[0], 128))

    def split_block(b, _):
        chi[b], clo[b], cnorm[b] = parts_of(cod[0, b].reshape(BLOCK, D))
        return 0

    lax.fori_loop(0, BLOCKS, split_block, 0)

    def score(high, low, norms, g):
        inner = lax.dot_general(
            jnp.concatenate([high, high, low], axis=1),
            jnp.concatenate([thi[g], tlo[g], thi[g]], axis=1),
            LAST,
            preferred_element_type=F32,
        )
        return inner - jnp.tile(norms, (1, TILE // 128))

    def add_up(g, tiles, carry):
        old_top, old_total = carry if carry is not None else (None, None)
        new_top = tops[g] if carry is None else jnp.maximum(old_top, tops[g])
        new_total = None if carry is None else old_total * jnp.exp2(old_top - new_top)
        for tile in tiles:
            more = jnp.sum(jnp.exp2(tile - new_top), axis=0, keepdims=True)
            new_total = more if new_total is None else new_total + more
        return new_top, new_total

    def publish(it, g, row_top, row_total):
        norm = tnorm[g]
        shift = (row_top - norm) + norm
        stats[it, g // BATCH, mine, g % BATCH] = shift + jnp.log2(row_total * jnp.exp2(row_top - shift))

    def send_stats(it, batch):
        own = stats.at[it, batch, mine]
        for j in range(1, GROUP):
            remote(own, own, st_send.at[it, batch], st_recv.at[it, batch], group_peer(j)).start()

    def normalise(it, batch):
        await_bytes(stats.at[it, batch, pl.ds(0, GROUP - 1)], st_recv.at[it, batch])
        for q in range(BATCH):
            g = batch * BATCH + q
            logs = stats[it, batch, :, q, 0, :]
            highest = jnp.max(logs, axis=0, keepdims=True)
            lognorm[g] = highest + jnp.log2(jnp.sum(jnp.exp2(logs - highest), axis=0, keepdims=True))

    def score_tile(g):
        tile = tok[g]
        thi[g], tlo[g] = split(tile)
        squares = tile * tile
        squares = squares[:, :128] + squares[:, 128:]
        tnorm[g] = jnp.sum(squares.T, axis=0, keepdims=True) * SHARPNESS
        high, low = chi[...].reshape(BLOCKS * BLOCK, D), clo[...].reshape(BLOCKS * BLOCK, D)
        tile_scores = score(high, low, cnorm[...].reshape(BLOCKS * BLOCK, 128), g)
        scores[:, g] = tile_scores.reshape(BLOCKS, BLOCK, TILE)
        tops[g] = jnp.max(tile_scores, axis=0, keepdims=True)

    def sum_tile(g):
        publish(0, g, *add_up(g, [scores[:, g].reshape(BLOCKS * BLOCK, TILE)], None))

    def source(i):
        place = jnp.where(i < 2, z, jnp.where(i < 6, jnp.where(i % 2 == 0, before, after), opposite))
        ours = (i == 0) | (i == 2) | (i == 3)
        return jnp.where(i < 6, jnp.where(ours, core, 1 - core), i - 6) * N + place

    def move_on(i):
        @pl.when(i == 1)
        def _():
            forward(2)
            await_shared(0)

        @pl.when(i == 2)
        def _():
            forward(3)
            share(1, tok.at[first + before], before)
            share(2, tok.at[first + after], after)

        @pl.when(i == 4)
        def _():
            await_shared(1)

        @pl.when(i == 5)
        def _():
            await_shared(2)

        @pl.when(i == 6)
        def _():
            await_forwarded()
            share(3, tok.at[first + opposite], opposite)
            await_shared(3)

    score_tile(source(0))

    def step(i, _):
        move_on(i)
        sum_tile(source(i - 1))
        score_tile(source(i))

        @pl.when(i == TILES - 1)
        def _():
            send_stats(0, 0)

        return 0

    lax.fori_loop(1, TILES, step, 0)
    sum_tile(source(TILES - 1))
    send_stats(0, 1)

    def gray(i):
        return jnp.bitwise_xor(i, i // 2)

    def weigh(blocks, tiles):
        lefts, rights, counts = [], [], None
        for g in tiles:
            pair_scores = jnp.concatenate([scores[b, g] for b in blocks], axis=0)
            weights = jnp.exp2(pair_scores - lognorm[g])
            for c in range(TILE // 128):
                piece = weights[:, c * 128 : (c + 1) * 128]
                counts = piece if counts is None else counts + piece
            high, low = split(weights)
            lefts += [high, high, low]
            rights += [thi[g], tlo[g], thi[g]]
        weighted = jnp.dot(jnp.concatenate(lefts, axis=1), jnp.concatenate(rights, axis=0), preferred_element_type=F32)
        for half in range(2):
            part[blocks[half], pl.ds(0, BLOCK)] += weighted[half * BLOCK : (half + 1) * BLOCK]
            row = jnp.sum(counts[half * BLOCK : (half + 1) * BLOCK].T, axis=0, keepdims=True)
            part[blocks[half], pl.ds(BLOCK, 8)] += jnp.broadcast_to(jnp.tile(row, (1, 2)), (8, D))

    def moments(it):
        batches = BATCHES if it == 0 else 1
        part[...] = jnp.zeros_like(part)
        normalise(it, 0)
        if batches == 1:
            normalise(it, 1)

        def step(i, _):
            o, batch = gray(N - 1 - i // batches), i % batches

            if batches > 1:

                @pl.when(i == 1)
                def _():
                    normalise(it, 1)

            blocks = [block_of(half, o) for half in range(2)]
            size = TILES // batches
            weigh(blocks, [batch * size + q for q in range(size)])

            @pl.when((batch == batches - 1) & (o != 0))
            def _():
                for half in range(2):
                    remote(
                        part.at[blocks[half]], rs1.at[it, half, o - 1], r1_send.at[it, half, o - 1], r1_recv.at[it, half, o - 1], along(half, o)
                    ).start()

            return 0

        lax.fori_loop(0, N * batches, step, 0)

    def reduce_sums(it, use):
        for half in range(2):
            for o in range(1, N):
                await_bytes(part.at[0], r1_recv.at[it, half, o - 1])
            row = part[block_of(half, 0)] + rs1[it, half, 0] + rs1[it, half, 1] + rs1[it, half, 2]
            for p in range(N):
                mid[half, p, pl.ds(0, HALF)] = row[p * HALF : (p + 1) * HALF]
                mid[half, p, pl.ds(HALF, 8)] = row[BLOCK:]
            for o in (2, 1, 3):
                remote(
                    mid.at[half, ahead(slot[half], o)], rs2.at[it, half, o - 1], r2_send.at[it, half, o - 1], r2_recv.at[it, half, o - 1], across(half, o)
                ).start()
        for half in range(2):
            for o in range(1, N):
                await_bytes(mid.at[0, 0], r2_recv.at[it, half, o - 1])
            sums = mid[half, slot[half]] + rs2[it, half, 0] + rs2[it, half, 1] + rs2[it, half, 2]
            flip[half] = jnp.broadcast_to(sums[HALF : HALF + 1, :128], (128, 128)).T
            count = flip[half, pl.ds(pl.multiple_of(slot[half] * HALF, HALF), HALF)]
            old = cod[it, block_of(half, 0), slot[half]]
            use(half, (sums[:HALF] + PRIOR_WEIGHT * old) / (jnp.tile(count, (1, 2)) + PRIOR_WEIGHT), count)

    def sent(it):
        for half in range(2):
            for o in range(1, N):
                await_bytes(part.at[0], r1_send.at[it, half, o - 1])
                await_bytes(mid.at[0, 0], r2_send.at[it, half, o - 1])

    def next_codes(half, codes, _):
        cod[1, block_of(half, 0), slot[half]] = codes
        start_stage1(1, half, cod.at[1, block_of(half, 0), slot[half]])

    moments(0)
    reduce_sums(0, next_codes)
    for half in range(2):
        await_stage1(1, half)
        start_stage2(1, half, (1, 3))

    def score_pair(o):
        blocks = [block_of(half, o) for half in range(2)]
        codes = jnp.concatenate([cod[1, b].reshape(BLOCK, D) for b in blocks], axis=0)
        high, low, norms = parts_of(codes)
        for g in range(TILES):
            tile_scores = score(high, low, norms, g)
            for half in range(2):
                scores[blocks[half], g] = tile_scores[half * BLOCK : (half + 1) * BLOCK]
            tops[g] = jnp.max(tile_scores, axis=0, keepdims=True)

    def sum_pair(o, g):
        blocks = [block_of(half, o) for half in range(2)]
        return add_up(g, [scores[b, g] for b in blocks], (top[g], total[g]))

    top[...] = jnp.full_like(top, -1e30)
    total[...] = jnp.zeros_like(total)
    score_pair(0)
    for half in range(2):
        start_stage2(1, half, (2,))

    def pair_step(i, _):
        o, previous = gray(i), gray(i - 1)
        for half in range(2):
            await_block(1, half, o)
        for g in range(TILES):
            top[g], total[g] = sum_pair(previous, g)
        score_pair(o)
        return 0

    lax.fori_loop(1, N, pair_step, 0)

    def last_sum(batch, _):
        for q in range(BATCH):
            g = batch * BATCH + q
            publish(1, g, *sum_pair(N // 2, g))
        send_stats(1, batch)
        return 0

    lax.fori_loop(0, BATCHES, last_sum, 0)
    sent(0)
    moments(1)

    def last_codes(half, codes, count):
        fin[z, pl.ds(half * HALF, HALF)] = codes
        flip[2, pl.ds(half * HALF, HALF)] = count

    flip[2] = jnp.zeros((128, 128), F32)
    reduce_sums(1, last_codes)
    fin[z, pl.ds(2 * HALF, 8)] = jnp.tile(flip[2].T[:8], (1, 2))
    for o in (2, 1, 3):
        remote(fin.at[z], fin.at[z], f_send.at[o - 1], f_recv.at[o - 1], at(ahead(z, o), x, y, core)).start()
    sent(1)

    for p in range(PIECES):
        for i in range(2):
            await_bytes(tok.at[0, rows_of(p)], tok_send.at[p, i])
            await_bytes(tok.at[0, rows_of(p, 0, 2)], tok_send.at[p, 2 + i])
    for i in range(4):
        await_bytes(tok.at[0], share_send.at[i])
    for it in range(ITERS):
        for batch in range(BATCHES):
            await_bytes(stats.at[it, batch, pl.ds(0, GROUP - 1)], st_send.at[it, batch])
        for half in range(2):
            for o in range(1, N):
                await_bytes(cod.at[it, 0, 0], c1_send.at[it, half, o - 1])
                await_bytes(cod.at[it, 0], c2_send.at[it, half, o - 1])
    for o in range(1, N):
        await_bytes(fin.at[0], f_send.at[o - 1])
        await_bytes(fin.at[0], f_recv.at[o - 1])
    for p in range(N):
        cent_out[pl.ds(p * 2 * HALF, 2 * HALF)] = fin[p, pl.ds(0, 2 * HALF)]
        count_out[:, pl.ds(p * 2 * HALF, 2 * HALF)] = fin[p, pl.ds(2 * HALF, 1), pl.ds(0, 2 * HALF)]


def on_device(tokens, codebook):
    vmem, dma = pltpu.VMEM, pltpu.SemaphoreType.DMA
    peers = N - 1
    centroids, counts = pl.pallas_call(
        em_kernel,
        out_shape=[jax.ShapeDtypeStruct((OWNED, D), F32), jax.ShapeDtypeStruct((1, OWNED), F32)],
        in_specs=[pl.BlockSpec(memory_space=pl.ANY)] * 2,
        out_specs=[pl.BlockSpec(memory_space=vmem)] * 2,
        scratch_shapes=[
            vmem((TILES, TILE, D), F32),
            vmem((TILES, TILE, D), BF16),
            vmem((TILES, TILE, D), BF16),
            vmem((TILES, 1, TILE), F32),
            vmem((ITERS, BLOCKS, N, HALF, D), F32),
            vmem((BLOCKS, BLOCK, D), BF16),
            vmem((BLOCKS, BLOCK, D), BF16),
            vmem((BLOCKS, BLOCK, 128), F32),
            vmem((BLOCKS, TILES, BLOCK, TILE), F32),
            vmem((TILES, 1, TILE), F32),
            vmem((TILES, 1, TILE), F32),
            vmem((TILES, 1, TILE), F32),
            vmem((TILES, 1, TILE), F32),
            vmem((ITERS, BATCHES, GROUP, BATCH, 1, TILE), F32),
            vmem((BLOCKS, SUMS, D), F32),
            vmem((ITERS, 2, peers, SUMS, D), F32),
            vmem((2, N, HALF + 8, D), F32),
            vmem((ITERS, 2, peers, HALF + 8, D), F32),
            vmem((N, 2 * HALF + 8, D), F32),
            vmem((3, 128, 128), F32),
            dma((3,)),
            dma((PIECES, 4)),
            dma((PIECES, 4)),
            dma((4,)),
            dma((4,)),
            dma((ITERS, 2, peers)),
            dma((ITERS, 2, peers)),
            dma((ITERS, 2, peers)),
            dma((ITERS, 2, peers)),
            dma((ITERS, BATCHES)),
            dma((ITERS, BATCHES)),
            dma((ITERS, 2, peers)),
            dma((ITERS, 2, peers)),
            dma((ITERS, 2, peers)),
            dma((ITERS, 2, peers)),
            dma((peers,)),
            dma((peers,)),
        ],
        compiler_params=pltpu.CompilerParams(collective_id=0, has_side_effects=True, vmem_limit_bytes=56 << 20),
        cost_estimate=pl.CostEstimate(
            flops=ITERS * 2 * 3 * 2 * TILES * TILE * BLOCKS * BLOCK * D,
            bytes_accessed=4 * (FRAMES + 2 * OWNED) * D,
            transcendentals=ITERS * 2 * TILES * TILE * BLOCKS * BLOCK,
        ),
    )(tokens, codebook.reshape(N, 2, HALF, D))
    return centroids, counts.reshape(OWNED)


def solution(mesh):
    return jax.shard_map(
        on_device,
        mesh=mesh,
        in_specs=(P(("tok", "code"), None), P("code", None)),
        out_specs=(P("code", None), P("code")),
        check_vma=False,
    )
```

```python
import functools
import math

import jax
import jax.numpy as jnp
from jax import lax
from jax.experimental import pallas as pl
from jax.experimental.pallas import tpu as pltpu
from jax.sharding import PartitionSpec as P

MESH = pl.DeviceIdType.MESH
F32, BF16 = jnp.float32, jnp.bfloat16
ITERS = 2
PRIOR_WEIGHT = 1.0
N = 4
CORES = 2
GROUP = N * CORES
D = 256
FRAMES = 512
OWNED = 256
HALF = OWNED // N // 2
BLOCK = N * HALF
BLOCKS = 2 * N
TILES = GROUP
TILE = FRAMES
PIECES = 4
ROWS = FRAMES // PIECES
BATCH = 4
BATCHES = TILES // BATCH
SUMS = BLOCK + 8
SHARPNESS = math.log2(math.e) / math.sqrt(D)
LAST = (((1,), (1,)), ((), ()))


def split(value):
    high = value.astype(BF16)
    return high, (value - high.astype(F32)).astype(BF16)


def em_kernel(
    frames, codebook, cent_out, count_out,
    tok, thi, tlo, tnorm, cod, chi, clo, cnorm, scores, tops, top, total, lognorm, stats, part, rs1, whole, line, mid, rs2, fin, flip,
    own_sem, tok_send, tok_recv, share_send, share_recv, c1_send, c1_recv, c2_send, c2_recv, st_send, st_recv,
    r1_send, r1_recv, r2_send, r2_recv, f_send, f_recv,
):
    z = lax.axis_index("tok")
    place = lax.axis_index("code")
    core = lax.rem(place, CORES)
    y = lax.rem(place // CORES, N)
    x = place // (CORES * N)
    mine = core * N + z

    def at(pz, px, py, pc):
        return (pz, (px * N + py) * CORES + pc)

    def ahead(p, o):
        return lax.rem(p + o, N)

    def remote(src, dst, send_sem, recv_sem, device):
        return pltpu.make_async_remote_copy(
            src_ref=src, dst_ref=dst, send_sem=send_sem, recv_sem=recv_sem, device_id=device, device_id_type=MESH
        )

    def await_bytes(ref, sem):
        pltpu.make_async_copy(ref, ref, sem).wait()

    def group_peer(j):
        peer = lax.rem(mine + j, GROUP)
        return at(lax.rem(peer, N), x, y, peer // N)

    barrier = pltpu.get_barrier_semaphore()
    peers = [at(z, ahead(x, o), y, core) for o in range(1, N)]
    peers += [at(z, x, ahead(y, o), core) for o in range(1, N)]
    peers += [group_peer(j) for j in range(1, GROUP)]
    for peer in peers:
        pl.semaphore_signal(barrier, inc=1, device_id=peer, device_id_type=MESH)
    pl.semaphore_wait(barrier, len(peers))

    def block_of(half, o):
        return ahead(y, o) if half == 0 else N + ahead(x, o)

    def across(half, o):
        return at(z, ahead(x, o), y, core) if half == 0 else at(z, x, ahead(y, o), core)

    def along(half, o):
        return at(z, x, ahead(y, o), core) if half == 0 else at(z, ahead(x, o), y, core)

    slot = (x, y)

    def start_stage1(half, src):
        dst = cod.at[0, block_of(half, 0), slot[half]]
        for o in (2, 1, 3):
            remote(src, dst, c1_send.at[half, o - 1], c1_recv.at[half, o - 1], across(half, o)).start()

    def await_stage1(half):
        for o in range(1, N):
            await_bytes(cod.at[0, 0, 0], c1_recv.at[half, o - 1])

    def start_stage2(it, half, places):
        block = cod.at[it, block_of(half, 0)]
        for o in places:
            remote(block, block, c2_send.at[it, half, o - 1], c2_recv.at[it, half, o - 1], along(half, o)).start()

    def await_block(it, half, o):
        await_bytes(cod.at[it, 0], c2_recv.at[it, half, N - 1 - o])

    before, after, opposite = ahead(z, N - 1), ahead(z, 1), ahead(z, 2)
    first, other = core * N, (1 - core) * N
    next_device, last_device = at(after, x, y, core), at(before, x, y, core)

    def rows_of(p, part=0, parts=1):
        return pl.ds(p * ROWS + part * (ROWS // parts), ROWS // parts)

    def direct(p):
        src, dst = frames.at[rows_of(p)], tok.at[first + z, rows_of(p)]
        remote(src, dst, tok_send.at[p, 0], tok_recv.at[p, 0], next_device).start()
        remote(src, dst, tok_send.at[p, 1], tok_recv.at[p, 1], last_device).start()

    def forward(p):
        await_bytes(tok.at[0, rows_of(p)], tok_recv.at[p, 0])
        low = tok.at[first + before, rows_of(p, 0, 2)]
        remote(low, low, tok_send.at[p, 2], tok_recv.at[p, 2], next_device).start()
        await_bytes(tok.at[0, rows_of(p)], tok_recv.at[p, 1])
        high = tok.at[first + after, rows_of(p, 1, 2)]
        remote(high, high, tok_send.at[p, 3], tok_recv.at[p, 3], last_device).start()

    def await_forwarded():
        for p in range(PIECES):
            await_bytes(tok.at[0, rows_of(p, 0, 2)], tok_recv.at[p, 2])
            await_bytes(tok.at[0, rows_of(p, 1, 2)], tok_recv.at[p, 3])

    def share(i, src, place):
        remote(src, tok.at[first + place], share_send.at[i], share_recv.at[i], at(z, x, y, 1 - core)).start()

    def await_shared(i):
        await_bytes(tok.at[0], share_recv.at[i])

    own_codes = [codebook.at[z, half] for half in range(2)]
    keep = [
        pltpu.make_async_copy(own_codes[0], cod.at[0, y, x], own_sem.at[0]),
        pltpu.make_async_copy(own_codes[1], cod.at[0, N + x, y], own_sem.at[1]),
        pltpu.make_async_copy(frames, tok.at[first + z], own_sem.at[2]),
    ]
    for half in range(2):
        start_stage1(half, own_codes[half])
    for copy in keep:
        copy.start()
    for p in range(PIECES):
        direct(p)
    share(0, frames, z)
    for copy in keep:
        copy.wait()
    for half in range(2):
        await_stage1(half)
        start_stage2(0, half, (1, 3, 2))
    forward(0)
    forward(1)
    for half in range(2):
        for o in range(1, N):
            await_block(0, half, o)

    def parts_of(codes):
        norms = jnp.sum(codes * codes, axis=1, keepdims=True) * SHARPNESS
        return *split(codes * (2.0 * SHARPNESS)), jnp.broadcast_to(norms, (codes.shape[0], 128))

    def split_block(b, _):
        chi[b], clo[b], cnorm[b] = parts_of(cod[0, b].reshape(BLOCK, D))
        return 0

    lax.fori_loop(0, BLOCKS, split_block, 0)

    def score(high, low, norms, g):
        inner = lax.dot_general(
            jnp.concatenate([high, high, low], axis=1),
            jnp.concatenate([thi[g], tlo[g], thi[g]], axis=1),
            LAST,
            preferred_element_type=F32,
        )
        return inner - jnp.tile(norms, (1, TILE // 128))

    def add_up(g, tiles, carry):
        old_top, old_total = carry if carry is not None else (None, None)
        new_top = tops[g] if carry is None else jnp.maximum(old_top, tops[g])
        new_total = None if carry is None else old_total * jnp.exp2(old_top - new_top)
        for tile in tiles:
            more = jnp.sum(jnp.exp2(tile - new_top), axis=0, keepdims=True)
            new_total = more if new_total is None else new_total + more
        return new_top, new_total

    def publish(it, g, row_top, row_total):
        norm = tnorm[g]
        shift = (row_top - norm) + norm
        stats[it, g // BATCH, mine, g % BATCH] = shift + jnp.log2(row_total * jnp.exp2(row_top - shift))

    def send_stats(it, batch):
        own = stats.at[it, batch, mine]
        for j in range(1, GROUP):
            remote(own, own, st_send.at[it, batch], st_recv.at[it, batch], group_peer(j)).start()

    def normalise(it, batch):
        await_bytes(stats.at[it, batch, pl.ds(0, GROUP - 1)], st_recv.at[it, batch])
        for q in range(BATCH):
            g = batch * BATCH + q
            logs = stats[it, batch, :, q, 0, :]
            highest = jnp.max(logs, axis=0, keepdims=True)
            lognorm[g] = highest + jnp.log2(jnp.sum(jnp.exp2(logs - highest), axis=0, keepdims=True))

    def score_tile(g):
        tile = tok[g]
        thi[g], tlo[g] = split(tile)
        squares = tile * tile
        squares = squares[:, :128] + squares[:, 128:]
        tnorm[g] = jnp.sum(squares.T, axis=0, keepdims=True) * SHARPNESS
        high, low = chi[...].reshape(BLOCKS * BLOCK, D), clo[...].reshape(BLOCKS * BLOCK, D)
        tile_scores = score(high, low, cnorm[...].reshape(BLOCKS * BLOCK, 128), g)
        scores[:, g] = tile_scores.reshape(BLOCKS, BLOCK, TILE)
        tops[g] = jnp.max(tile_scores, axis=0, keepdims=True)

    def sum_tile(g):
        publish(0, g, *add_up(g, [scores[:, g].reshape(BLOCKS * BLOCK, TILE)], None))

    def source(i):
        place = jnp.where(i < 2, z, jnp.where(i < 6, jnp.where(i % 2 == 0, before, after), opposite))
        ours = (i == 0) | (i == 2) | (i == 3)
        return jnp.where(i < 6, jnp.where(ours, core, 1 - core), i - 6) * N + place

    def move_on(i):
        @pl.when(i == 1)
        def _():
            forward(2)
            await_shared(0)

        @pl.when(i == 2)
        def _():
            forward(3)
            share(1, tok.at[first + before], before)
            share(2, tok.at[first + after], after)

        @pl.when(i == 4)
        def _():
            await_shared(1)

        @pl.when(i == 5)
        def _():
            await_shared(2)

        @pl.when(i == 6)
        def _():
            await_forwarded()
            share(3, tok.at[first + opposite], opposite)
            await_shared(3)

    score_tile(source(0))

    def step(i, _):
        move_on(i)
        sum_tile(source(i - 1))
        score_tile(source(i))

        @pl.when(i == TILES - 1)
        def _():
            send_stats(0, 0)

        return 0

    lax.fori_loop(1, TILES, step, 0)
    sum_tile(source(TILES - 1))
    send_stats(0, 1)

    def gray(i):
        return jnp.bitwise_xor(i, i // 2)

    def weigh(blocks, tiles):
        lefts, rights, counts = [], [], None
        for g in tiles:
            pair_scores = jnp.concatenate([scores[b, g] for b in blocks], axis=0)
            weights = jnp.exp2(pair_scores - lognorm[g])
            for c in range(TILE // 128):
                piece = weights[:, c * 128 : (c + 1) * 128]
                counts = piece if counts is None else counts + piece
            high, low = split(weights)
            lefts += [high, high, low]
            rights += [thi[g], tlo[g], thi[g]]
        weighted = jnp.dot(jnp.concatenate(lefts, axis=1), jnp.concatenate(rights, axis=0), preferred_element_type=F32)
        for half in range(2):
            part[blocks[half], pl.ds(0, BLOCK)] += weighted[half * BLOCK : (half + 1) * BLOCK]
            row = jnp.sum(counts[half * BLOCK : (half + 1) * BLOCK].T, axis=0, keepdims=True)
            part[blocks[half], pl.ds(BLOCK, 8)] += jnp.broadcast_to(jnp.tile(row, (1, 2)), (8, D))

    def moments(it):
        batches = BATCHES if it == 0 else 1
        part[...] = jnp.zeros_like(part)
        normalise(it, 0)
        if batches == 1:
            normalise(it, 1)

        def step(i, _):
            o, batch = gray(N - 1 - i // batches), i % batches

            if batches > 1:

                @pl.when(i == 1)
                def _():
                    normalise(it, 1)

            blocks = [block_of(half, o) for half in range(2)]
            size = TILES // batches
            weigh(blocks, [batch * size + q for q in range(size)])

            @pl.when((batch == batches - 1) & (o != 0))
            def _():
                for half in range(2):
                    remote(
                        part.at[blocks[half]], rs1.at[it, half, o - 1], r1_send.at[it, half, o - 1], r1_recv.at[it, half, o - 1], along(half, o)
                    ).start()

            return 0

        lax.fori_loop(0, N * batches, step, 0)

    def reduce_sums(use):
        for half in range(2):
            for o in range(1, N):
                await_bytes(part.at[0], r1_recv.at[1, half, o - 1])
            row = part[block_of(half, 0)] + rs1[1, half, 0] + rs1[1, half, 1] + rs1[1, half, 2]
            for p in range(N):
                mid[half, p, pl.ds(0, HALF)] = row[p * HALF : (p + 1) * HALF]
                mid[half, p, pl.ds(HALF, 8)] = row[BLOCK:]
            for o in (2, 1, 3):
                remote(
                    mid.at[half, ahead(slot[half], o)], rs2.at[half, o - 1], r2_send.at[1, half, o - 1], r2_recv.at[1, half, o - 1], across(half, o)
                ).start()
        for half in range(2):
            for o in range(1, N):
                await_bytes(mid.at[0, 0], r2_recv.at[1, half, o - 1])
            sums = mid[half, slot[half]] + rs2[half, 0] + rs2[half, 1] + rs2[half, 2]
            flip[half] = jnp.broadcast_to(sums[HALF : HALF + 1, :128], (128, 128)).T
            count = flip[half, pl.ds(pl.multiple_of(slot[half] * HALF, HALF), HALF)]
            old = cod[1, block_of(half, 0), slot[half]]
            use(half, (sums[:HALF] + PRIOR_WEIGHT * old) / (jnp.tile(count, (1, 2)) + PRIOR_WEIGHT), count)

    def sums_sent():
        for half in range(2):
            for o in range(1, N):
                await_bytes(part.at[0], r1_send.at[0, half, o - 1])
                await_bytes(whole.at[0], r2_send.at[0, half, o - 1])

    moments(0)

    for half in range(2):
        for o in range(1, N):
            await_bytes(part.at[0], r1_recv.at[0, half, o - 1])
        whole[half] = part[block_of(half, 0)] + rs1[0, half, 0] + rs1[0, half, 1] + rs1[0, half, 2]
        for o in (2, 1, 3):
            remote(
                whole.at[half], line.at[half, o - 1], r2_send.at[0, half, o - 1], r2_recv.at[0, half, o - 1], across(half, o)
            ).start()
    for half in range(2):
        for o in range(1, N):
            await_bytes(whole.at[0], r2_recv.at[0, half, o - 1])
        sums = whole[half] + line[half, 0] + line[half, 1] + line[half, 2]
        count = jnp.tile(jnp.broadcast_to(sums[BLOCK : BLOCK + 1, :128], (128, 128)).T, (1, 2))
        block = block_of(half, 0)
        new = (sums[:BLOCK] + PRIOR_WEIGHT * cod[0, block].reshape(BLOCK, D)) / (count + PRIOR_WEIGHT)
        cod[1, block] = new.reshape(N, HALF, D)
        start_stage2(1, half, (1, 3, 2))

    def score_pair(o):
        blocks = [block_of(half, o) for half in range(2)]
        codes = jnp.concatenate([cod[1, b].reshape(BLOCK, D) for b in blocks], axis=0)
        high, low, norms = parts_of(codes)
        for g in range(TILES):
            tile_scores = score(high, low, norms, g)
            for half in range(2):
                scores[blocks[half], g] = tile_scores[half * BLOCK : (half + 1) * BLOCK]
            tops[g] = jnp.max(tile_scores, axis=0, keepdims=True)

    def sum_pair(o, g):
        blocks = [block_of(half, o) for half in range(2)]
        return add_up(g, [scores[b, g] for b in blocks], (top[g], total[g]))

    top[...] = jnp.full_like(top, -1e30)
    total[...] = jnp.zeros_like(total)
    score_pair(0)

    def pair_step(i, _):
        o, previous = gray(i), gray(i - 1)
        for half in range(2):
            await_block(1, half, o)
        for g in range(TILES):
            top[g], total[g] = sum_pair(previous, g)
        score_pair(o)
        return 0

    lax.fori_loop(1, N, pair_step, 0)

    def last_sum(batch, _):
        for q in range(BATCH):
            g = batch * BATCH + q
            publish(1, g, *sum_pair(N // 2, g))
        send_stats(1, batch)
        return 0

    lax.fori_loop(0, BATCHES, last_sum, 0)
    sums_sent()
    moments(1)

    def last_codes(half, codes, count):
        fin[z, pl.ds(half * HALF, HALF)] = codes
        flip[2, pl.ds(half * HALF, HALF)] = count

    flip[2] = jnp.zeros((128, 128), F32)
    reduce_sums(last_codes)
    fin[z, pl.ds(2 * HALF, 8)] = jnp.tile(flip[2].T[:8], (1, 2))
    for o in (2, 1, 3):
        remote(fin.at[z], fin.at[z], f_send.at[o - 1], f_recv.at[o - 1], at(ahead(z, o), x, y, core)).start()
    for half in range(2):
        for o in range(1, N):
            await_bytes(part.at[0], r1_send.at[1, half, o - 1])
            await_bytes(mid.at[0, 0], r2_send.at[1, half, o - 1])

    for p in range(PIECES):
        for i in range(2):
            await_bytes(tok.at[0, rows_of(p)], tok_send.at[p, i])
            await_bytes(tok.at[0, rows_of(p, 0, 2)], tok_send.at[p, 2 + i])
    for i in range(4):
        await_bytes(tok.at[0], share_send.at[i])
    for it in range(ITERS):
        for batch in range(BATCHES):
            await_bytes(stats.at[it, batch, pl.ds(0, GROUP - 1)], st_send.at[it, batch])
        for half in range(2):
            for o in range(1, N):
                if it == 0:
                    await_bytes(cod.at[0, 0, 0], c1_send.at[half, o - 1])
                await_bytes(cod.at[it, 0], c2_send.at[it, half, o - 1])
    for o in range(1, N):
        await_bytes(fin.at[0], f_send.at[o - 1])
        await_bytes(fin.at[0], f_recv.at[o - 1])
    for p in range(N):
        cent_out[pl.ds(p * 2 * HALF, 2 * HALF)] = fin[p, pl.ds(0, 2 * HALF)]
        count_out[:, pl.ds(p * 2 * HALF, 2 * HALF)] = fin[p, pl.ds(2 * HALF, 1), pl.ds(0, 2 * HALF)]


def hand_on(cent, count, cent_out, count_out):
    cent_out[...] = cent[...]
    count_out[...] = count[...]


def on_device(tokens, codebook):
    vmem, dma = pltpu.VMEM, pltpu.SemaphoreType.DMA
    peers = N - 1
    results = [jax.ShapeDtypeStruct((OWNED, D), F32), jax.ShapeDtypeStruct((1, OWNED), F32)]
    centroids, counts = pl.pallas_call(
        em_kernel,
        out_shape=results,
        in_specs=[pl.BlockSpec(memory_space=pl.ANY)] * 2,
        out_specs=[pl.BlockSpec(memory_space=vmem)] * 2,
        scratch_shapes=[
            vmem((TILES, TILE, D), F32),
            vmem((TILES, TILE, D), BF16),
            vmem((TILES, TILE, D), BF16),
            vmem((TILES, 1, TILE), F32),
            vmem((ITERS, BLOCKS, N, HALF, D), F32),
            vmem((BLOCKS, BLOCK, D), BF16),
            vmem((BLOCKS, BLOCK, D), BF16),
            vmem((BLOCKS, BLOCK, 128), F32),
            vmem((BLOCKS, TILES, BLOCK, TILE), F32),
            vmem((TILES, 1, TILE), F32),
            vmem((TILES, 1, TILE), F32),
            vmem((TILES, 1, TILE), F32),
            vmem((TILES, 1, TILE), F32),
            vmem((ITERS, BATCHES, GROUP, BATCH, 1, TILE), F32),
            vmem((BLOCKS, SUMS, D), F32),
            vmem((ITERS, 2, peers, SUMS, D), F32),
            vmem((2, SUMS, D), F32),
            vmem((2, peers, SUMS, D), F32),
            vmem((2, N, HALF + 8, D), F32),
            vmem((2, peers, HALF + 8, D), F32),
            vmem((N, 2 * HALF + 8, D), F32),
            vmem((3, 128, 128), F32),
            dma((3,)),
            dma((PIECES, 4)),
            dma((PIECES, 4)),
            dma((4,)),
            dma((4,)),
            dma((2, peers)),
            dma((2, peers)),
            dma((ITERS, 2, peers)),
            dma((ITERS, 2, peers)),
            dma((ITERS, BATCHES)),
            dma((ITERS, BATCHES)),
            dma((ITERS, 2, peers)),
            dma((ITERS, 2, peers)),
            dma((ITERS, 2, peers)),
            dma((ITERS, 2, peers)),
            dma((peers,)),
            dma((peers,)),
        ],
        compiler_params=pltpu.CompilerParams(collective_id=0, has_side_effects=True, vmem_limit_bytes=56 << 20),
        cost_estimate=pl.CostEstimate(
            flops=ITERS * 2 * 3 * 2 * TILES * TILE * BLOCKS * BLOCK * D,
            bytes_accessed=4 * (FRAMES + 2 * OWNED) * D,
            transcendentals=ITERS * 2 * TILES * TILE * BLOCKS * BLOCK,
        ),
    )(tokens, codebook.reshape(N, 2, HALF, D))
    centroids, counts = pl.pallas_call(
        hand_on,
        out_shape=results,
        in_specs=[pl.BlockSpec(memory_space=vmem)] * 2,
        out_specs=[pl.BlockSpec(memory_space=vmem)] * 2,
    )(centroids, counts)
    return centroids, counts.reshape(OWNED)


def solution(mesh):
    return jax.shard_map(
        on_device,
        mesh=mesh,
        in_specs=(P(("tok", "code"), None), P("code", None)),
        out_specs=(P("code", None), P("code")),
        check_vma=False,
    )
```

```python
import functools
import math

import jax
import jax.numpy as jnp
from jax import lax
from jax.experimental import pallas as pl
from jax.experimental.pallas import tpu as pltpu
from jax.sharding import PartitionSpec as P

MESH = pl.DeviceIdType.MESH
F32, BF16 = jnp.float32, jnp.bfloat16
ITERS = 2
PRIOR_WEIGHT = 1.0
N = 4
CORES = 2
GROUP = N * CORES
D = 256
FRAMES = 512
OWNED = 256
HALF = OWNED // N // 2
BLOCK = N * HALF
BLOCKS = 2 * N
TILES = GROUP
TILE = FRAMES
PIECES = 4
ROWS = FRAMES // PIECES
BATCH = 4
BATCHES = TILES // BATCH
SUMS = BLOCK + 8
SHARPNESS = math.log2(math.e) / math.sqrt(D)
LAST = (((1,), (1,)), ((), ()))


def split(value):
    high = value.astype(BF16)
    return high, (value - high.astype(F32)).astype(BF16)


def em_kernel(
    frames, codebook, cent_out, count_out,
    tok, thi, tlo, tnorm, cod, chi, clo, cnorm, scores, tops, top, total, lognorm, stats, part, rs1, mid, rs2, fin, flip,
    own_sem, tok_send, tok_recv, share_send, share_recv, c1_send, c1_recv, c2_send, c2_recv, st_send, st_recv,
    r1_send, r1_recv, r2_send, r2_recv, f_send, f_recv,
):
    z = lax.axis_index("tok")
    place = lax.axis_index("code")
    core = lax.rem(place, CORES)
    y = lax.rem(place // CORES, N)
    x = place // (CORES * N)
    mine = core * N + z

    def at(pz, px, py, pc):
        return (pz, (px * N + py) * CORES + pc)

    def ahead(p, o):
        return lax.rem(p + o, N)

    def remote(src, dst, send_sem, recv_sem, device):
        return pltpu.make_async_remote_copy(
            src_ref=src, dst_ref=dst, send_sem=send_sem, recv_sem=recv_sem, device_id=device, device_id_type=MESH
        )

    def await_bytes(ref, sem):
        pltpu.make_async_copy(ref, ref, sem).wait()

    def group_peer(j):
        peer = lax.rem(mine + j, GROUP)
        return at(lax.rem(peer, N), x, y, peer // N)

    barrier = pltpu.get_barrier_semaphore()
    peers = [at(z, ahead(x, o), y, core) for o in range(1, N)]
    peers += [at(z, x, ahead(y, o), core) for o in range(1, N)]
    peers += [group_peer(j) for j in range(1, GROUP)]
    for peer in peers:
        pl.semaphore_signal(barrier, inc=1, device_id=peer, device_id_type=MESH)
    pl.semaphore_wait(barrier, len(peers))

    def block_of(half, o):
        return ahead(y, o) if half == 0 else N + ahead(x, o)

    def across(half, o):
        return at(z, ahead(x, o), y, core) if half == 0 else at(z, x, ahead(y, o), core)

    def along(half, o):
        return at(z, x, ahead(y, o), core) if half == 0 else at(z, ahead(x, o), y, core)

    slot = (x, y)

    def start_stage1(it, half, src):
        dst = cod.at[it, block_of(half, 0), slot[half]]
        for o in (2, 1, 3):
            remote(src, dst, c1_send.at[it, half, o - 1], c1_recv.at[it, half, o - 1], across(half, o)).start()

    def await_stage1(it, half):
        for o in range(1, N):
            await_bytes(cod.at[it, 0, 0], c1_recv.at[it, half, o - 1])

    def start_stage2(it, half, places):
        block = cod.at[it, block_of(half, 0)]
        for o in places:
            remote(block, block, c2_send.at[it, half, o - 1], c2_recv.at[it, half, o - 1], along(half, o)).start()

    def await_block(it, half, o):
        await_bytes(cod.at[it, 0], c2_recv.at[it, half, N - 1 - o])

    before, after, opposite = ahead(z, N - 1), ahead(z, 1), ahead(z, 2)
    first, other = core * N, (1 - core) * N
    next_device, last_device = at(after, x, y, core), at(before, x, y, core)

    def rows_of(p, part=0, parts=1):
        return pl.ds(p * ROWS + part * (ROWS // parts), ROWS // parts)

    def direct(p):
        src, dst = frames.at[rows_of(p)], tok.at[first + z, rows_of(p)]
        remote(src, dst, tok_send.at[p, 0], tok_recv.at[p, 0], next_device).start()
        remote(src, dst, tok_send.at[p, 1], tok_recv.at[p, 1], last_device).start()

    def forward(p):
        await_bytes(tok.at[0, rows_of(p)], tok_recv.at[p, 0])
        low = tok.at[first + before, rows_of(p, 0, 2)]
        remote(low, low, tok_send.at[p, 2], tok_recv.at[p, 2], next_device).start()
        await_bytes(tok.at[0, rows_of(p)], tok_recv.at[p, 1])
        high = tok.at[first + after, rows_of(p, 1, 2)]
        remote(high, high, tok_send.at[p, 3], tok_recv.at[p, 3], last_device).start()

    def await_forwarded():
        for p in range(PIECES):
            await_bytes(tok.at[0, rows_of(p, 0, 2)], tok_recv.at[p, 2])
            await_bytes(tok.at[0, rows_of(p, 1, 2)], tok_recv.at[p, 3])

    def share(i, src, place):
        remote(src, tok.at[first + place], share_send.at[i], share_recv.at[i], at(z, x, y, 1 - core)).start()

    def await_shared(i):
        await_bytes(tok.at[0], share_recv.at[i])

    own_codes = [codebook.at[z, half] for half in range(2)]
    keep = [
        pltpu.make_async_copy(own_codes[0], cod.at[0, y, x], own_sem.at[0]),
        pltpu.make_async_copy(own_codes[1], cod.at[0, N + x, y], own_sem.at[1]),
        pltpu.make_async_copy(frames, tok.at[first + z], own_sem.at[2]),
    ]
    for half in range(2):
        start_stage1(0, half, own_codes[half])
    for copy in keep:
        copy.start()
    for p in range(PIECES):
        direct(p)
    share(0, frames, z)
    for copy in keep:
        copy.wait()
    for half in range(2):
        await_stage1(0, half)
        start_stage2(0, half, (1, 3, 2))
    forward(0)
    forward(1)
    for half in range(2):
        for o in range(1, N):
            await_block(0, half, o)

    def parts_of(codes):
        norms = jnp.sum(codes * codes, axis=1, keepdims=True) * SHARPNESS
        return *split(codes * (2.0 * SHARPNESS)), jnp.broadcast_to(norms, (codes.shape[0], 128))

    def split_block(b, _):
        chi[b], clo[b], cnorm[b] = parts_of(cod[0, b].reshape(BLOCK, D))
        return 0

    lax.fori_loop(0, BLOCKS, split_block, 0)

    def score(high, low, norms, g):
        inner = lax.dot_general(
            jnp.concatenate([high, high, low], axis=1),
            jnp.concatenate([thi[g], tlo[g], thi[g]], axis=1),
            LAST,
            preferred_element_type=F32,
        )
        return inner - jnp.tile(norms, (1, TILE // 128))

    def add_up(g, tiles, carry):
        old_top, old_total = carry if carry is not None else (None, None)
        new_top = tops[g] if carry is None else jnp.maximum(old_top, tops[g])
        new_total = None if carry is None else old_total * jnp.exp2(old_top - new_top)
        for tile in tiles:
            more = jnp.sum(jnp.exp2(tile - new_top), axis=0, keepdims=True)
            new_total = more if new_total is None else new_total + more
        return new_top, new_total

    def publish(it, g, row_top, row_total):
        norm = tnorm[g]
        shift = (row_top - norm) + norm
        stats[it, g // BATCH, mine, g % BATCH] = shift + jnp.log2(row_total * jnp.exp2(row_top - shift))

    def send_stats(it, batch):
        own = stats.at[it, batch, mine]
        for j in range(1, GROUP):
            remote(own, own, st_send.at[it, batch], st_recv.at[it, batch], group_peer(j)).start()

    def normalise(it, batch):
        await_bytes(stats.at[it, batch, pl.ds(0, GROUP - 1)], st_recv.at[it, batch])
        for q in range(BATCH):
            g = batch * BATCH + q
            logs = stats[it, batch, :, q, 0, :]
            highest = jnp.max(logs, axis=0, keepdims=True)
            lognorm[g] = highest + jnp.log2(jnp.sum(jnp.exp2(logs - highest), axis=0, keepdims=True))

    def score_tile(g):
        thi[g], tlo[g] = split(tok[g])
        high, low = chi[...].reshape(BLOCKS * BLOCK, D), clo[...].reshape(BLOCKS * BLOCK, D)
        tile_scores = score(high, low, cnorm[...].reshape(BLOCKS * BLOCK, 128), g)
        scores[:, g] = tile_scores.reshape(BLOCKS, BLOCK, TILE)
        tops[g] = jnp.max(tile_scores, axis=0, keepdims=True)

    def sum_tile(g):
        squares = tok[g] * tok[g]
        squares = squares[:, :128] + squares[:, 128:]
        tnorm[g] = jnp.sum(squares.T, axis=0, keepdims=True) * SHARPNESS
        publish(0, g, *add_up(g, [scores[:, g].reshape(BLOCKS * BLOCK, TILE)], None))

    def source(i):
        place = jnp.where(i < 2, z, jnp.where(i < 6, jnp.where(i % 2 == 0, before, after), opposite))
        ours = (i == 0) | (i == 2) | (i == 3)
        return jnp.where(i < 6, jnp.where(ours, core, 1 - core), i - 6) * N + place

    def move_on(i):
        @pl.when(i == 1)
        def _():
            forward(2)
            await_shared(0)

        @pl.when(i == 2)
        def _():
            forward(3)
            share(1, tok.at[first + before], before)
            share(2, tok.at[first + after], after)

        @pl.when(i == 4)
        def _():
            await_shared(1)

        @pl.when(i == 5)
        def _():
            await_shared(2)

        @pl.when(i == 6)
        def _():
            await_forwarded()
            share(3, tok.at[first + opposite], opposite)
            await_shared(3)

    score_tile(source(0))

    def step(i, _):
        move_on(i)
        sum_tile(source(i - 1))
        score_tile(source(i))

        @pl.when(i == TILES - 1)
        def _():
            send_stats(0, 0)

        return 0

    lax.fori_loop(1, TILES, step, 0)
    sum_tile(source(TILES - 1))
    send_stats(0, 1)

    def gray(i):
        return jnp.bitwise_xor(i, i // 2)

    def weigh(blocks, tiles):
        lefts, rights, counts = [], [], None
        for g in tiles:
            pair_scores = jnp.concatenate([scores[b, g] for b in blocks], axis=0)
            weights = jnp.exp2(pair_scores - lognorm[g])
            for c in range(TILE // 128):
                piece = weights[:, c * 128 : (c + 1) * 128]
                counts = piece if counts is None else counts + piece
            high, low = split(weights)
            lefts += [high, high, low]
            rights += [thi[g], tlo[g], thi[g]]
        weighted = jnp.dot(jnp.concatenate(lefts, axis=1), jnp.concatenate(rights, axis=0), preferred_element_type=F32)
        for half in range(2):
            part[blocks[half], pl.ds(0, BLOCK)] += weighted[half * BLOCK : (half + 1) * BLOCK]
            row = jnp.sum(counts[half * BLOCK : (half + 1) * BLOCK].T, axis=0, keepdims=True)
            part[blocks[half], pl.ds(BLOCK, 8)] += jnp.broadcast_to(jnp.tile(row, (1, 2)), (8, D))

    def moments(it):
        batches = BATCHES if it == 0 else 1
        part[...] = jnp.zeros_like(part)
        normalise(it, 0)
        if batches == 1:
            normalise(it, 1)

        def step(i, _):
            o, batch = gray(N - 1 - i // batches), i % batches

            if batches > 1:

                @pl.when(i == 1)
                def _():
                    normalise(it, 1)

            blocks = [block_of(half, o) for half in range(2)]
            size = TILES // batches
            weigh(blocks, [batch * size + q for q in range(size)])

            @pl.when((batch == batches - 1) & (o != 0))
            def _():
                for half in range(2):
                    remote(
                        part.at[blocks[half]], rs1.at[it, half, o - 1], r1_send.at[it, half, o - 1], r1_recv.at[it, half, o - 1], along(half, o)
                    ).start()

            return 0

        lax.fori_loop(0, N * batches, step, 0)

    def reduce_sums(it, use):
        for half in range(2):
            for o in range(1, N):
                await_bytes(part.at[0], r1_recv.at[it, half, o - 1])
            row = part[block_of(half, 0)] + rs1[it, half, 0] + rs1[it, half, 1] + rs1[it, half, 2]
            for p in range(N):
                mid[half, p, pl.ds(0, HALF)] = row[p * HALF : (p + 1) * HALF]
                mid[half, p, pl.ds(HALF, 8)] = row[BLOCK:]
            for o in (2, 1, 3):
                remote(
                    mid.at[half, ahead(slot[half], o)], rs2.at[it, half, o - 1], r2_send.at[it, half, o - 1], r2_recv.at[it, half, o - 1], across(half, o)
                ).start()
        for half in range(2):
            for o in range(1, N):
                await_bytes(mid.at[0, 0], r2_recv.at[it, half, o - 1])
            sums = mid[half, slot[half]] + rs2[it, half, 0] + rs2[it, half, 1] + rs2[it, half, 2]
            flip[half] = jnp.broadcast_to(sums[HALF : HALF + 1, :128], (128, 128)).T
            count = flip[half, pl.ds(pl.multiple_of(slot[half] * HALF, HALF), HALF)]
            old = cod[it, block_of(half, 0), slot[half]]
            use(half, (sums[:HALF] + PRIOR_WEIGHT * old) / (jnp.tile(count, (1, 2)) + PRIOR_WEIGHT), count)

    def sent(it):
        for half in range(2):
            for o in range(1, N):
                await_bytes(part.at[0], r1_send.at[it, half, o - 1])
                await_bytes(mid.at[0, 0], r2_send.at[it, half, o - 1])

    def next_codes(half, codes, _):
        cod[1, block_of(half, 0), slot[half]] = codes
        start_stage1(1, half, cod.at[1, block_of(half, 0), slot[half]])

    moments(0)
    reduce_sums(0, next_codes)
    for half in range(2):
        await_stage1(1, half)
        start_stage2(1, half, (1, 3))

    def score_pair(o):
        blocks = [block_of(half, o) for half in range(2)]
        codes = jnp.concatenate([cod[1, b].reshape(BLOCK, D) for b in blocks], axis=0)
        high, low, norms = parts_of(codes)
        for g in range(TILES):
            tile_scores = score(high, low, norms, g)
            for half in range(2):
                scores[blocks[half], g] = tile_scores[half * BLOCK : (half + 1) * BLOCK]
            tops[g] = jnp.max(tile_scores, axis=0, keepdims=True)

    def sum_pair(o, g):
        blocks = [block_of(half, o) for half in range(2)]
        return add_up(g, [scores[b, g] for b in blocks], (top[g], total[g]))

    top[...] = jnp.full_like(top, -1e30)
    total[...] = jnp.zeros_like(total)
    score_pair(0)
    for half in range(2):
        start_stage2(1, half, (2,))

    def pair_step(i, _):
        o, previous = gray(i), gray(i - 1)
        for half in range(2):
            await_block(1, half, o)
        for g in range(TILES):
            top[g], total[g] = sum_pair(previous, g)
        score_pair(o)
        return 0

    lax.fori_loop(1, N, pair_step, 0)

    def last_sum(batch, _):
        for q in range(BATCH):
            g = batch * BATCH + q
            publish(1, g, *sum_pair(N // 2, g))
        send_stats(1, batch)
        return 0

    lax.fori_loop(0, BATCHES, last_sum, 0)
    sent(0)
    moments(1)

    def last_codes(half, codes, count):
        fin[z, pl.ds(half * HALF, HALF)] = codes
        flip[2, pl.ds(half * HALF, HALF)] = count

    flip[2] = jnp.zeros((128, 128), F32)
    reduce_sums(1, last_codes)
    fin[z, pl.ds(2 * HALF, 8)] = jnp.tile(flip[2].T[:8], (1, 2))
    for o in (2, 1, 3):
        remote(fin.at[z], fin.at[z], f_send.at[o - 1], f_recv.at[o - 1], at(ahead(z, o), x, y, core)).start()
    sent(1)

    for p in range(PIECES):
        for i in range(2):
            await_bytes(tok.at[0, rows_of(p)], tok_send.at[p, i])
            await_bytes(tok.at[0, rows_of(p, 0, 2)], tok_send.at[p, 2 + i])
    for i in range(4):
        await_bytes(tok.at[0], share_send.at[i])
    for it in range(ITERS):
        for batch in range(BATCHES):
            await_bytes(stats.at[it, batch, pl.ds(0, GROUP - 1)], st_send.at[it, batch])
        for half in range(2):
            for o in range(1, N):
                await_bytes(cod.at[it, 0, 0], c1_send.at[it, half, o - 1])
                await_bytes(cod.at[it, 0], c2_send.at[it, half, o - 1])
    for o in range(1, N):
        await_bytes(fin.at[0], f_send.at[o - 1])
        await_bytes(fin.at[0], f_recv.at[o - 1])
    for p in range(N):
        cent_out[pl.ds(p * 2 * HALF, 2 * HALF)] = fin[p, pl.ds(0, 2 * HALF)]
        count_out[:, pl.ds(p * 2 * HALF, 2 * HALF)] = fin[p, pl.ds(2 * HALF, 1), pl.ds(0, 2 * HALF)]


def hand_on(cent, count, cent_out, count_out):
    cent_out[...] = cent[...]
    count_out[...] = count[...]


def on_device(tokens, codebook):
    vmem, dma = pltpu.VMEM, pltpu.SemaphoreType.DMA
    peers = N - 1
    results = [jax.ShapeDtypeStruct((OWNED, D), F32), jax.ShapeDtypeStruct((1, OWNED), F32)]
    centroids, counts = pl.pallas_call(
        em_kernel,
        out_shape=results,
        in_specs=[pl.BlockSpec(memory_space=pl.ANY)] * 2,
        out_specs=[pl.BlockSpec(memory_space=vmem)] * 2,
        scratch_shapes=[
            vmem((TILES, TILE, D), F32),
            vmem((TILES, TILE, D), BF16),
            vmem((TILES, TILE, D), BF16),
            vmem((TILES, 1, TILE), F32),
            vmem((ITERS, BLOCKS, N, HALF, D), F32),
            vmem((BLOCKS, BLOCK, D), BF16),
            vmem((BLOCKS, BLOCK, D), BF16),
            vmem((BLOCKS, BLOCK, 128), F32),
            vmem((BLOCKS, TILES, BLOCK, TILE), F32),
            vmem((TILES, 1, TILE), F32),
            vmem((TILES, 1, TILE), F32),
            vmem((TILES, 1, TILE), F32),
            vmem((TILES, 1, TILE), F32),
            vmem((ITERS, BATCHES, GROUP, BATCH, 1, TILE), F32),
            vmem((BLOCKS, SUMS, D), F32),
            vmem((ITERS, 2, peers, SUMS, D), F32),
            vmem((2, N, HALF + 8, D), F32),
            vmem((ITERS, 2, peers, HALF + 8, D), F32),
            vmem((N, 2 * HALF + 8, D), F32),
            vmem((3, 128, 128), F32),
            dma((3,)),
            dma((PIECES, 4)),
            dma((PIECES, 4)),
            dma((4,)),
            dma((4,)),
            dma((ITERS, 2, peers)),
            dma((ITERS, 2, peers)),
            dma((ITERS, 2, peers)),
            dma((ITERS, 2, peers)),
            dma((ITERS, BATCHES)),
            dma((ITERS, BATCHES)),
            dma((ITERS, 2, peers)),
            dma((ITERS, 2, peers)),
            dma((ITERS, 2, peers)),
            dma((ITERS, 2, peers)),
            dma((peers,)),
            dma((peers,)),
        ],
        compiler_params=pltpu.CompilerParams(collective_id=0, has_side_effects=True, vmem_limit_bytes=56 << 20),
        cost_estimate=pl.CostEstimate(
            flops=ITERS * 2 * 3 * 2 * TILES * TILE * BLOCKS * BLOCK * D,
            bytes_accessed=4 * (FRAMES + 2 * OWNED) * D,
            transcendentals=ITERS * 2 * TILES * TILE * BLOCKS * BLOCK,
        ),
    )(tokens, codebook.reshape(N, 2, HALF, D))
    centroids, counts = pl.pallas_call(
        hand_on,
        out_shape=results,
        in_specs=[pl.BlockSpec(memory_space=vmem)] * 2,
        out_specs=[pl.BlockSpec(memory_space=vmem)] * 2,
    )(centroids, counts)
    return centroids, counts.reshape(OWNED)


def solution(mesh):
    return jax.shard_map(
        on_device,
        mesh=mesh,
        in_specs=(P(("tok", "code"), None), P("code", None)),
        out_specs=(P("code", None), P("code")),
        check_vma=False,
    )
```

```python
import functools
import math

import jax
import jax.numpy as jnp
from jax import lax
from jax.experimental import pallas as pl
from jax.experimental.pallas import tpu as pltpu
from jax.sharding import PartitionSpec as P

MESH = pl.DeviceIdType.MESH
F32, BF16 = jnp.float32, jnp.bfloat16
ITERS = 2
PRIOR_WEIGHT = 1.0
N = 4
CORES = 2
GROUP = N * CORES
D = 256
FRAMES = 512
OWNED = 256
HALF = OWNED // N // 2
BLOCK = N * HALF
BLOCKS = 2 * N
TILES = GROUP
TILE = FRAMES
PIECES = 4
ROWS = FRAMES // PIECES
BATCH = 4
BATCHES = TILES // BATCH
SUMS = BLOCK + 8
SHARPNESS = math.log2(math.e) / math.sqrt(D)
LAST = (((1,), (1,)), ((), ()))


def split(value):
    high = value.astype(BF16)
    return high, (value - high.astype(F32)).astype(BF16)


def em_kernel(
    frames, codebook, cent_out, count_out,
    tok, thi, tlo, tnorm, cod, chi, clo, cnorm, scores, tops, top, total, lognorm, stats, part, rs1, mid, rs2, fin, flip,
    own_sem, tok_send, tok_recv, share_send, share_recv, c1_send, c1_recv, c2_send, c2_recv, st_send, st_recv,
    r1_send, r1_recv, r2_send, r2_recv, f_send, f_recv,
):
    z = lax.axis_index("tok")
    place = lax.axis_index("code")
    core = lax.rem(place, CORES)
    y = lax.rem(place // CORES, N)
    x = place // (CORES * N)
    mine = core * N + z

    def at(pz, px, py, pc):
        return (pz, (px * N + py) * CORES + pc)

    def ahead(p, o):
        return lax.rem(p + o, N)

    def remote(src, dst, send_sem, recv_sem, device):
        return pltpu.make_async_remote_copy(
            src_ref=src, dst_ref=dst, send_sem=send_sem, recv_sem=recv_sem, device_id=device, device_id_type=MESH
        )

    def await_bytes(ref, sem):
        pltpu.make_async_copy(ref, ref, sem).wait()

    def group_peer(j):
        peer = lax.rem(mine + j, GROUP)
        return at(lax.rem(peer, N), x, y, peer // N)

    barrier = pltpu.get_barrier_semaphore()
    peers = [at(z, ahead(x, o), y, core) for o in range(1, N)]
    peers += [at(z, x, ahead(y, o), core) for o in range(1, N)]
    peers += [group_peer(j) for j in range(1, GROUP)]
    for peer in peers:
        pl.semaphore_signal(barrier, inc=1, device_id=peer, device_id_type=MESH)
    pl.semaphore_wait(barrier, len(peers))

    def block_of(half, o):
        return ahead(y, o) if half == 0 else N + ahead(x, o)

    def across(half, o):
        return at(z, ahead(x, o), y, core) if half == 0 else at(z, x, ahead(y, o), core)

    def along(half, o):
        return at(z, x, ahead(y, o), core) if half == 0 else at(z, ahead(x, o), y, core)

    slot = (x, y)

    def start_stage1(it, half, src):
        dst = cod.at[it, block_of(half, 0), slot[half]]
        for o in (2, 1, 3):
            remote(src, dst, c1_send.at[it, half, o - 1], c1_recv.at[it, half, o - 1], across(half, o)).start()

    def await_stage1(it, half):
        for o in range(1, N):
            await_bytes(cod.at[it, 0, 0], c1_recv.at[it, half, o - 1])

    def start_stage2(it, half, places):
        block = cod.at[it, block_of(half, 0)]
        for o in places:
            remote(block, block, c2_send.at[it, half, o - 1], c2_recv.at[it, half, o - 1], along(half, o)).start()

    def await_block(it, half, o):
        await_bytes(cod.at[it, 0], c2_recv.at[it, half, N - 1 - o])

    before, after, opposite = ahead(z, N - 1), ahead(z, 1), ahead(z, 2)
    first, other = core * N, (1 - core) * N
    next_device, last_device = at(after, x, y, core), at(before, x, y, core)

    def rows_of(p, part=0, parts=1):
        return pl.ds(p * ROWS + part * (ROWS // parts), ROWS // parts)

    def direct(p):
        src, dst = frames.at[rows_of(p)], tok.at[first + z, rows_of(p)]
        remote(src, dst, tok_send.at[p, 0], tok_recv.at[p, 0], next_device).start()
        remote(src, dst, tok_send.at[p, 1], tok_recv.at[p, 1], last_device).start()

    def forward(p):
        await_bytes(tok.at[0, rows_of(p)], tok_recv.at[p, 0])
        low = tok.at[first + before, rows_of(p, 0, 2)]
        remote(low, low, tok_send.at[p, 2], tok_recv.at[p, 2], next_device).start()
        await_bytes(tok.at[0, rows_of(p)], tok_recv.at[p, 1])
        high = tok.at[first + after, rows_of(p, 1, 2)]
        remote(high, high, tok_send.at[p, 3], tok_recv.at[p, 3], last_device).start()

    def await_forwarded():
        for p in range(PIECES):
            await_bytes(tok.at[0, rows_of(p, 0, 2)], tok_recv.at[p, 2])
            await_bytes(tok.at[0, rows_of(p, 1, 2)], tok_recv.at[p, 3])

    def share(i, src, place):
        remote(src, tok.at[first + place], share_send.at[i], share_recv.at[i], at(z, x, y, 1 - core)).start()

    def await_shared(i):
        await_bytes(tok.at[0], share_recv.at[i])

    own_codes = [codebook.at[z, half] for half in range(2)]
    keep = [
        pltpu.make_async_copy(own_codes[0], cod.at[0, y, x], own_sem.at[0]),
        pltpu.make_async_copy(own_codes[1], cod.at[0, N + x, y], own_sem.at[1]),
        pltpu.make_async_copy(frames, tok.at[first + z], own_sem.at[2]),
    ]
    for half in range(2):
        start_stage1(0, half, own_codes[half])
    for copy in keep:
        copy.start()
    for p in range(PIECES):
        direct(p)
    share(0, frames, z)
    for copy in keep:
        copy.wait()
    for half in range(2):
        await_stage1(0, half)
        start_stage2(0, half, (1, 3, 2))
    forward(0)
    forward(1)
    for half in range(2):
        for o in range(1, N):
            await_block(0, half, o)
    forward(2)

    def parts_of(codes):
        norms = jnp.sum(codes * codes, axis=1, keepdims=True) * SHARPNESS
        return *split(codes * (2.0 * SHARPNESS)), jnp.broadcast_to(norms, (codes.shape[0], 128))

    def split_block(b, _):
        chi[b], clo[b], cnorm[b] = parts_of(cod[0, b].reshape(BLOCK, D))
        return 0

    lax.fori_loop(0, BLOCKS, split_block, 0)

    def score(high, low, norms, g):
        inner = lax.dot_general(
            jnp.concatenate([high, high, low], axis=1),
            jnp.concatenate([thi[g], tlo[g], thi[g]], axis=1),
            LAST,
            preferred_element_type=F32,
        )
        return inner - jnp.tile(norms, (1, TILE // 128))

    def add_up(g, tiles, carry):
        old_top, old_total = carry if carry is not None else (None, None)
        new_top = tops[g] if carry is None else jnp.maximum(old_top, tops[g])
        new_total = None if carry is None else old_total * jnp.exp2(old_top - new_top)
        for tile in tiles:
            more = jnp.sum(jnp.exp2(tile - new_top), axis=0, keepdims=True)
            new_total = more if new_total is None else new_total + more
        return new_top, new_total

    def publish(it, g, row_top, row_total):
        norm = tnorm[g]
        shift = (row_top - norm) + norm
        stats[it, g // BATCH, mine, g % BATCH] = shift + jnp.log2(row_total * jnp.exp2(row_top - shift))

    def send_stats(it, batch):
        own = stats.at[it, batch, mine]
        for j in range(1, GROUP):
            remote(own, own, st_send.at[it, batch], st_recv.at[it, batch], group_peer(j)).start()

    def normalise(it, batch):
        await_bytes(stats.at[it, batch, pl.ds(0, GROUP - 1)], st_recv.at[it, batch])
        for q in range(BATCH):
            g = batch * BATCH + q
            logs = stats[it, batch, :, q, 0, :]
            highest = jnp.max(logs, axis=0, keepdims=True)
            lognorm[g] = highest + jnp.log2(jnp.sum(jnp.exp2(logs - highest), axis=0, keepdims=True))

    def score_tile(g):
        thi[g], tlo[g] = split(tok[g])
        high, low = chi[...].reshape(BLOCKS * BLOCK, D), clo[...].reshape(BLOCKS * BLOCK, D)
        tile_scores = score(high, low, cnorm[...].reshape(BLOCKS * BLOCK, 128), g)
        scores[:, g] = tile_scores.reshape(BLOCKS, BLOCK, TILE)
        tops[g] = jnp.max(tile_scores, axis=0, keepdims=True)

    def sum_tile(g):
        squares = tok[g] * tok[g]
        squares = squares[:, :128] + squares[:, 128:]
        tnorm[g] = jnp.sum(squares.T, axis=0, keepdims=True) * SHARPNESS
        publish(0, g, *add_up(g, [scores[:, g].reshape(BLOCKS * BLOCK, TILE)], None))

    def source(i):
        place = jnp.where(i < 2, z, jnp.where(i < 6, jnp.where(i % 2 == 0, before, after), opposite))
        ours = (i == 0) | (i == 2) | (i == 3)
        return jnp.where(i < 6, jnp.where(ours, core, 1 - core), i - 6) * N + place

    def move_on(i):
        @pl.when(i == 1)
        def _():
            forward(3)
            share(1, tok.at[first + before], before)
            share(2, tok.at[first + after], after)
            await_shared(0)

        @pl.when(i == 4)
        def _():
            await_shared(1)

        @pl.when(i == 5)
        def _():
            await_shared(2)

        @pl.when(i == 6)
        def _():
            await_forwarded()
            share(3, tok.at[first + opposite], opposite)
            await_shared(3)

    score_tile(source(0))

    def step(i, _):
        move_on(i)
        sum_tile(source(i - 1))
        score_tile(source(i))

        @pl.when(i == TILES - 1)
        def _():
            send_stats(0, 0)

        return 0

    lax.fori_loop(1, TILES, step, 0)
    sum_tile(source(TILES - 1))
    send_stats(0, 1)

    def gray(i):
        return jnp.bitwise_xor(i, i // 2)

    def weigh(blocks, tiles):
        lefts, rights, counts = [], [], None
        for g in tiles:
            pair_scores = jnp.concatenate([scores[b, g] for b in blocks], axis=0)
            weights = jnp.exp2(pair_scores - lognorm[g])
            for c in range(TILE // 128):
                piece = weights[:, c * 128 : (c + 1) * 128]
                counts = piece if counts is None else counts + piece
            high, low = split(weights)
            lefts += [high, high, low]
            rights += [thi[g], tlo[g], thi[g]]
        weighted = jnp.dot(jnp.concatenate(lefts, axis=1), jnp.concatenate(rights, axis=0), preferred_element_type=F32)
        for half in range(2):
            part[blocks[half], pl.ds(0, BLOCK)] += weighted[half * BLOCK : (half + 1) * BLOCK]
            row = jnp.sum(counts[half * BLOCK : (half + 1) * BLOCK].T, axis=0, keepdims=True)
            part[blocks[half], pl.ds(BLOCK, 8)] += jnp.broadcast_to(jnp.tile(row, (1, 2)), (8, D))

    def moments(it):
        batches = BATCHES if it == 0 else 1
        part[...] = jnp.zeros_like(part)
        normalise(it, 0)
        if batches == 1:
            normalise(it, 1)

        def step(i, _):
            o, batch = gray(N - 1 - i // batches), i % batches

            if batches > 1:

                @pl.when(i == 1)
                def _():
                    normalise(it, 1)

            blocks = [block_of(half, o) for half in range(2)]
            size = TILES // batches
            weigh(blocks, [batch * size + q for q in range(size)])

            @pl.when((batch == batches - 1) & (o != 0))
            def _():
                for half in range(2):
                    remote(
                        part.at[blocks[half]], rs1.at[it, half, o - 1], r1_send.at[it, half, o - 1], r1_recv.at[it, half, o - 1], along(half, o)
                    ).start()

            return 0

        lax.fori_loop(0, N * batches, step, 0)

    def reduce_sums(it, use):
        for half in range(2):
            for o in range(1, N):
                await_bytes(part.at[0], r1_recv.at[it, half, o - 1])
            row = part[block_of(half, 0)] + rs1[it, half, 0] + rs1[it, half, 1] + rs1[it, half, 2]
            for p in range(N):
                mid[half, p, pl.ds(0, HALF)] = row[p * HALF : (p + 1) * HALF]
                mid[half, p, pl.ds(HALF, 8)] = row[BLOCK:]
            for o in (2, 1, 3):
                remote(
                    mid.at[half, ahead(slot[half], o)], rs2.at[it, half, o - 1], r2_send.at[it, half, o - 1], r2_recv.at[it, half, o - 1], across(half, o)
                ).start()
        for half in range(2):
            for o in range(1, N):
                await_bytes(mid.at[0, 0], r2_recv.at[it, half, o - 1])
            sums = mid[half, slot[half]] + rs2[it, half, 0] + rs2[it, half, 1] + rs2[it, half, 2]
            flip[half] = jnp.broadcast_to(sums[HALF : HALF + 1, :128], (128, 128)).T
            count = flip[half, pl.ds(pl.multiple_of(slot[half] * HALF, HALF), HALF)]
            old = cod[it, block_of(half, 0), slot[half]]
            use(half, (sums[:HALF] + PRIOR_WEIGHT * old) / (jnp.tile(count, (1, 2)) + PRIOR_WEIGHT), count)

    def sent(it):
        for half in range(2):
            for o in range(1, N):
                await_bytes(part.at[0], r1_send.at[it, half, o - 1])
                await_bytes(mid.at[0, 0], r2_send.at[it, half, o - 1])

    def next_codes(half, codes, _):
        cod[1, block_of(half, 0), slot[half]] = codes
        start_stage1(1, half, cod.at[1, block_of(half, 0), slot[half]])

    moments(0)
    reduce_sums(0, next_codes)
    for half in range(2):
        await_stage1(1, half)
        start_stage2(1, half, (1, 3))

    def score_pair(o):
        blocks = [block_of(half, o) for half in range(2)]
        codes = jnp.concatenate([cod[1, b].reshape(BLOCK, D) for b in blocks], axis=0)
        high, low, norms = parts_of(codes)
        for g in range(TILES):
            tile_scores = score(high, low, norms, g)
            for half in range(2):
                scores[blocks[half], g] = tile_scores[half * BLOCK : (half + 1) * BLOCK]
            tops[g] = jnp.max(tile_scores, axis=0, keepdims=True)

    def sum_pair(o, g):
        blocks = [block_of(half, o) for half in range(2)]
        return add_up(g, [scores[b, g] for b in blocks], (top[g], total[g]))

    top[...] = jnp.full_like(top, -1e30)
    total[...] = jnp.zeros_like(total)
    score_pair(0)
    for half in range(2):
        start_stage2(1, half, (2,))

    def pair_step(i, _):
        o, previous = gray(i), gray(i - 1)
        for half in range(2):
            await_block(1, half, o)
        for g in range(TILES):
            top[g], total[g] = sum_pair(previous, g)
        score_pair(o)
        return 0

    lax.fori_loop(1, N, pair_step, 0)

    def last_sum(batch, _):
        for q in range(BATCH):
            g = batch * BATCH + q
            publish(1, g, *sum_pair(N // 2, g))
        send_stats(1, batch)
        return 0

    lax.fori_loop(0, BATCHES, last_sum, 0)
    sent(0)
    moments(1)

    def last_codes(half, codes, count):
        fin[z, pl.ds(half * HALF, HALF)] = codes
        flip[2, pl.ds(half * HALF, HALF)] = count

    flip[2] = jnp.zeros((128, 128), F32)
    reduce_sums(1, last_codes)
    fin[z, pl.ds(2 * HALF, 8)] = jnp.tile(flip[2].T[:8], (1, 2))
    for o in (2, 1, 3):
        remote(fin.at[z], fin.at[z], f_send.at[o - 1], f_recv.at[o - 1], at(ahead(z, o), x, y, core)).start()
    sent(1)

    for p in range(PIECES):
        for i in range(2):
            await_bytes(tok.at[0, rows_of(p)], tok_send.at[p, i])
            await_bytes(tok.at[0, rows_of(p, 0, 2)], tok_send.at[p, 2 + i])
    for i in range(4):
        await_bytes(tok.at[0], share_send.at[i])
    for it in range(ITERS):
        for batch in range(BATCHES):
            await_bytes(stats.at[it, batch, pl.ds(0, GROUP - 1)], st_send.at[it, batch])
        for half in range(2):
            for o in range(1, N):
                await_bytes(cod.at[it, 0, 0], c1_send.at[it, half, o - 1])
                await_bytes(cod.at[it, 0], c2_send.at[it, half, o - 1])
    for o in range(1, N):
        await_bytes(fin.at[0], f_send.at[o - 1])
        await_bytes(fin.at[0], f_recv.at[o - 1])
    for p in range(N):
        cent_out[pl.ds(p * 2 * HALF, 2 * HALF)] = fin[p, pl.ds(0, 2 * HALF)]
        count_out[:, pl.ds(p * 2 * HALF, 2 * HALF)] = fin[p, pl.ds(2 * HALF, 1), pl.ds(0, 2 * HALF)]


def hand_on(cent, count, cent_out, count_out):
    cent_out[...] = cent[...]
    count_out[...] = count[...]


def on_device(tokens, codebook):
    vmem, dma = pltpu.VMEM, pltpu.SemaphoreType.DMA
    peers = N - 1
    results = [jax.ShapeDtypeStruct((OWNED, D), F32), jax.ShapeDtypeStruct((1, OWNED), F32)]
    centroids, counts = pl.pallas_call(
        em_kernel,
        out_shape=results,
        in_specs=[pl.BlockSpec(memory_space=pl.ANY)] * 2,
        out_specs=[pl.BlockSpec(memory_space=vmem)] * 2,
        scratch_shapes=[
            vmem((TILES, TILE, D), F32),
            vmem((TILES, TILE, D), BF16),
            vmem((TILES, TILE, D), BF16),
            vmem((TILES, 1, TILE), F32),
            vmem((ITERS, BLOCKS, N, HALF, D), F32),
            vmem((BLOCKS, BLOCK, D), BF16),
            vmem((BLOCKS, BLOCK, D), BF16),
            vmem((BLOCKS, BLOCK, 128), F32),
            vmem((BLOCKS, TILES, BLOCK, TILE), F32),
            vmem((TILES, 1, TILE), F32),
            vmem((TILES, 1, TILE), F32),
            vmem((TILES, 1, TILE), F32),
            vmem((TILES, 1, TILE), F32),
            vmem((ITERS, BATCHES, GROUP, BATCH, 1, TILE), F32),
            vmem((BLOCKS, SUMS, D), F32),
            vmem((ITERS, 2, peers, SUMS, D), F32),
            vmem((2, N, HALF + 8, D), F32),
            vmem((ITERS, 2, peers, HALF + 8, D), F32),
            vmem((N, 2 * HALF + 8, D), F32),
            vmem((3, 128, 128), F32),
            dma((3,)),
            dma((PIECES, 4)),
            dma((PIECES, 4)),
            dma((4,)),
            dma((4,)),
            dma((ITERS, 2, peers)),
            dma((ITERS, 2, peers)),
            dma((ITERS, 2, peers)),
            dma((ITERS, 2, peers)),
            dma((ITERS, BATCHES)),
            dma((ITERS, BATCHES)),
            dma((ITERS, 2, peers)),
            dma((ITERS, 2, peers)),
            dma((ITERS, 2, peers)),
            dma((ITERS, 2, peers)),
            dma((peers,)),
            dma((peers,)),
        ],
        compiler_params=pltpu.CompilerParams(collective_id=0, has_side_effects=True, vmem_limit_bytes=56 << 20),
        cost_estimate=pl.CostEstimate(
            flops=ITERS * 2 * 3 * 2 * TILES * TILE * BLOCKS * BLOCK * D,
            bytes_accessed=4 * (FRAMES + 2 * OWNED) * D,
            transcendentals=ITERS * 2 * TILES * TILE * BLOCKS * BLOCK,
        ),
    )(tokens, codebook.reshape(N, 2, HALF, D))
    centroids, counts = pl.pallas_call(
        hand_on,
        out_shape=results,
        in_specs=[pl.BlockSpec(memory_space=vmem)] * 2,
        out_specs=[pl.BlockSpec(memory_space=vmem)] * 2,
    )(centroids, counts)
    return centroids, counts.reshape(OWNED)


def solution(mesh):
    return jax.shard_map(
        on_device,
        mesh=mesh,
        in_specs=(P(("tok", "code"), None), P("code", None)),
        out_specs=(P("code", None), P("code")),
        check_vma=False,
    )
```

```python
import functools
import math

import jax
import jax.numpy as jnp
from jax import lax
from jax.experimental import pallas as pl
from jax.experimental.pallas import tpu as pltpu
from jax.sharding import PartitionSpec as P

MESH = pl.DeviceIdType.MESH
F32, BF16 = jnp.float32, jnp.bfloat16
ITERS = 2
PRIOR_WEIGHT = 1.0
N = 4
CORES = 2
GROUP = N * CORES
D = 256
FRAMES = 512
OWNED = 256
HALF = OWNED // N // 2
BLOCK = N * HALF
BLOCKS = 2 * N
TILES = GROUP
TILE = FRAMES
PIECES = 4
ROWS = FRAMES // PIECES
BATCH = 4
BATCHES = TILES // BATCH
SUMS = BLOCK + 8
SHARPNESS = math.log2(math.e) / math.sqrt(D)
LAST = (((1,), (1,)), ((), ()))


def split(value):
    high = value.astype(BF16)
    return high, (value - high.astype(F32)).astype(BF16)


def em_kernel(
    frames, codebook, cent_out, count_out,
    tok, thi, tlo, tnorm, cod, chi, clo, cnorm, scores, tops, top, total, lognorm, stats, part, rs1, mid, rs2, fin, flip,
    own_sem, tok_send, tok_recv, share_send, share_recv, c1_send, c1_recv, c2_send, c2_recv, st_send, st_recv,
    r1_send, r1_recv, r2_send, r2_recv, f_send, f_recv,
):
    z = lax.axis_index("tok")
    place = lax.axis_index("code")
    core = lax.rem(place, CORES)
    y = lax.rem(place // CORES, N)
    x = place // (CORES * N)
    mine = core * N + z

    def at(pz, px, py, pc):
        return (pz, (px * N + py) * CORES + pc)

    def ahead(p, o):
        return lax.rem(p + o, N)

    def remote(src, dst, send_sem, recv_sem, device):
        return pltpu.make_async_remote_copy(
            src_ref=src, dst_ref=dst, send_sem=send_sem, recv_sem=recv_sem, device_id=device, device_id_type=MESH
        )

    def await_bytes(ref, sem):
        pltpu.make_async_copy(ref, ref, sem).wait()

    def group_peer(j):
        peer = lax.rem(mine + j, GROUP)
        return at(lax.rem(peer, N), x, y, peer // N)

    barrier = pltpu.get_barrier_semaphore()
    peers = [at(z, ahead(x, o), y, core) for o in range(1, N)]
    peers += [at(z, x, ahead(y, o), core) for o in range(1, N)]
    peers += [group_peer(j) for j in range(1, GROUP)]
    for peer in peers:
        pl.semaphore_signal(barrier, inc=1, device_id=peer, device_id_type=MESH)
    pl.semaphore_wait(barrier, len(peers))

    def block_of(half, o):
        return ahead(y, o) if half == 0 else N + ahead(x, o)

    def across(half, o):
        return at(z, ahead(x, o), y, core) if half == 0 else at(z, x, ahead(y, o), core)

    def along(half, o):
        return at(z, x, ahead(y, o), core) if half == 0 else at(z, ahead(x, o), y, core)

    slot = (x, y)

    def start_stage1(it, half, src):
        dst = cod.at[it, block_of(half, 0), slot[half]]
        for o in (2, 1, 3):
            remote(src, dst, c1_send.at[it, half, o - 1], c1_recv.at[it, half, o - 1], across(half, o)).start()

    def await_stage1(it, half):
        for o in range(1, N):
            await_bytes(cod.at[it, 0, 0], c1_recv.at[it, half, o - 1])

    def start_stage2(it, half, places):
        block = cod.at[it, block_of(half, 0)]
        for o in places:
            remote(block, block, c2_send.at[it, half, o - 1], c2_recv.at[it, half, o - 1], along(half, o)).start()

    def await_block(it, half, o):
        await_bytes(cod.at[it, 0], c2_recv.at[it, half, N - 1 - o])

    before, after, opposite = ahead(z, N - 1), ahead(z, 1), ahead(z, 2)
    first, other = core * N, (1 - core) * N
    next_device, last_device = at(after, x, y, core), at(before, x, y, core)

    def rows_of(p, part=0, parts=1):
        return pl.ds(p * ROWS + part * (ROWS // parts), ROWS // parts)

    def direct(p):
        src, dst = frames.at[rows_of(p)], tok.at[first + z, rows_of(p)]
        remote(src, dst, tok_send.at[p, 0], tok_recv.at[p, 0], next_device).start()
        remote(src, dst, tok_send.at[p, 1], tok_recv.at[p, 1], last_device).start()

    def forward(p):
        await_bytes(tok.at[0, rows_of(p)], tok_recv.at[p, 0])
        low = tok.at[first + before, rows_of(p, 0, 2)]
        remote(low, low, tok_send.at[p, 2], tok_recv.at[p, 2], next_device).start()
        await_bytes(tok.at[0, rows_of(p)], tok_recv.at[p, 1])
        high = tok.at[first + after, rows_of(p, 1, 2)]
        remote(high, high, tok_send.at[p, 3], tok_recv.at[p, 3], last_device).start()

    def await_forwarded():
        for p in range(PIECES):
            await_bytes(tok.at[0, rows_of(p, 0, 2)], tok_recv.at[p, 2])
            await_bytes(tok.at[0, rows_of(p, 1, 2)], tok_recv.at[p, 3])

    def share(i, src, place):
        remote(src, tok.at[first + place], share_send.at[i], share_recv.at[i], at(z, x, y, 1 - core)).start()

    def await_shared(i):
        await_bytes(tok.at[0], share_recv.at[i])

    own_codes = [codebook.at[z, half] for half in range(2)]
    keep = [
        pltpu.make_async_copy(own_codes[0], cod.at[0, y, x], own_sem.at[0]),
        pltpu.make_async_copy(own_codes[1], cod.at[0, N + x, y], own_sem.at[1]),
        pltpu.make_async_copy(frames, tok.at[first + z], own_sem.at[2]),
    ]
    for half in range(2):
        start_stage1(0, half, own_codes[half])
    for copy in keep:
        copy.start()
    for p in range(PIECES):
        direct(p)
    share(0, frames, z)
    for copy in keep:
        copy.wait()
    for half in range(2):
        await_stage1(0, half)
        start_stage2(0, half, (1, 3, 2))
    forward(0)
    forward(1)
    for half in range(2):
        for o in range(1, N):
            await_block(0, half, o)

    def parts_of(codes):
        norms = jnp.sum(codes * codes, axis=1, keepdims=True) * SHARPNESS
        return *split(codes * (2.0 * SHARPNESS)), jnp.broadcast_to(norms, (codes.shape[0], 128))

    def split_block(b, _):
        chi[b], clo[b], cnorm[b] = parts_of(cod[0, b].reshape(BLOCK, D))
        return 0

    lax.fori_loop(0, BLOCKS, split_block, 0)

    def score(high, low, norms, g):
        inner = lax.dot_general(
            jnp.concatenate([high, high, low], axis=1),
            jnp.concatenate([thi[g], tlo[g], thi[g]], axis=1),
            LAST,
            preferred_element_type=F32,
        )
        return inner - jnp.tile(norms, (1, TILE // 128))

    def add_up(g, tiles, carry):
        old_top, old_total = carry if carry is not None else (None, None)
        new_top = tops[g] if carry is None else jnp.maximum(old_top, tops[g])
        new_total = None if carry is None else old_total * jnp.exp2(old_top - new_top)
        for tile in tiles:
            more = jnp.sum(jnp.exp2(tile - new_top), axis=0, keepdims=True)
            new_total = more if new_total is None else new_total + more
        return new_top, new_total

    def publish(it, g, row_top, row_total):
        norm = tnorm[g]
        shift = (row_top - norm) + norm
        stats[it, g // BATCH, mine, g % BATCH] = shift + jnp.log2(row_total * jnp.exp2(row_top - shift))

    def send_stats(it, batch):
        own = stats.at[it, batch, mine]
        for j in range(1, GROUP):
            remote(own, own, st_send.at[it, batch], st_recv.at[it, batch], group_peer(j)).start()

    def normalise(it, batch):
        await_bytes(stats.at[it, batch, pl.ds(0, GROUP - 1)], st_recv.at[it, batch])
        for q in range(BATCH):
            g = batch * BATCH + q
            logs = stats[it, batch, :, q, 0, :]
            highest = jnp.max(logs, axis=0, keepdims=True)
            lognorm[g] = highest + jnp.log2(jnp.sum(jnp.exp2(logs - highest), axis=0, keepdims=True))

    def score_tile(g):
        thi[g], tlo[g] = split(tok[g])
        high, low = chi[...].reshape(BLOCKS * BLOCK, D), clo[...].reshape(BLOCKS * BLOCK, D)
        tile_scores = score(high, low, cnorm[...].reshape(BLOCKS * BLOCK, 128), g)
        scores[:, g] = tile_scores.reshape(BLOCKS, BLOCK, TILE)
        tops[g] = jnp.max(tile_scores, axis=0, keepdims=True)

    def sum_tile(g):
        squares = tok[g] * tok[g]
        squares = squares[:, :128] + squares[:, 128:]
        tnorm[g] = jnp.sum(squares.T, axis=0, keepdims=True) * SHARPNESS
        publish(0, g, *add_up(g, [scores[:, g].reshape(BLOCKS * BLOCK, TILE)], None))

    def source(i):
        place = jnp.where(i < 2, z, jnp.where(i < 6, jnp.where(i % 2 == 0, before, after), opposite))
        ours = (i == 0) | (i == 2) | (i == 3)
        return jnp.where(i < 6, jnp.where(ours, core, 1 - core), i - 6) * N + place

    def move_on(i):
        @pl.when(i == 1)
        def _():
            await_shared(0)

        @pl.when(i == 2)
        def _():
            forward(2)
            forward(3)
            share(1, tok.at[first + before], before)
            share(2, tok.at[first + after], after)

        @pl.when(i == 4)
        def _():
            await_shared(1)

        @pl.when(i == 5)
        def _():
            await_shared(2)

        @pl.when(i == 6)
        def _():
            await_forwarded()
            share(3, tok.at[first + opposite], opposite)
            await_shared(3)

    score_tile(source(0))

    def step(i, _):
        move_on(i)
        sum_tile(source(i - 1))
        score_tile(source(i))

        @pl.when(i == TILES - 1)
        def _():
            send_stats(0, 0)

        return 0

    lax.fori_loop(1, TILES, step, 0)
    sum_tile(source(TILES - 1))
    send_stats(0, 1)

    def gray(i):
        return jnp.bitwise_xor(i, i // 2)

    def weigh(blocks, tiles):
        lefts, rights, counts = [], [], None
        for g in tiles:
            pair_scores = jnp.concatenate([scores[b, g] for b in blocks], axis=0)
            weights = jnp.exp2(pair_scores - lognorm[g])
            for c in range(TILE // 128):
                piece = weights[:, c * 128 : (c + 1) * 128]
                counts = piece if counts is None else counts + piece
            high, low = split(weights)
            lefts += [high, high, low]
            rights += [thi[g], tlo[g], thi[g]]
        weighted = jnp.dot(jnp.concatenate(lefts, axis=1), jnp.concatenate(rights, axis=0), preferred_element_type=F32)
        for half in range(2):
            part[blocks[half], pl.ds(0, BLOCK)] += weighted[half * BLOCK : (half + 1) * BLOCK]
            row = jnp.sum(counts[half * BLOCK : (half + 1) * BLOCK].T, axis=0, keepdims=True)
            part[blocks[half], pl.ds(BLOCK, 8)] += jnp.broadcast_to(jnp.tile(row, (1, 2)), (8, D))

    def moments(it):
        batches = BATCHES if it == 0 else 1
        part[...] = jnp.zeros_like(part)
        normalise(it, 0)
        if batches == 1:
            normalise(it, 1)

        def step(i, _):
            o, batch = gray(N - 1 - i // batches), i % batches

            if batches > 1:

                @pl.when(i == 1)
                def _():
                    normalise(it, 1)

            blocks = [block_of(half, o) for half in range(2)]
            size = TILES // batches
            weigh(blocks, [batch * size + q for q in range(size)])

            @pl.when((batch == batches - 1) & (o != 0))
            def _():
                for half in range(2):
                    remote(
                        part.at[blocks[half]], rs1.at[it, half, o - 1], r1_send.at[it, half, o - 1], r1_recv.at[it, half, o - 1], along(half, o)
                    ).start()

            return 0

        lax.fori_loop(0, N * batches, step, 0)

    def reduce_sums(it, use):
        for half in range(2):
            for o in range(1, N):
                await_bytes(part.at[0], r1_recv.at[it, half, o - 1])
            row = part[block_of(half, 0)] + rs1[it, half, 0] + rs1[it, half, 1] + rs1[it, half, 2]
            for p in range(N):
                mid[half, p, pl.ds(0, HALF)] = row[p * HALF : (p + 1) * HALF]
                mid[half, p, pl.ds(HALF, 8)] = row[BLOCK:]
            for o in (2, 1, 3):
                remote(
                    mid.at[half, ahead(slot[half], o)], rs2.at[it, half, o - 1], r2_send.at[it, half, o - 1], r2_recv.at[it, half, o - 1], across(half, o)
                ).start()
        for half in range(2):
            for o in range(1, N):
                await_bytes(mid.at[0, 0], r2_recv.at[it, half, o - 1])
            sums = mid[half, slot[half]] + rs2[it, half, 0] + rs2[it, half, 1] + rs2[it, half, 2]
            flip[half] = jnp.broadcast_to(sums[HALF : HALF + 1, :128], (128, 128)).T
            count = flip[half, pl.ds(pl.multiple_of(slot[half] * HALF, HALF), HALF)]
            old = cod[it, block_of(half, 0), slot[half]]
            use(half, (sums[:HALF] + PRIOR_WEIGHT * old) / (jnp.tile(count, (1, 2)) + PRIOR_WEIGHT), count)

    def sent(it):
        for half in range(2):
            for o in range(1, N):
                await_bytes(part.at[0], r1_send.at[it, half, o - 1])
                await_bytes(mid.at[0, 0], r2_send.at[it, half, o - 1])

    def next_codes(half, codes, _):
        cod[1, block_of(half, 0), slot[half]] = codes
        start_stage1(1, half, cod.at[1, block_of(half, 0), slot[half]])

    moments(0)
    reduce_sums(0, next_codes)
    for half in range(2):
        await_stage1(1, half)
        start_stage2(1, half, (1, 3))

    def score_pair(o):
        blocks = [block_of(half, o) for half in range(2)]
        codes = jnp.concatenate([cod[1, b].reshape(BLOCK, D) for b in blocks], axis=0)
        high, low, norms = parts_of(codes)
        for g in range(TILES):
            tile_scores = score(high, low, norms, g)
            for half in range(2):
                scores[blocks[half], g] = tile_scores[half * BLOCK : (half + 1) * BLOCK]
            tops[g] = jnp.max(tile_scores, axis=0, keepdims=True)

    def sum_pair(o, g):
        blocks = [block_of(half, o) for half in range(2)]
        return add_up(g, [scores[b, g] for b in blocks], (top[g], total[g]))

    top[...] = jnp.full_like(top, -1e30)
    total[...] = jnp.zeros_like(total)
    score_pair(0)
    for half in range(2):
        start_stage2(1, half, (2,))

    def pair_step(i, _):
        o, previous = gray(i), gray(i - 1)
        for half in range(2):
            await_block(1, half, o)
        for g in range(TILES):
            top[g], total[g] = sum_pair(previous, g)
        score_pair(o)
        return 0

    lax.fori_loop(1, N, pair_step, 0)

    def last_sum(batch, _):
        for q in range(BATCH):
            g = batch * BATCH + q
            publish(1, g, *sum_pair(N // 2, g))
        send_stats(1, batch)
        return 0

    lax.fori_loop(0, BATCHES, last_sum, 0)
    sent(0)
    moments(1)

    def last_codes(half, codes, count):
        fin[z, pl.ds(half * HALF, HALF)] = codes
        flip[2, pl.ds(half * HALF, HALF)] = count

    flip[2] = jnp.zeros((128, 128), F32)
    reduce_sums(1, last_codes)
    fin[z, pl.ds(2 * HALF, 8)] = jnp.tile(flip[2].T[:8], (1, 2))
    for o in (2, 1, 3):
        remote(fin.at[z], fin.at[z], f_send.at[o - 1], f_recv.at[o - 1], at(ahead(z, o), x, y, core)).start()
    sent(1)

    for p in range(PIECES):
        for i in range(2):
            await_bytes(tok.at[0, rows_of(p)], tok_send.at[p, i])
            await_bytes(tok.at[0, rows_of(p, 0, 2)], tok_send.at[p, 2 + i])
    for i in range(4):
        await_bytes(tok.at[0], share_send.at[i])
    for it in range(ITERS):
        for batch in range(BATCHES):
            await_bytes(stats.at[it, batch, pl.ds(0, GROUP - 1)], st_send.at[it, batch])
        for half in range(2):
            for o in range(1, N):
                await_bytes(cod.at[it, 0, 0], c1_send.at[it, half, o - 1])
                await_bytes(cod.at[it, 0], c2_send.at[it, half, o - 1])
    for o in range(1, N):
        await_bytes(fin.at[0], f_send.at[o - 1])
        await_bytes(fin.at[0], f_recv.at[o - 1])
    for p in range(N):
        cent_out[pl.ds(p * 2 * HALF, 2 * HALF)] = fin[p, pl.ds(0, 2 * HALF)]
        count_out[:, pl.ds(p * 2 * HALF, 2 * HALF)] = fin[p, pl.ds(2 * HALF, 1), pl.ds(0, 2 * HALF)]


def hand_on(cent, count, cent_out, count_out):
    cent_out[...] = cent[...]
    count_out[...] = count[...]


def on_device(tokens, codebook):
    vmem, dma = pltpu.VMEM, pltpu.SemaphoreType.DMA
    peers = N - 1
    results = [jax.ShapeDtypeStruct((OWNED, D), F32), jax.ShapeDtypeStruct((1, OWNED), F32)]
    centroids, counts = pl.pallas_call(
        em_kernel,
        out_shape=results,
        in_specs=[pl.BlockSpec(memory_space=pl.ANY)] * 2,
        out_specs=[pl.BlockSpec(memory_space=vmem)] * 2,
        scratch_shapes=[
            vmem((TILES, TILE, D), F32),
            vmem((TILES, TILE, D), BF16),
            vmem((TILES, TILE, D), BF16),
            vmem((TILES, 1, TILE), F32),
            vmem((ITERS, BLOCKS, N, HALF, D), F32),
            vmem((BLOCKS, BLOCK, D), BF16),
            vmem((BLOCKS, BLOCK, D), BF16),
            vmem((BLOCKS, BLOCK, 128), F32),
            vmem((BLOCKS, TILES, BLOCK, TILE), F32),
            vmem((TILES, 1, TILE), F32),
            vmem((TILES, 1, TILE), F32),
            vmem((TILES, 1, TILE), F32),
            vmem((TILES, 1, TILE), F32),
            vmem((ITERS, BATCHES, GROUP, BATCH, 1, TILE), F32),
            vmem((BLOCKS, SUMS, D), F32),
            vmem((ITERS, 2, peers, SUMS, D), F32),
            vmem((2, N, HALF + 8, D), F32),
            vmem((ITERS, 2, peers, HALF + 8, D), F32),
            vmem((N, 2 * HALF + 8, D), F32),
            vmem((3, 128, 128), F32),
            dma((3,)),
            dma((PIECES, 4)),
            dma((PIECES, 4)),
            dma((4,)),
            dma((4,)),
            dma((ITERS, 2, peers)),
            dma((ITERS, 2, peers)),
            dma((ITERS, 2, peers)),
            dma((ITERS, 2, peers)),
            dma((ITERS, BATCHES)),
            dma((ITERS, BATCHES)),
            dma((ITERS, 2, peers)),
            dma((ITERS, 2, peers)),
            dma((ITERS, 2, peers)),
            dma((ITERS, 2, peers)),
            dma((peers,)),
            dma((peers,)),
        ],
        compiler_params=pltpu.CompilerParams(collective_id=0, has_side_effects=True, vmem_limit_bytes=56 << 20),
        cost_estimate=pl.CostEstimate(
            flops=ITERS * 2 * 3 * 2 * TILES * TILE * BLOCKS * BLOCK * D,
            bytes_accessed=4 * (FRAMES + 2 * OWNED) * D,
            transcendentals=ITERS * 2 * TILES * TILE * BLOCKS * BLOCK,
        ),
    )(tokens, codebook.reshape(N, 2, HALF, D))
    centroids, counts = pl.pallas_call(
        hand_on,
        out_shape=results,
        in_specs=[pl.BlockSpec(memory_space=vmem)] * 2,
        out_specs=[pl.BlockSpec(memory_space=vmem)] * 2,
    )(centroids, counts)
    return centroids, counts.reshape(OWNED)


def solution(mesh):
    return jax.shard_map(
        on_device,
        mesh=mesh,
        in_specs=(P(("tok", "code"), None), P("code", None)),
        out_specs=(P("code", None), P("code")),
        check_vma=False,
    )
```

```python
import functools
import math

import jax
import jax.numpy as jnp
from jax import lax
from jax.experimental import pallas as pl
from jax.experimental.pallas import tpu as pltpu
from jax.sharding import PartitionSpec as P

MESH = pl.DeviceIdType.MESH
F32, BF16 = jnp.float32, jnp.bfloat16
ITERS = 2
PRIOR_WEIGHT = 1.0
N = 4
CORES = 2
GROUP = N * CORES
D = 256
FRAMES = 512
OWNED = 256
HALF = OWNED // N // 2
BLOCK = N * HALF
BLOCKS = 2 * N
TILES = GROUP
TILE = FRAMES
PIECES = 4
ROWS = FRAMES // PIECES
BATCH = 4
BATCHES = TILES // BATCH
SUMS = BLOCK + 8
SHARPNESS = math.log2(math.e) / math.sqrt(D)
LAST = (((1,), (1,)), ((), ()))


def split(value):
    high = value.astype(BF16)
    return high, (value - high.astype(F32)).astype(BF16)


def em_kernel(
    frames, codebook, cent_out, count_out,
    tok, thi, tlo, tnorm, cod, chi, clo, cnorm, scores, tops, top, total, lognorm, stats, part, rs1, mid, rs2, fin, flip,
    own_sem, tok_send, tok_recv, share_send, share_recv, c1_send, c1_recv, c2_send, c2_recv, st_send, st_recv,
    r1_send, r1_recv, r2_send, r2_recv, f_send, f_recv,
):
    z = lax.axis_index("tok")
    place = lax.axis_index("code")
    core = lax.rem(place, CORES)
    y = lax.rem(place // CORES, N)
    x = place // (CORES * N)
    mine = core * N + z

    def at(pz, px, py, pc):
        return (pz, (px * N + py) * CORES + pc)

    def ahead(p, o):
        return lax.rem(p + o, N)

    def remote(src, dst, send_sem, recv_sem, device):
        return pltpu.make_async_remote_copy(
            src_ref=src, dst_ref=dst, send_sem=send_sem, recv_sem=recv_sem, device_id=device, device_id_type=MESH
        )

    def await_bytes(ref, sem):
        pltpu.make_async_copy(ref, ref, sem).wait()

    def group_peer(j):
        peer = lax.rem(mine + j, GROUP)
        return at(lax.rem(peer, N), x, y, peer // N)

    barrier = pltpu.get_barrier_semaphore()
    peers = [at(z, ahead(x, o), y, core) for o in range(1, N)]
    peers += [at(z, x, ahead(y, o), core) for o in range(1, N)]
    peers += [group_peer(j) for j in range(1, GROUP)]
    for peer in peers:
        pl.semaphore_signal(barrier, inc=1, device_id=peer, device_id_type=MESH)
    pl.semaphore_wait(barrier, len(peers))

    def block_of(half, o):
        return ahead(y, o) if half == 0 else N + ahead(x, o)

    def across(half, o):
        return at(z, ahead(x, o), y, core) if half == 0 else at(z, x, ahead(y, o), core)

    def along(half, o):
        return at(z, x, ahead(y, o), core) if half == 0 else at(z, ahead(x, o), y, core)

    slot = (x, y)

    def start_stage1(it, half, src):
        dst = cod.at[it, block_of(half, 0), slot[half]]
        for o in (2, 1, 3):
            remote(src, dst, c1_send.at[it, half, o - 1], c1_recv.at[it, half, o - 1], across(half, o)).start()

    def await_stage1(it, half):
        for o in range(1, N):
            await_bytes(cod.at[it, 0, 0], c1_recv.at[it, half, o - 1])

    def start_stage2(it, half, places):
        block = cod.at[it, block_of(half, 0)]
        for o in places:
            remote(block, block, c2_send.at[it, half, o - 1], c2_recv.at[it, half, o - 1], along(half, o)).start()

    def await_block(it, half, o):
        await_bytes(cod.at[it, 0], c2_recv.at[it, half, N - 1 - o])

    before, after, opposite = ahead(z, N - 1), ahead(z, 1), ahead(z, 2)
    first, other = core * N, (1 - core) * N
    next_device, last_device = at(after, x, y, core), at(before, x, y, core)

    def rows_of(p, part=0, parts=1):
        return pl.ds(p * ROWS + part * (ROWS // parts), ROWS // parts)

    def direct(p):
        src, dst = frames.at[rows_of(p)], tok.at[first + z, rows_of(p)]
        remote(src, dst, tok_send.at[p, 0], tok_recv.at[p, 0], next_device).start()
        remote(src, dst, tok_send.at[p, 1], tok_recv.at[p, 1], last_device).start()

    def forward(p):
        await_bytes(tok.at[0, rows_of(p)], tok_recv.at[p, 0])
        low = tok.at[first + before, rows_of(p, 0, 2)]
        remote(low, low, tok_send.at[p, 2], tok_recv.at[p, 2], next_device).start()
        await_bytes(tok.at[0, rows_of(p)], tok_recv.at[p, 1])
        high = tok.at[first + after, rows_of(p, 1, 2)]
        remote(high, high, tok_send.at[p, 3], tok_recv.at[p, 3], last_device).start()

    def await_forwarded():
        for p in range(PIECES):
            await_bytes(tok.at[0, rows_of(p, 0, 2)], tok_recv.at[p, 2])
            await_bytes(tok.at[0, rows_of(p, 1, 2)], tok_recv.at[p, 3])

    def share(i, src, place):
        remote(src, tok.at[first + place], share_send.at[i], share_recv.at[i], at(z, x, y, 1 - core)).start()

    def await_shared(i):
        await_bytes(tok.at[0], share_recv.at[i])

    own_codes = [codebook.at[z, half] for half in range(2)]
    keep = [
        pltpu.make_async_copy(own_codes[0], cod.at[0, y, x], own_sem.at[0]),
        pltpu.make_async_copy(own_codes[1], cod.at[0, N + x, y], own_sem.at[1]),
        pltpu.make_async_copy(frames, tok.at[first + z], own_sem.at[2]),
    ]
    for half in range(2):
        start_stage1(0, half, own_codes[half])
    for copy in keep:
        copy.start()
    for p in range(PIECES):
        direct(p)
    share(0, frames, z)
    for copy in keep:
        copy.wait()
    for half in range(2):
        await_stage1(0, half)
        start_stage2(0, half, (1, 3, 2))
    forward(0)
    forward(1)

    def parts_of(codes):
        norms = jnp.sum(codes * codes, axis=1, keepdims=True) * SHARPNESS
        return *split(codes * (2.0 * SHARPNESS)), jnp.broadcast_to(norms, (codes.shape[0], 128))

    for o in (0, 1, 3, 2):
        for half in range(2):
            if o > 0:
                await_block(0, half, o)
            b = block_of(half, o)
            chi[b], clo[b], cnorm[b] = parts_of(cod[0, b].reshape(BLOCK, D))

    def score(high, low, norms, g):
        inner = lax.dot_general(
            jnp.concatenate([high, high, low], axis=1),
            jnp.concatenate([thi[g], tlo[g], thi[g]], axis=1),
            LAST,
            preferred_element_type=F32,
        )
        return inner - jnp.tile(norms, (1, TILE // 128))

    def add_up(g, tiles, carry):
        old_top, old_total = carry if carry is not None else (None, None)
        new_top = tops[g] if carry is None else jnp.maximum(old_top, tops[g])
        new_total = None if carry is None else old_total * jnp.exp2(old_top - new_top)
        for tile in tiles:
            more = jnp.sum(jnp.exp2(tile - new_top), axis=0, keepdims=True)
            new_total = more if new_total is None else new_total + more
        return new_top, new_total

    def publish(it, g, row_top, row_total):
        norm = tnorm[g]
        shift = (row_top - norm) + norm
        stats[it, g // BATCH, mine, g % BATCH] = shift + jnp.log2(row_total * jnp.exp2(row_top - shift))

    def send_stats(it, batch):
        own = stats.at[it, batch, mine]
        for j in range(1, GROUP):
            remote(own, own, st_send.at[it, batch], st_recv.at[it, batch], group_peer(j)).start()

    def normalise(it, batch):
        await_bytes(stats.at[it, batch, pl.ds(0, GROUP - 1)], st_recv.at[it, batch])
        for q in range(BATCH):
            g = batch * BATCH + q
            logs = stats[it, batch, :, q, 0, :]
            highest = jnp.max(logs, axis=0, keepdims=True)
            lognorm[g] = highest + jnp.log2(jnp.sum(jnp.exp2(logs - highest), axis=0, keepdims=True))

    def score_tile(g):
        thi[g], tlo[g] = split(tok[g])
        high, low = chi[...].reshape(BLOCKS * BLOCK, D), clo[...].reshape(BLOCKS * BLOCK, D)
        tile_scores = score(high, low, cnorm[...].reshape(BLOCKS * BLOCK, 128), g)
        scores[:, g] = tile_scores.reshape(BLOCKS, BLOCK, TILE)
        tops[g] = jnp.max(tile_scores, axis=0, keepdims=True)

    def sum_tile(g):
        squares = tok[g] * tok[g]
        squares = squares[:, :128] + squares[:, 128:]
        tnorm[g] = jnp.sum(squares.T, axis=0, keepdims=True) * SHARPNESS
        publish(0, g, *add_up(g, [scores[:, g].reshape(BLOCKS * BLOCK, TILE)], None))

    def source(i):
        place = jnp.where(i < 2, z, jnp.where(i < 6, jnp.where(i % 2 == 0, before, after), opposite))
        ours = (i == 0) | (i == 2) | (i == 3)
        return jnp.where(i < 6, jnp.where(ours, core, 1 - core), i - 6) * N + place

    def move_on(i):
        @pl.when(i == 1)
        def _():
            await_shared(0)

        @pl.when(i == 2)
        def _():
            forward(2)
            forward(3)
            share(1, tok.at[first + before], before)
            share(2, tok.at[first + after], after)

        @pl.when(i == 4)
        def _():
            await_shared(1)

        @pl.when(i == 5)
        def _():
            await_shared(2)

        @pl.when(i == 6)
        def _():
            await_forwarded()
            share(3, tok.at[first + opposite], opposite)
            await_shared(3)

    score_tile(source(0))

    def step(i, _):
        move_on(i)
        sum_tile(source(i - 1))
        score_tile(source(i))

        @pl.when(i == TILES - 1)
        def _():
            send_stats(0, 0)

        return 0

    lax.fori_loop(1, TILES, step, 0)
    sum_tile(source(TILES - 1))
    send_stats(0, 1)

    def gray(i):
        return jnp.bitwise_xor(i, i // 2)

    def weigh(blocks, tiles):
        lefts, rights, counts = [], [], None
        for g in tiles:
            pair_scores = jnp.concatenate([scores[b, g] for b in blocks], axis=0)
            weights = jnp.exp2(pair_scores - lognorm[g])
            for c in range(TILE // 128):
                piece = weights[:, c * 128 : (c + 1) * 128]
                counts = piece if counts is None else counts + piece
            high, low = split(weights)
            lefts += [high, high, low]
            rights += [thi[g], tlo[g], thi[g]]
        weighted = jnp.dot(jnp.concatenate(lefts, axis=1), jnp.concatenate(rights, axis=0), preferred_element_type=F32)
        for half in range(2):
            part[blocks[half], pl.ds(0, BLOCK)] += weighted[half * BLOCK : (half + 1) * BLOCK]
            row = jnp.sum(counts[half * BLOCK : (half + 1) * BLOCK].T, axis=0, keepdims=True)
            part[blocks[half], pl.ds(BLOCK, 8)] += jnp.broadcast_to(jnp.tile(row, (1, 2)), (8, D))

    def moments(it):
        batches = BATCHES if it == 0 else 1
        part[...] = jnp.zeros_like(part)
        normalise(it, 0)
        if batches == 1:
            normalise(it, 1)

        def step(i, _):
            o, batch = gray(N - 1 - i // batches), i % batches

            if batches > 1:

                @pl.when(i == 1)
                def _():
                    normalise(it, 1)

            blocks = [block_of(half, o) for half in range(2)]
            size = TILES // batches
            weigh(blocks, [batch * size + q for q in range(size)])

            @pl.when((batch == batches - 1) & (o != 0))
            def _():
                for half in range(2):
                    remote(
                        part.at[blocks[half]], rs1.at[it, half, o - 1], r1_send.at[it, half, o - 1], r1_recv.at[it, half, o - 1], along(half, o)
                    ).start()

            return 0

        lax.fori_loop(0, N * batches, step, 0)

    def reduce_sums(it, use):
        for half in range(2):
            for o in range(1, N):
                await_bytes(part.at[0], r1_recv.at[it, half, o - 1])
            row = part[block_of(half, 0)] + rs1[it, half, 0] + rs1[it, half, 1] + rs1[it, half, 2]
            for p in range(N):
                mid[half, p, pl.ds(0, HALF)] = row[p * HALF : (p + 1) * HALF]
                mid[half, p, pl.ds(HALF, 8)] = row[BLOCK:]
            for o in (2, 1, 3):
                remote(
                    mid.at[half, ahead(slot[half], o)], rs2.at[it, half, o - 1], r2_send.at[it, half, o - 1], r2_recv.at[it, half, o - 1], across(half, o)
                ).start()
        for half in range(2):
            for o in range(1, N):
                await_bytes(mid.at[0, 0], r2_recv.at[it, half, o - 1])
            sums = mid[half, slot[half]] + rs2[it, half, 0] + rs2[it, half, 1] + rs2[it, half, 2]
            flip[half] = jnp.broadcast_to(sums[HALF : HALF + 1, :128], (128, 128)).T
            count = flip[half, pl.ds(pl.multiple_of(slot[half] * HALF, HALF), HALF)]
            old = cod[it, block_of(half, 0), slot[half]]
            use(half, (sums[:HALF] + PRIOR_WEIGHT * old) / (jnp.tile(count, (1, 2)) + PRIOR_WEIGHT), count)

    def sent(it):
        for half in range(2):
            for o in range(1, N):
                await_bytes(part.at[0], r1_send.at[it, half, o - 1])
                await_bytes(mid.at[0, 0], r2_send.at[it, half, o - 1])

    def next_codes(half, codes, _):
        cod[1, block_of(half, 0), slot[half]] = codes
        start_stage1(1, half, cod.at[1, block_of(half, 0), slot[half]])

    moments(0)
    reduce_sums(0, next_codes)
    for half in range(2):
        await_stage1(1, half)
        start_stage2(1, half, (1, 3))

    def score_pair(o):
        blocks = [block_of(half, o) for half in range(2)]
        codes = jnp.concatenate([cod[1, b].reshape(BLOCK, D) for b in blocks], axis=0)
        high, low, norms = parts_of(codes)
        for g in range(TILES):
            tile_scores = score(high, low, norms, g)
            for half in range(2):
                scores[blocks[half], g] = tile_scores[half * BLOCK : (half + 1) * BLOCK]
            tops[g] = jnp.max(tile_scores, axis=0, keepdims=True)

    def sum_pair(o, g):
        blocks = [block_of(half, o) for half in range(2)]
        return add_up(g, [scores[b, g] for b in blocks], (top[g], total[g]))

    top[...] = jnp.full_like(top, -1e30)
    total[...] = jnp.zeros_like(total)
    score_pair(0)
    for half in range(2):
        start_stage2(1, half, (2,))

    def pair_step(i, _):
        o, previous = gray(i), gray(i - 1)
        for half in range(2):
            await_block(1, half, o)
        for g in range(TILES):
            top[g], total[g] = sum_pair(previous, g)
        score_pair(o)
        return 0

    lax.fori_loop(1, N, pair_step, 0)

    def last_sum(batch, _):
        for q in range(BATCH):
            g = batch * BATCH + q
            publish(1, g, *sum_pair(N // 2, g))
        send_stats(1, batch)
        return 0

    lax.fori_loop(0, BATCHES, last_sum, 0)
    sent(0)
    moments(1)

    def last_codes(half, codes, count):
        fin[z, pl.ds(half * HALF, HALF)] = codes
        flip[2, pl.ds(half * HALF, HALF)] = count

    flip[2] = jnp.zeros((128, 128), F32)
    reduce_sums(1, last_codes)
    fin[z, pl.ds(2 * HALF, 8)] = jnp.tile(flip[2].T[:8], (1, 2))
    for o in (2, 1, 3):
        remote(fin.at[z], fin.at[z], f_send.at[o - 1], f_recv.at[o - 1], at(ahead(z, o), x, y, core)).start()
    sent(1)

    for p in range(PIECES):
        for i in range(2):
            await_bytes(tok.at[0, rows_of(p)], tok_send.at[p, i])
            await_bytes(tok.at[0, rows_of(p, 0, 2)], tok_send.at[p, 2 + i])
    for i in range(4):
        await_bytes(tok.at[0], share_send.at[i])
    for it in range(ITERS):
        for batch in range(BATCHES):
            await_bytes(stats.at[it, batch, pl.ds(0, GROUP - 1)], st_send.at[it, batch])
        for half in range(2):
            for o in range(1, N):
                await_bytes(cod.at[it, 0, 0], c1_send.at[it, half, o - 1])
                await_bytes(cod.at[it, 0], c2_send.at[it, half, o - 1])
    for o in range(1, N):
        await_bytes(fin.at[0], f_send.at[o - 1])
        await_bytes(fin.at[0], f_recv.at[o - 1])
    for p in range(N):
        cent_out[pl.ds(p * 2 * HALF, 2 * HALF)] = fin[p, pl.ds(0, 2 * HALF)]
        count_out[:, pl.ds(p * 2 * HALF, 2 * HALF)] = fin[p, pl.ds(2 * HALF, 1), pl.ds(0, 2 * HALF)]


def hand_on(cent, count, cent_out, count_out):
    cent_out[...] = cent[...]
    count_out[...] = count[...]


def on_device(tokens, codebook):
    vmem, dma = pltpu.VMEM, pltpu.SemaphoreType.DMA
    peers = N - 1
    results = [jax.ShapeDtypeStruct((OWNED, D), F32), jax.ShapeDtypeStruct((1, OWNED), F32)]
    centroids, counts = pl.pallas_call(
        em_kernel,
        out_shape=results,
        in_specs=[pl.BlockSpec(memory_space=pl.ANY)] * 2,
        out_specs=[pl.BlockSpec(memory_space=vmem)] * 2,
        scratch_shapes=[
            vmem((TILES, TILE, D), F32),
            vmem((TILES, TILE, D), BF16),
            vmem((TILES, TILE, D), BF16),
            vmem((TILES, 1, TILE), F32),
            vmem((ITERS, BLOCKS, N, HALF, D), F32),
            vmem((BLOCKS, BLOCK, D), BF16),
            vmem((BLOCKS, BLOCK, D), BF16),
            vmem((BLOCKS, BLOCK, 128), F32),
            vmem((BLOCKS, TILES, BLOCK, TILE), F32),
            vmem((TILES, 1, TILE), F32),
            vmem((TILES, 1, TILE), F32),
            vmem((TILES, 1, TILE), F32),
            vmem((TILES, 1, TILE), F32),
            vmem((ITERS, BATCHES, GROUP, BATCH, 1, TILE), F32),
            vmem((BLOCKS, SUMS, D), F32),
            vmem((ITERS, 2, peers, SUMS, D), F32),
            vmem((2, N, HALF + 8, D), F32),
            vmem((ITERS, 2, peers, HALF + 8, D), F32),
            vmem((N, 2 * HALF + 8, D), F32),
            vmem((3, 128, 128), F32),
            dma((3,)),
            dma((PIECES, 4)),
            dma((PIECES, 4)),
            dma((4,)),
            dma((4,)),
            dma((ITERS, 2, peers)),
            dma((ITERS, 2, peers)),
            dma((ITERS, 2, peers)),
            dma((ITERS, 2, peers)),
            dma((ITERS, BATCHES)),
            dma((ITERS, BATCHES)),
            dma((ITERS, 2, peers)),
            dma((ITERS, 2, peers)),
            dma((ITERS, 2, peers)),
            dma((ITERS, 2, peers)),
            dma((peers,)),
            dma((peers,)),
        ],
        compiler_params=pltpu.CompilerParams(collective_id=0, has_side_effects=True, vmem_limit_bytes=56 << 20),
        cost_estimate=pl.CostEstimate(
            flops=ITERS * 2 * 3 * 2 * TILES * TILE * BLOCKS * BLOCK * D,
            bytes_accessed=4 * (FRAMES + 2 * OWNED) * D,
            transcendentals=ITERS * 2 * TILES * TILE * BLOCKS * BLOCK,
        ),
    )(tokens, codebook.reshape(N, 2, HALF, D))
    centroids, counts = pl.pallas_call(
        hand_on,
        out_shape=results,
        in_specs=[pl.BlockSpec(memory_space=vmem)] * 2,
        out_specs=[pl.BlockSpec(memory_space=vmem)] * 2,
    )(centroids, counts)
    return centroids, counts.reshape(OWNED)


def solution(mesh):
    return jax.shard_map(
        on_device,
        mesh=mesh,
        in_specs=(P(("tok", "code"), None), P("code", None)),
        out_specs=(P("code", None), P("code")),
        check_vma=False,
    )
```

```python
import functools
import math

import jax
import jax.numpy as jnp
from jax import lax
from jax.experimental import pallas as pl
from jax.experimental.pallas import tpu as pltpu
from jax.sharding import PartitionSpec as P

MESH = pl.DeviceIdType.MESH
F32, BF16 = jnp.float32, jnp.bfloat16
ITERS = 2
PRIOR_WEIGHT = 1.0
N = 4
CORES = 2
GROUP = N * CORES
D = 256
FRAMES = 512
OWNED = 256
HALF = OWNED // N // 2
BLOCK = N * HALF
BLOCKS = 2 * N
TILES = GROUP
TILE = FRAMES
PIECES = 4
ROWS = FRAMES // PIECES
BATCH = 4
BATCHES = TILES // BATCH
SUMS = BLOCK + 8
SHARPNESS = math.log2(math.e) / math.sqrt(D)
LAST = (((1,), (1,)), ((), ()))


def split(value):
    high = value.astype(BF16)
    return high, (value - high.astype(F32)).astype(BF16)


def em_kernel(
    frames, codebook, cent_out, count_out,
    tok, thi, tlo, tnorm, cod, chi, clo, cnorm, scores, tops, top, total, lognorm, stats, part, rs1, mid, rs2, fin, flip,
    own_sem, tok_send, tok_recv, share_send, share_recv, c1_send, c1_recv, c2_send, c2_recv, st_send, st_recv,
    r1_send, r1_recv, r2_send, r2_recv, f_send, f_recv,
):
    z = lax.axis_index("tok")
    place = lax.axis_index("code")
    core = lax.rem(place, CORES)
    y = lax.rem(place // CORES, N)
    x = place // (CORES * N)
    mine = core * N + z

    def at(pz, px, py, pc):
        return (pz, (px * N + py) * CORES + pc)

    def ahead(p, o):
        return lax.rem(p + o, N)

    def remote(src, dst, send_sem, recv_sem, device):
        return pltpu.make_async_remote_copy(
            src_ref=src, dst_ref=dst, send_sem=send_sem, recv_sem=recv_sem, device_id=device, device_id_type=MESH
        )

    def await_bytes(ref, sem):
        pltpu.make_async_copy(ref, ref, sem).wait()

    def group_peer(j):
        peer = lax.rem(mine + j, GROUP)
        return at(lax.rem(peer, N), x, y, peer // N)

    barrier = pltpu.get_barrier_semaphore()
    peers = [at(z, ahead(x, o), y, core) for o in range(1, N)]
    peers += [at(z, x, ahead(y, o), core) for o in range(1, N)]
    peers += [group_peer(j) for j in range(1, GROUP)]
    for peer in peers:
        pl.semaphore_signal(barrier, inc=1, device_id=peer, device_id_type=MESH)
    pl.semaphore_wait(barrier, len(peers))

    def block_of(half, o):
        return ahead(y, o) if half == 0 else N + ahead(x, o)

    def across(half, o):
        return at(z, ahead(x, o), y, core) if half == 0 else at(z, x, ahead(y, o), core)

    def along(half, o):
        return at(z, x, ahead(y, o), core) if half == 0 else at(z, ahead(x, o), y, core)

    slot = (x, y)

    def start_stage1(it, half, src):
        dst = cod.at[it, block_of(half, 0), slot[half]]
        for o in (2, 1, 3):
            remote(src, dst, c1_send.at[it, half, o - 1], c1_recv.at[it, half, o - 1], across(half, o)).start()

    def await_stage1(it, half):
        for o in range(1, N):
            await_bytes(cod.at[it, 0, 0], c1_recv.at[it, half, o - 1])

    def start_stage2(it, half, places):
        block = cod.at[it, block_of(half, 0)]
        for o in places:
            remote(block, block, c2_send.at[it, half, o - 1], c2_recv.at[it, half, o - 1], along(half, o)).start()

    def await_block(it, half, o):
        await_bytes(cod.at[it, 0], c2_recv.at[it, half, N - 1 - o])

    before, after, opposite = ahead(z, N - 1), ahead(z, 1), ahead(z, 2)
    first, other = core * N, (1 - core) * N
    next_device, last_device = at(after, x, y, core), at(before, x, y, core)

    def rows_of(p, part=0, parts=1):
        return pl.ds(p * ROWS + part * (ROWS // parts), ROWS // parts)

    def direct(p):
        src, dst = frames.at[rows_of(p)], tok.at[first + z, rows_of(p)]
        remote(src, dst, tok_send.at[p, 0], tok_recv.at[p, 0], next_device).start()
        remote(src, dst, tok_send.at[p, 1], tok_recv.at[p, 1], last_device).start()

    def forward(p):
        await_bytes(tok.at[0, rows_of(p)], tok_recv.at[p, 0])
        low = tok.at[first + before, rows_of(p, 0, 2)]
        remote(low, low, tok_send.at[p, 2], tok_recv.at[p, 2], next_device).start()
        await_bytes(tok.at[0, rows_of(p)], tok_recv.at[p, 1])
        high = tok.at[first + after, rows_of(p, 1, 2)]
        remote(high, high, tok_send.at[p, 3], tok_recv.at[p, 3], last_device).start()

    def await_forwarded():
        for p in range(PIECES):
            await_bytes(tok.at[0, rows_of(p, 0, 2)], tok_recv.at[p, 2])
            await_bytes(tok.at[0, rows_of(p, 1, 2)], tok_recv.at[p, 3])

    def share(i, src, place):
        remote(src, tok.at[first + place], share_send.at[i], share_recv.at[i], at(z, x, y, 1 - core)).start()

    def await_shared(i):
        await_bytes(tok.at[0], share_recv.at[i])

    own_codes = [codebook.at[z, half] for half in range(2)]
    keep = [
        pltpu.make_async_copy(own_codes[0], cod.at[0, y, x], own_sem.at[0]),
        pltpu.make_async_copy(own_codes[1], cod.at[0, N + x, y], own_sem.at[1]),
        pltpu.make_async_copy(frames, tok.at[first + z], own_sem.at[2]),
    ]
    for half in range(2):
        start_stage1(0, half, own_codes[half])
    for copy in keep:
        copy.start()
    for p in range(PIECES):
        direct(p)
    share(0, frames, z)
    for copy in keep:
        copy.wait()
    for half in range(2):
        await_stage1(0, half)
        start_stage2(0, half, (1, 3, 2))
    forward(0)
    for half in range(2):
        for o in range(1, N):
            await_block(0, half, o)

    def parts_of(codes):
        norms = jnp.sum(codes * codes, axis=1, keepdims=True) * SHARPNESS
        return *split(codes * (2.0 * SHARPNESS)), jnp.broadcast_to(norms, (codes.shape[0], 128))

    def split_block(b, _):
        chi[b], clo[b], cnorm[b] = parts_of(cod[0, b].reshape(BLOCK, D))
        return 0

    lax.fori_loop(0, BLOCKS, split_block, 0)

    def score(high, low, norms, g):
        inner = lax.dot_general(
            jnp.concatenate([high, high, low], axis=1),
            jnp.concatenate([thi[g], tlo[g], thi[g]], axis=1),
            LAST,
            preferred_element_type=F32,
        )
        return inner - jnp.tile(norms, (1, TILE // 128))

    def add_up(g, tiles, carry):
        old_top, old_total = carry if carry is not None else (None, None)
        new_top = tops[g] if carry is None else jnp.maximum(old_top, tops[g])
        new_total = None if carry is None else old_total * jnp.exp2(old_top - new_top)
        for tile in tiles:
            more = jnp.sum(jnp.exp2(tile - new_top), axis=0, keepdims=True)
            new_total = more if new_total is None else new_total + more
        return new_top, new_total

    def publish(it, g, row_top, row_total):
        norm = tnorm[g]
        shift = (row_top - norm) + norm
        stats[it, g // BATCH, mine, g % BATCH] = shift + jnp.log2(row_total * jnp.exp2(row_top - shift))

    def send_stats(it, batch):
        own = stats.at[it, batch, mine]
        for j in range(1, GROUP):
            remote(own, own, st_send.at[it, batch], st_recv.at[it, batch], group_peer(j)).start()

    def normalise(it, batch):
        await_bytes(stats.at[it, batch, pl.ds(0, GROUP - 1)], st_recv.at[it, batch])
        for q in range(BATCH):
            g = batch * BATCH + q
            logs = stats[it, batch, :, q, 0, :]
            highest = jnp.max(logs, axis=0, keepdims=True)
            lognorm[g] = highest + jnp.log2(jnp.sum(jnp.exp2(logs - highest), axis=0, keepdims=True))

    def score_tile(g):
        thi[g], tlo[g] = split(tok[g])
        high, low = chi[...].reshape(BLOCKS * BLOCK, D), clo[...].reshape(BLOCKS * BLOCK, D)
        tile_scores = score(high, low, cnorm[...].reshape(BLOCKS * BLOCK, 128), g)
        scores[:, g] = tile_scores.reshape(BLOCKS, BLOCK, TILE)
        tops[g] = jnp.max(tile_scores, axis=0, keepdims=True)

    def sum_tile(g):
        squares = tok[g] * tok[g]
        squares = squares[:, :128] + squares[:, 128:]
        tnorm[g] = jnp.sum(squares.T, axis=0, keepdims=True) * SHARPNESS
        publish(0, g, *add_up(g, [scores[:, g].reshape(BLOCKS * BLOCK, TILE)], None))

    def source(i):
        place = jnp.where(i < 2, z, jnp.where(i < 6, jnp.where(i % 2 == 0, before, after), opposite))
        ours = (i == 0) | (i == 2) | (i == 3)
        return jnp.where(i < 6, jnp.where(ours, core, 1 - core), i - 6) * N + place

    def move_on(i):
        @pl.when(i == 1)
        def _():
            forward(1)
            await_shared(0)

        @pl.when(i == 2)
        def _():
            forward(2)
            forward(3)
            share(1, tok.at[first + before], before)
            share(2, tok.at[first + after], after)

        @pl.when(i == 4)
        def _():
            await_shared(1)

        @pl.when(i == 5)
        def _():
            await_shared(2)

        @pl.when(i == 6)
        def _():
            await_forwarded()
            share(3, tok.at[first + opposite], opposite)
            await_shared(3)

    score_tile(source(0))

    def step(i, _):
        move_on(i)
        sum_tile(source(i - 1))
        score_tile(source(i))

        @pl.when(i == TILES - 1)
        def _():
            send_stats(0, 0)

        return 0

    lax.fori_loop(1, TILES, step, 0)
    sum_tile(source(TILES - 1))
    send_stats(0, 1)

    def gray(i):
        return jnp.bitwise_xor(i, i // 2)

    def weigh(blocks, tiles):
        lefts, rights, counts = [], [], None
        for g in tiles:
            pair_scores = jnp.concatenate([scores[b, g] for b in blocks], axis=0)
            weights = jnp.exp2(pair_scores - lognorm[g])
            for c in range(TILE // 128):
                piece = weights[:, c * 128 : (c + 1) * 128]
                counts = piece if counts is None else counts + piece
            high, low = split(weights)
            lefts += [high, high, low]
            rights += [thi[g], tlo[g], thi[g]]
        weighted = jnp.dot(jnp.concatenate(lefts, axis=1), jnp.concatenate(rights, axis=0), preferred_element_type=F32)
        for half in range(2):
            part[blocks[half], pl.ds(0, BLOCK)] += weighted[half * BLOCK : (half + 1) * BLOCK]
            row = jnp.sum(counts[half * BLOCK : (half + 1) * BLOCK].T, axis=0, keepdims=True)
            part[blocks[half], pl.ds(BLOCK, 8)] += jnp.broadcast_to(jnp.tile(row, (1, 2)), (8, D))

    def moments(it):
        batches = BATCHES if it == 0 else 1
        part[...] = jnp.zeros_like(part)
        normalise(it, 0)
        if batches == 1:
            normalise(it, 1)

        def step(i, _):
            o, batch = gray(N - 1 - i // batches), i % batches

            if batches > 1:

                @pl.when(i == 1)
                def _():
                    normalise(it, 1)

            blocks = [block_of(half, o) for half in range(2)]
            size = TILES // batches
            weigh(blocks, [batch * size + q for q in range(size)])

            @pl.when((batch == batches - 1) & (o != 0))
            def _():
                for half in range(2):
                    remote(
                        part.at[blocks[half]], rs1.at[it, half, o - 1], r1_send.at[it, half, o - 1], r1_recv.at[it, half, o - 1], along(half, o)
                    ).start()

            return 0

        lax.fori_loop(0, N * batches, step, 0)

    def reduce_sums(it, use):
        for half in range(2):
            for o in range(1, N):
                await_bytes(part.at[0], r1_recv.at[it, half, o - 1])
            row = part[block_of(half, 0)] + rs1[it, half, 0] + rs1[it, half, 1] + rs1[it, half, 2]
            for p in range(N):
                mid[half, p, pl.ds(0, HALF)] = row[p * HALF : (p + 1) * HALF]
                mid[half, p, pl.ds(HALF, 8)] = row[BLOCK:]
            for o in (2, 1, 3):
                remote(
                    mid.at[half, ahead(slot[half], o)], rs2.at[it, half, o - 1], r2_send.at[it, half, o - 1], r2_recv.at[it, half, o - 1], across(half, o)
                ).start()
        for half in range(2):
            for o in range(1, N):
                await_bytes(mid.at[0, 0], r2_recv.at[it, half, o - 1])
            sums = mid[half, slot[half]] + rs2[it, half, 0] + rs2[it, half, 1] + rs2[it, half, 2]
            flip[half] = jnp.broadcast_to(sums[HALF : HALF + 1, :128], (128, 128)).T
            count = flip[half, pl.ds(pl.multiple_of(slot[half] * HALF, HALF), HALF)]
            old = cod[it, block_of(half, 0), slot[half]]
            use(half, (sums[:HALF] + PRIOR_WEIGHT * old) / (jnp.tile(count, (1, 2)) + PRIOR_WEIGHT), count)

    def sent(it):
        for half in range(2):
            for o in range(1, N):
                await_bytes(part.at[0], r1_send.at[it, half, o - 1])
                await_bytes(mid.at[0, 0], r2_send.at[it, half, o - 1])

    def next_codes(half, codes, _):
        cod[1, block_of(half, 0), slot[half]] = codes
        start_stage1(1, half, cod.at[1, block_of(half, 0), slot[half]])

    moments(0)
    reduce_sums(0, next_codes)
    for half in range(2):
        await_stage1(1, half)
        start_stage2(1, half, (1, 3))

    def score_pair(o):
        blocks = [block_of(half, o) for half in range(2)]
        codes = jnp.concatenate([cod[1, b].reshape(BLOCK, D) for b in blocks], axis=0)
        high, low, norms = parts_of(codes)
        for g in range(TILES):
            tile_scores = score(high, low, norms, g)
            for half in range(2):
                scores[blocks[half], g] = tile_scores[half * BLOCK : (half + 1) * BLOCK]
            tops[g] = jnp.max(tile_scores, axis=0, keepdims=True)

    def sum_pair(o, g):
        blocks = [block_of(half, o) for half in range(2)]
        return add_up(g, [scores[b, g] for b in blocks], (top[g], total[g]))

    top[...] = jnp.full_like(top, -1e30)
    total[...] = jnp.zeros_like(total)
    score_pair(0)
    for half in range(2):
        start_stage2(1, half, (2,))

    def pair_step(i, _):
        o, previous = gray(i), gray(i - 1)
        for half in range(2):
            await_block(1, half, o)
        for g in range(TILES):
            top[g], total[g] = sum_pair(previous, g)
        score_pair(o)
        return 0

    lax.fori_loop(1, N, pair_step, 0)

    def last_sum(batch, _):
        for q in range(BATCH):
            g = batch * BATCH + q
            publish(1, g, *sum_pair(N // 2, g))
        send_stats(1, batch)
        return 0

    lax.fori_loop(0, BATCHES, last_sum, 0)
    sent(0)
    moments(1)

    def last_codes(half, codes, count):
        fin[z, pl.ds(half * HALF, HALF)] = codes
        flip[2, pl.ds(half * HALF, HALF)] = count

    flip[2] = jnp.zeros((128, 128), F32)
    reduce_sums(1, last_codes)
    fin[z, pl.ds(2 * HALF, 8)] = jnp.tile(flip[2].T[:8], (1, 2))
    for o in (2, 1, 3):
        remote(fin.at[z], fin.at[z], f_send.at[o - 1], f_recv.at[o - 1], at(ahead(z, o), x, y, core)).start()
    sent(1)

    for p in range(PIECES):
        for i in range(2):
            await_bytes(tok.at[0, rows_of(p)], tok_send.at[p, i])
            await_bytes(tok.at[0, rows_of(p, 0, 2)], tok_send.at[p, 2 + i])
    for i in range(4):
        await_bytes(tok.at[0], share_send.at[i])
    for it in range(ITERS):
        for batch in range(BATCHES):
            await_bytes(stats.at[it, batch, pl.ds(0, GROUP - 1)], st_send.at[it, batch])
        for half in range(2):
            for o in range(1, N):
                await_bytes(cod.at[it, 0, 0], c1_send.at[it, half, o - 1])
                await_bytes(cod.at[it, 0], c2_send.at[it, half, o - 1])
    for o in range(1, N):
        await_bytes(fin.at[0], f_send.at[o - 1])
        await_bytes(fin.at[0], f_recv.at[o - 1])
    for p in range(N):
        cent_out[pl.ds(p * 2 * HALF, 2 * HALF)] = fin[p, pl.ds(0, 2 * HALF)]
        count_out[:, pl.ds(p * 2 * HALF, 2 * HALF)] = fin[p, pl.ds(2 * HALF, 1), pl.ds(0, 2 * HALF)]


def hand_on(cent, count, cent_out, count_out):
    cent_out[...] = cent[...]
    count_out[...] = count[...]


def on_device(tokens, codebook):
    vmem, dma = pltpu.VMEM, pltpu.SemaphoreType.DMA
    peers = N - 1
    results = [jax.ShapeDtypeStruct((OWNED, D), F32), jax.ShapeDtypeStruct((1, OWNED), F32)]
    centroids, counts = pl.pallas_call(
        em_kernel,
        out_shape=results,
        in_specs=[pl.BlockSpec(memory_space=pl.ANY)] * 2,
        out_specs=[pl.BlockSpec(memory_space=vmem)] * 2,
        scratch_shapes=[
            vmem((TILES, TILE, D), F32),
            vmem((TILES, TILE, D), BF16),
            vmem((TILES, TILE, D), BF16),
            vmem((TILES, 1, TILE), F32),
            vmem((ITERS, BLOCKS, N, HALF, D), F32),
            vmem((BLOCKS, BLOCK, D), BF16),
            vmem((BLOCKS, BLOCK, D), BF16),
            vmem((BLOCKS, BLOCK, 128), F32),
            vmem((BLOCKS, TILES, BLOCK, TILE), F32),
            vmem((TILES, 1, TILE), F32),
            vmem((TILES, 1, TILE), F32),
            vmem((TILES, 1, TILE), F32),
            vmem((TILES, 1, TILE), F32),
            vmem((ITERS, BATCHES, GROUP, BATCH, 1, TILE), F32),
            vmem((BLOCKS, SUMS, D), F32),
            vmem((ITERS, 2, peers, SUMS, D), F32),
            vmem((2, N, HALF + 8, D), F32),
            vmem((ITERS, 2, peers, HALF + 8, D), F32),
            vmem((N, 2 * HALF + 8, D), F32),
            vmem((3, 128, 128), F32),
            dma((3,)),
            dma((PIECES, 4)),
            dma((PIECES, 4)),
            dma((4,)),
            dma((4,)),
            dma((ITERS, 2, peers)),
            dma((ITERS, 2, peers)),
            dma((ITERS, 2, peers)),
            dma((ITERS, 2, peers)),
            dma((ITERS, BATCHES)),
            dma((ITERS, BATCHES)),
            dma((ITERS, 2, peers)),
            dma((ITERS, 2, peers)),
            dma((ITERS, 2, peers)),
            dma((ITERS, 2, peers)),
            dma((peers,)),
            dma((peers,)),
        ],
        compiler_params=pltpu.CompilerParams(collective_id=0, has_side_effects=True, vmem_limit_bytes=56 << 20),
        cost_estimate=pl.CostEstimate(
            flops=ITERS * 2 * 3 * 2 * TILES * TILE * BLOCKS * BLOCK * D,
            bytes_accessed=4 * (FRAMES + 2 * OWNED) * D,
            transcendentals=ITERS * 2 * TILES * TILE * BLOCKS * BLOCK,
        ),
    )(tokens, codebook.reshape(N, 2, HALF, D))
    centroids, counts = pl.pallas_call(
        hand_on,
        out_shape=results,
        in_specs=[pl.BlockSpec(memory_space=vmem)] * 2,
        out_specs=[pl.BlockSpec(memory_space=vmem)] * 2,
    )(centroids, counts)
    return centroids, counts.reshape(OWNED)


def solution(mesh):
    return jax.shard_map(
        on_device,
        mesh=mesh,
        in_specs=(P(("tok", "code"), None), P("code", None)),
        out_specs=(P("code", None), P("code")),
        check_vma=False,
    )
```
